32 devices in a mesh: grp: 2 (over x), lat: 2 (over core), lon: 8 (over z, y).
Axes of the slice: x: 2, y: 2, z: 4, core: 2. Of those that a mesh axis runs over, the one named last changes fastest.
Arguments:
- fields: bfloat16 [256, 128, 768], P(('grp', 'lat'), 'lon'), parts along dimension 0, may hold values from -6 to 6
- ocean: int32 [256, 128], P(('grp', 'lat'), 'lon'), parts along dimension 0, may hold values 0 or 1
- w_query1: bfloat16 [768, 768], replicated, may hold values from -4 to 4
- w_key1: bfloat16 [768, 768], replicated, may hold values from -4 to 4
- w_value1: bfloat16 [768, 768], replicated, may hold values from -0.21875 to 0.21875
- w_out1: bfloat16 [768, 768], replicated, may hold values from -0.21875 to 0.21875
- w_query2: bfloat16 [768, 768], replicated, may hold values from -4 to 4
- w_key2: bfloat16 [768, 768], replicated, may hold values from -4 to 4
- w_value2: bfloat16 [768, 768], replicated, may hold values from -0.21875 to 0.21875
- w_out2: bfloat16 [768, 768], replicated, may hold values from -0.21875 to 0.21875
Outputs:
- forecast: bfloat16 [256, 128, 768], P(('grp', 'lat'), 'lon'), parts along dimension 0
The draws below stay inside these ranges and needn't reach their ends.
There are 2 independent parts, one for each index of `grp`. The reference program is written for one: setup_inputs(seed, part) draws one part's arguments, and reference() takes and returns one part's arrays. A program takes and returns all parts, laid end to end along the dimension named above; an argument that names none is the same for every part. Nothing has to cross between parts.
All inputs are finite; a program needn't handle non-finite values. No bound on the sum of `ocean` on one device may be relied on, other than what follows from the above.
Results may differ from the reference program's by a relative error of at most 0.006.
Values may be sent and summed in bfloat16 or wider, within the bound.
No kernel may reach another device: no remote copies, remote signals or barrier semaphores. Data moves between devices by JAX's collectives and lax.ppermute only.
A program may use at most 128 MiB of HBM per device.

```python
import jax
import jax.numpy as jnp
from jax import lax

D = 768
HEADS = 12
LATS = 128
LONS = 128


def weight_pair(key, salt):
    first = jax.random.normal(jax.random.fold_in(key, salt), (D, D), jnp.float32) * D ** (-0.5)
    second = jax.random.normal(jax.random.fold_in(key, salt + 1), (D, D), jnp.float32) * D ** (-0.5)
    return (jnp.clip(first, -4.0, 4.0), jnp.clip(second, -4.0, 4.0))


def draw_w_query1(key, part):
    return weight_pair(key, 101)[0].astype(jnp.bfloat16)


def draw_w_key1(key, part):
    return weight_pair(key, 101)[1].astype(jnp.bfloat16)


def draw_w_query2(key, part):
    return weight_pair(key, 203)[0].astype(jnp.bfloat16)


def draw_w_key2(key, part):
    return weight_pair(key, 203)[1].astype(jnp.bfloat16)


def touch_ends(drawn, own_key, smallest, largest):
    spot = [jax.random.randint(jax.random.fold_in(own_key, axis), (), 0, length) for axis, length in enumerate(drawn.shape)]
    main_axis = drawn.shape.index(max(drawn.shape))
    beside = spot[:main_axis] + [(spot[main_axis] + 1) % drawn.shape[main_axis]] + spot[main_axis + 1:]
    return drawn.at[tuple(spot)].set(smallest).at[tuple(beside)].set(largest)


def levels(own_key, dims, shards, least, largest):
    loudness = 1.0
    for position, parts in shards:
        heights = jax.random.uniform(jax.random.fold_in(jax.random.fold_in(own_key, 6), position), (parts,), jnp.float32, least / len(shards), largest / len(shards))
        loudness = loudness * jnp.repeat(jnp.exp(heights), dims[position] // parts).reshape((-1,) + (1,) * (len(dims) - 1 - position))
    return loudness


def centred(rng, shape, scale, limit, split=(), kind=jnp.bfloat16):
    drawn = scale * jax.random.normal(rng, shape, jnp.float32)
    if split:
        drawn = drawn * levels(rng, shape, split, -0.22, 0.18)
    return jnp.clip(drawn, -limit, limit).astype(kind)


def setup_inputs(seed: int = 0, part: int = 0) -> dict:
    key_of = jax.random.split(jax.random.key(seed), 11)
    own_keys = jax.random.split(jax.random.fold_in(key_of[10], part), 11)
    fields = centred(own_keys[0], (LATS, LONS, D), 1.0, 6.0, ((0, 2), (1, 8)))
    ocean = touch_ends((jax.random.randint(own_keys[1], (LATS, LONS), 0, 4) < 3).astype(jnp.int32), jax.random.fold_in(own_keys[1], 1), 0, 1)
    w_query1 = draw_w_query1(jax.random.fold_in(key_of[10], 71), part)
    w_key1 = draw_w_key1(jax.random.fold_in(key_of[10], 71), part)
    w_value1 = centred(key_of[4], (D, D), D ** -0.5, 0.21875)
    w_out1 = centred(key_of[5], (D, D), D ** -0.5, 0.21875)
    w_query2 = draw_w_query2(jax.random.fold_in(key_of[10], 71), part)
    w_key2 = draw_w_key2(jax.random.fold_in(key_of[10], 71), part)
    w_value2 = centred(key_of[8], (D, D), D ** -0.5, 0.21875)
    w_out2 = centred(key_of[9], (D, D), D ** -0.5, 0.21875)
    return dict(fields=fields, ocean=ocean, w_query1=w_query1, w_key1=w_key1, w_value1=w_value1, w_out1=w_out1, w_query2=w_query2, w_key2=w_key2, w_value2=w_value2, w_out2=w_out2)


EPS = 1e-05
NEG = -1e+30

def norm_rows(a):
    af = a.astype(jnp.float32)
    mean = lax.optimization_barrier(jnp.mean(af, -1, keepdims=True))
    var = lax.optimization_barrier(jnp.mean((af - mean) * (af - mean), -1, keepdims=True))
    return ((af - mean) * lax.rsqrt(var + EPS)).astype(jnp.bfloat16)

def project(h, weight):
    return jnp.dot(h, weight, preferred_element_type=jnp.float32).astype(jnp.bfloat16)

def masked_softmax(scores, key_ok, land_query):
    top = lax.optimization_barrier(jnp.max(jnp.where(key_ok, scores, NEG), -1, keepdims=True))
    expo = jnp.where(key_ok, jnp.exp(scores - top), 0.0)
    total = lax.optimization_barrier(jnp.sum(expo, -1, keepdims=True)) + land_query[..., None]
    return (expo / total).astype(jnp.bfloat16)

def window_attend(query, keys, values, flags):
    rows, cols, width = query.shape
    nh = HEADS
    hd = width // nh
    scale = hd ** (-0.5)

    def tiles(a):
        a = a.reshape(rows // 8, 8, cols // 8, 8, nh, hd).transpose(0, 2, 4, 1, 3, 5)
        return a.reshape(rows // 8, cols // 8, nh, 64, hd).astype(jnp.float32)
    marks = flags.reshape(rows // 8, 8, cols // 8, 8).transpose(0, 2, 1, 3).reshape(rows // 8, cols // 8, 64)
    key_ok = (marks > 0)[:, :, None, None, :]
    land_query = (marks <= 0).astype(jnp.float32)[:, :, None, :]
    scores = jnp.einsum('abhqd,abhkd->abhqk', tiles(query), tiles(keys)) * scale
    probs = masked_softmax(scores, key_ok, land_query)
    outs = jnp.einsum('abhqk,abhkd->abhqd', probs.astype(jnp.float32), tiles(values))
    outs = outs * (1.0 - land_query)[..., None]
    outs = outs.astype(jnp.bfloat16).reshape(rows // 8, cols // 8, nh, 8, 8, hd)
    return outs.transpose(0, 3, 1, 4, 2, 5).reshape(rows, cols, width)

def row_attend(query, keys, values, flags):
    rows, length, width = query.shape
    nh = HEADS
    hd = width // nh
    scale = hd ** (-0.5)
    key_ok = (flags > 0)[:, None, :]
    land_query = (flags <= 0).astype(jnp.float32)

    def head(index):
        qh = lax.dynamic_slice_in_dim(query, index * hd, hd, 2).astype(jnp.float32)
        kh = lax.dynamic_slice_in_dim(keys, index * hd, hd, 2).astype(jnp.float32)
        vh = lax.dynamic_slice_in_dim(values, index * hd, hd, 2).astype(jnp.float32)
        scores = jnp.einsum('rqd,rkd->rqk', qh, kh) * scale
        probs = masked_softmax(scores, key_ok, land_query)
        return jnp.einsum('rqk,rkd->rqd', probs.astype(jnp.float32), vh)
    outs = lax.map(head, jnp.arange(nh, dtype=jnp.int32))
    outs = outs.transpose(1, 2, 0, 3).reshape(rows, length, width)
    return (outs * (1.0 - land_query)[..., None]).astype(jnp.bfloat16)

def reference(fields, ocean, w_query1, w_key1, w_value1, w_out1, w_query2, w_key2, w_value2, w_out2):
    h1 = jnp.roll(norm_rows(fields), -4, 1)
    marks = jnp.roll(ocean, -4, 1)
    q1 = project(h1, w_query1)
    k1 = project(h1, w_key1)
    v1 = project(h1, w_value1)
    lats, lons, width = q1.shape

    def band(items):
        return window_attend(items[0], items[1], items[2], items[3])
    grouped = (q1.reshape(lats // 8, 8, lons, width), k1.reshape(lats // 8, 8, lons, width), v1.reshape(lats // 8, 8, lons, width), marks.reshape(lats // 8, 8, lons))
    o1 = jnp.roll(lax.map(band, grouped).reshape(lats, lons, width), 4, 1)
    y1 = (fields.astype(jnp.float32) + jnp.dot(o1, w_out1, preferred_element_type=jnp.float32)).astype(jnp.bfloat16)
    h2 = norm_rows(y1)
    q2 = project(h2, w_query2)
    k2 = project(h2, w_key2)
    v2 = project(h2, w_value2)

    def one_row(items):
        return row_attend(items[0][None], items[1][None], items[2][None], items[3][None])[0]
    o2 = lax.map(one_row, (q2, k2, v2, ocean))
    return (y1.astype(jnp.float32) + jnp.dot(o2, w_out2, preferred_element_type=jnp.float32)).astype(jnp.bfloat16)
```

```python
import functools

import jax
import jax.numpy as jnp
from jax import lax
from jax.experimental import pallas as pl
from jax.experimental.pallas import tpu as pltpu
from jax.sharding import PartitionSpec as P

HEADS = 12


EPS = 1e-05
NEG = -1e30

GROUPS = (4, 4)


def passed_along(value, axis, steps):
    count = lax.axis_size(axis)
    pairs = [(source, (source + steps) % count) for source in range(count)]
    return lax.ppermute(value, axis, pairs)


def norm_rows(a):
    af = a.astype(jnp.float32)
    mean = jnp.mean(af, -1, keepdims=True)
    var = jnp.mean((af - mean) * (af - mean), -1, keepdims=True)
    return ((af - mean) * lax.rsqrt(var + EPS)).astype(jnp.bfloat16)


def project(h, weight):
    return jnp.dot(h, weight, preferred_element_type=jnp.float32).astype(jnp.bfloat16)


def masked_softmax(scores, key_ok, land_query):
    top = jnp.max(jnp.where(key_ok, scores, NEG), -1, keepdims=True)
    expo = jnp.where(key_ok, jnp.exp(scores - top), 0.0)
    total = jnp.sum(expo, -1, keepdims=True) + land_query[..., None]
    return (expo / total).astype(jnp.bfloat16)


def window_attend(query, keys, values, flags):
    rows, cols, width = query.shape
    nh = HEADS
    hd = width // nh
    scale = hd ** (-0.5)

    def tiles(a):
        a = a.reshape(rows // 8, 8, cols // 8, 8, nh, hd).transpose(0, 2, 4, 1, 3, 5)
        return a.reshape(rows // 8, cols // 8, nh, 64, hd)

    marks = (
        flags.reshape(rows // 8, 8, cols // 8, 8)
        .transpose(0, 2, 1, 3)
        .reshape(rows // 8, cols // 8, 64)
    )
    key_ok = (marks > 0)[:, :, None, None, :]
    land_query = (marks <= 0).astype(jnp.float32)[:, :, None, :]
    scores = (
        jnp.einsum(
            "abhqd,abhkd->abhqk", tiles(query), tiles(keys), preferred_element_type=jnp.float32
        )
        * scale
    )
    probs = masked_softmax(scores, key_ok, land_query)
    outs = jnp.einsum(
        "abhqk,abhkd->abhqd", probs, tiles(values), preferred_element_type=jnp.float32
    )
    outs = outs * (1.0 - land_query)[..., None]
    outs = outs.astype(jnp.bfloat16).reshape(rows // 8, cols // 8, nh, 8, 8, hd)
    return outs.transpose(0, 3, 1, 4, 2, 5).reshape(rows, cols, width)


def row_attend(query, keys, values, flags):
    rows, length, width = query.shape
    nh = HEADS
    hd = width // nh
    scale = hd ** (-0.5)
    key_ok = (flags > 0)[:, None, :]
    land_query = (flags <= 0).astype(jnp.float32)

    def head(index):
        qh = lax.dynamic_slice_in_dim(query, index * hd, hd, 2)
        kh = lax.dynamic_slice_in_dim(keys, index * hd, hd, 2)
        vh = lax.dynamic_slice_in_dim(values, index * hd, hd, 2)
        scores = jnp.einsum("rqd,rkd->rqk", qh, kh, preferred_element_type=jnp.float32) * scale
        probs = masked_softmax(scores, key_ok, land_query)
        return jnp.einsum("rqk,rkd->rqd", probs, vh, preferred_element_type=jnp.float32)

    outs = lax.map(head, jnp.arange(nh, dtype=jnp.int32))
    outs = outs.transpose(1, 2, 0, 3).reshape(rows, length, width)
    return (outs * (1.0 - land_query)[..., None]).astype(jnp.bfloat16)


def attend_columns(columns, marks, w_query1, w_key1, w_value1):
    return window_attend(
        project(columns, w_query1), project(columns, w_key1), project(columns, w_value1), marks
    )


def spread_rows(
    fields, ocean, w_query1, w_key1, w_value1, w_out1, w_query2, w_key2, w_value2, w_out2
):
    rows, cols, width = fields.shape
    normed = norm_rows(fields)
    marks = ocean.astype(jnp.bfloat16)
    edge_feats, edge_marks = passed_along((normed[:, cols - 4 :], marks[:, cols - 4 :]), "lon", 1)
    columns = jnp.concatenate([edge_feats, normed[:, : cols - 4]], 1)
    column_marks = jnp.concatenate([edge_marks, marks[:, : cols - 4]], 1)
    extended = attend_columns(columns, column_marks, w_query1, w_key1, w_value1)
    returned = passed_along(extended[:, :4], "lon", -1)
    o1 = jnp.concatenate([extended[:, 4:], returned], 1)
    y1 = (
        fields.astype(jnp.float32) + jnp.dot(o1, w_out1, preferred_element_type=jnp.float32)
    ).astype(jnp.bfloat16)
    h2 = norm_rows(y1)
    q2 = project(h2, w_query2)
    k2 = project(h2, w_key2)
    v2 = project(h2, w_value2)
    row_q, row_k, row_v, row_marks = (
        lax.all_to_all(q2, "lon", split_axis=0, concat_axis=1, tiled=True),
        lax.all_to_all(k2, "lon", split_axis=0, concat_axis=1, tiled=True),
        lax.all_to_all(v2, "lon", split_axis=0, concat_axis=1, tiled=True),
        lax.all_to_all(marks, "lon", split_axis=0, concat_axis=1, tiled=True),
    )
    row_out = row_attend(row_q, row_k, row_v, row_marks)
    o2 = lax.all_to_all(row_out, "lon", split_axis=1, concat_axis=0, tiled=True)
    return (
        y1.astype(jnp.float32) + jnp.dot(o2, w_out2, preferred_element_type=jnp.float32)
    ).astype(jnp.bfloat16)


def normed_f32(a):
    mean = jnp.mean(a, -1, keepdims=True)
    centred = a - mean
    var = jnp.mean(centred * centred, -1, keepdims=True)
    return (centred * lax.rsqrt(var + EPS)).astype(jnp.bfloat16)


def dot_f32(a, b):
    return jnp.dot(a, b, preferred_element_type=jnp.float32)


def pair_attend(q, k, v, key_bias, land_query):
    n = q.shape[0]
    low = lax.broadcasted_iota(jnp.int32, (n, 128), 1) < 64
    zero = jnp.zeros_like(q)
    both = jnp.concatenate([jnp.where(low, q, zero), jnp.where(low, zero, q)], 0)
    scores = lax.dot_general(both, k, (((1,), (1,)), ((), ())), preferred_element_type=jnp.float32)
    scores = scores + key_bias
    top = jnp.max(scores, -1, keepdims=True)
    expo = jnp.exp(scores - top).astype(jnp.bfloat16)
    wide = jnp.concatenate([v, jnp.ones_like(v)], 1)
    sums = dot_f32(expo, wide)
    upper = jnp.where(low, sums[:n, :128], sums[n:, :128])
    total = jnp.where(low, sums[:n, 128:], sums[n:, 128:]) + land_query
    return (upper / total * (1.0 - land_query)).astype(jnp.bfloat16)


def window_kernel(straddling, count, x_ref, bias_ref, land_ref, wq, wk, wv, wo, wq2, wk2, wv2,
                  y_ref, q2_ref, k2_ref, v2_ref, held, q_s, k_s, v_s, o_s, rows_s, sems):
    width = x_ref.shape[-1]
    scale = (width // HEADS) ** (-0.5)
    copies = [
        pltpu.make_async_copy(source, held.at[i], sems.at[i])
        for i, source in enumerate((wq, wk, wv, wo, wq2, wk2, wv2))
    ]
    for copy in copies:
        copy.start()
    x = x_ref[...].astype(jnp.float32)
    if straddling:
        column = lax.broadcasted_iota(jnp.int32, x.shape, 0) % 8
        x = jnp.where(column < 4, x, jnp.concatenate([x[64:], x[:64]], 0))
    h = normed_f32(x)
    copies[0].wait()
    q_s[...] = (dot_f32(h, held[0]) * scale).astype(jnp.bfloat16)
    copies[1].wait()
    k_s[...] = dot_f32(h, held[1]).astype(jnp.bfloat16)
    copies[2].wait()
    v_s[...] = dot_f32(h, held[2]).astype(jnp.bfloat16)
    for w in range(count):
        here = slice(64 * w, 64 * w + 64)
        for p in range(HEADS // 2):
            lanes = slice(128 * p, 128 * p + 128)
            o_s[here, lanes] = pair_attend(
                q_s[here, lanes], k_s[here, lanes], v_s[here, lanes],
                bias_ref[w : w + 1, :], land_ref[here, :],
            )
    copies[3].wait()
    y = (x + dot_f32(o_s[...], held[3])).astype(jnp.bfloat16).astype(jnp.float32)
    for w in range(count):
        for r in range(8):
            at = 64 * w + 8 * r
            rows_s[r, 8 * w : 8 * w + 8, :] = y[at : at + 8]
    y = rows_s[...].reshape(8 * 8 * count, width)
    y_ref[...] = y.astype(jnp.bfloat16).reshape(y_ref.shape)
    h = normed_f32(y)
    copies[4].wait()
    q2_ref[...] = (dot_f32(h, held[4]) * scale).astype(jnp.bfloat16).reshape(q2_ref.shape)
    copies[5].wait()
    k2_ref[...] = dot_f32(h, held[5]).astype(jnp.bfloat16).reshape(k2_ref.shape)
    copies[6].wait()
    v2_ref[...] = dot_f32(h, held[6]).astype(jnp.bfloat16).reshape(v2_ref.shape)


def window_layer(straddling, x, bias, land, weights):
    count, width = bias.shape[0], x.shape[-1]
    tokens = 64 * count
    half = jax.ShapeDtypeStruct((8, 8 * count, width), jnp.bfloat16)
    vmem = pl.BlockSpec(memory_space=pltpu.VMEM)
    anywhere = pl.BlockSpec(memory_space=pl.ANY)
    work = pltpu.VMEM((tokens, width), jnp.bfloat16)
    return pl.pallas_call(
        functools.partial(window_kernel, straddling, count),
        out_shape=(half,) * 4,
        in_specs=[vmem] * 3 + [anywhere] * 7,
        out_specs=(vmem,) * 4,
        scratch_shapes=[
            pltpu.VMEM((7, width, width), jnp.bfloat16),
            work, work, work, work,
            pltpu.VMEM((8, 8 * count, width), jnp.float32),
            pltpu.SemaphoreType.DMA((7,)),
        ],
        compiler_params=pltpu.CompilerParams(vmem_limit_bytes=40 * 1024 * 1024),
        cost_estimate=pl.CostEstimate(
            flops=2 * tokens * width * (7 * width + 512), bytes_accessed=16 << 20, transcendentals=tokens * 64 * HEADS
        ),
        name="window_layer",
    )(x, bias, land, *weights)


def row_kernel(rows, count, ya, yb, qa, qb, ka, kb, va, vb, bias_ref, land_ref, wo, out_ref, held, o_s, sem):
    width = ya.shape[-1]
    length = 16 * count
    copy = pltpu.make_async_copy(wo, held, sem)
    copy.start()
    for r in range(rows):
        here = slice(length * r, length * r + length)
        for p in range(HEADS // 2):
            lanes = slice(128 * p, 128 * p + 128)
            q = jnp.concatenate([qa[r, :, lanes], qb[r, :, lanes]], 0)
            k = jnp.concatenate([ka[r, :, lanes], kb[r, :, lanes]], 0)
            v = jnp.concatenate([va[r, :, lanes], vb[r, :, lanes]], 0)
            o_s[here, lanes] = pair_attend(q, k, v, bias_ref[r : r + 1, :], land_ref[here, :])
    copy.wait()
    added = dot_f32(o_s[...], held[...])
    for r in range(rows):
        at = length * r
        fa = added[at : at + 8 * count] + ya[r].astype(jnp.float32)
        fb = added[at + 8 * count : at + length] + yb[r].astype(jnp.float32)
        column = lax.broadcasted_iota(jnp.int32, (8, width), 0)
        for d in range(count):
            before = (d + count - 1) % count
            a = fa[8 * d : 8 * d + 8]
            first = jnp.where(column < 4, a, fb[8 * before : 8 * before + 8])
            last = jnp.where(column < 4, fb[8 * d : 8 * d + 8], a)
            out_ref[d, r] = jnp.concatenate(
                [pltpu.roll(first, 4, 0), pltpu.roll(last, 4, 0)], 0
            ).astype(jnp.bfloat16)


def row_layer(start, rows, count, halves, bias, land, w_out):
    ya = halves[0]
    width = ya.shape[-1]
    length = 16 * count
    vmem = pl.BlockSpec(memory_space=pltpu.VMEM)
    anywhere = pl.BlockSpec(memory_space=pl.ANY)
    step = start // rows
    half = pl.BlockSpec((rows, 8 * count, width), lambda i: (step, 0, 0))
    return pl.pallas_call(
        functools.partial(row_kernel, rows, count),
        out_shape=jax.ShapeDtypeStruct((count, rows, 16, width), jnp.bfloat16),
        grid=(1,),
        in_specs=[half] * 8 + [
            pl.BlockSpec((rows, length), lambda i: (0, 0)),
            pl.BlockSpec((rows * length, 1), lambda i: (0, 0)),
            anywhere,
        ],
        out_specs=pl.BlockSpec((count, rows, 16, width), lambda i: (0, 0, 0, 0)),
        scratch_shapes=[
            pltpu.VMEM((width, width), jnp.bfloat16),
            pltpu.VMEM((rows * length, width), jnp.bfloat16),
            pltpu.SemaphoreType.DMA,
        ],
        compiler_params=pltpu.CompilerParams(vmem_limit_bytes=40 * 1024 * 1024),
        cost_estimate=pl.CostEstimate(
            flops=2 * rows * length * width * (width + 1024), bytes_accessed=8 << 20,
            transcendentals=rows * length * length * HEADS,
        ),
        name="row_layer",
    )(*halves, bias[start : start + rows], land[start * length : (start + rows) * length], w_out)


def gathered_bands(
    fields, ocean, w_query1, w_key1, w_value1, w_out1, w_query2, w_key2, w_value2, w_out2
):
    count = lax.axis_size("lon")
    me = lax.axis_index("lon")

    def regroup(a):
        return lax.all_to_all(a, "lon", split_axis=0, concat_axis=0, tiled=True)

    marks = lax.all_gather(ocean, "lon", axis=1, tiled=True)
    rows, cols, width = fields.shape
    first = regroup(fields[:, 4:12])
    second = regroup(jnp.concatenate([fields[:, 12:], fields[:, :4]], 1))

    band = lax.dynamic_slice_in_dim(marks, 8 * me, 8, 0)
    band = jnp.roll(band, -4, 1).reshape(8, count, 2, 8)
    land = (band <= 0).astype(jnp.float32)
    by_window = land.transpose(2, 1, 0, 3).reshape(2, count, 64)
    by_row = land.transpose(0, 2, 1, 3).reshape(8, 16 * count)

    weights = (w_query1, w_key1, w_value1, w_out1, w_query2, w_key2, w_value2)
    halves = [
        window_layer(
            i == 1, x.reshape(64 * count, width), by_window[i] * NEG, by_window[i].reshape(64 * count, 1), weights
        )
        for i, x in enumerate((first, second))
    ]
    joined = [half for pair in zip(*halves) for half in pair]
    parts, start = [], 0
    for size in GROUPS:
        sent = row_layer(start, size, count, joined, by_row * NEG, by_row.reshape(8 * 16 * count, 1), w_out2)
        back = regroup(sent.reshape(count * size, cols, width))
        parts.append(back.reshape(count, size, cols, width))
        start += size
    return jnp.concatenate(parts, 1).reshape(rows, cols, width)


def on_device(fields, *rest):
    rows, cols, width = fields.shape
    if rows == 8 * lax.axis_size("lon") and cols == 16 and width == 64 * HEADS:
        return gathered_bands(fields, *rest)
    return spread_rows(fields, *rest)


def solution(mesh):
    in_specs = (
        P(("grp", "lat"), "lon", None),
        P(("grp", "lat"), "lon"),
        P(),
        P(),
        P(),
        P(),
        P(),
        P(),
        P(),
        P(),
    )
    out_specs = P(("grp", "lat"), "lon", None)
    return jax.shard_map(
        on_device, mesh=mesh, in_specs=in_specs, out_specs=out_specs, check_vma=False
    )
```

```python
import functools

import jax
import jax.numpy as jnp
from jax import lax
from jax.experimental import pallas as pl
from jax.experimental.pallas import tpu as pltpu
from jax.sharding import PartitionSpec as P

HEADS = 12


EPS = 1e-05
NEG = -1e30

GROUPS = (4, 4)


def passed_along(value, axis, steps):
    count = lax.axis_size(axis)
    pairs = [(source, (source + steps) % count) for source in range(count)]
    return lax.ppermute(value, axis, pairs)


def norm_rows(a):
    af = a.astype(jnp.float32)
    mean = jnp.mean(af, -1, keepdims=True)
    var = jnp.mean((af - mean) * (af - mean), -1, keepdims=True)
    return ((af - mean) * lax.rsqrt(var + EPS)).astype(jnp.bfloat16)


def project(h, weight):
    return jnp.dot(h, weight, preferred_element_type=jnp.float32).astype(jnp.bfloat16)


def masked_softmax(scores, key_ok, land_query):
    top = jnp.max(jnp.where(key_ok, scores, NEG), -1, keepdims=True)
    expo = jnp.where(key_ok, jnp.exp(scores - top), 0.0)
    total = jnp.sum(expo, -1, keepdims=True) + land_query[..., None]
    return (expo / total).astype(jnp.bfloat16)


def window_attend(query, keys, values, flags):
    rows, cols, width = query.shape
    nh = HEADS
    hd = width // nh
    scale = hd ** (-0.5)

    def tiles(a):
        a = a.reshape(rows // 8, 8, cols // 8, 8, nh, hd).transpose(0, 2, 4, 1, 3, 5)
        return a.reshape(rows // 8, cols // 8, nh, 64, hd)

    marks = (
        flags.reshape(rows // 8, 8, cols // 8, 8)
        .transpose(0, 2, 1, 3)
        .reshape(rows // 8, cols // 8, 64)
    )
    key_ok = (marks > 0)[:, :, None, None, :]
    land_query = (marks <= 0).astype(jnp.float32)[:, :, None, :]
    scores = (
        jnp.einsum(
            "abhqd,abhkd->abhqk", tiles(query), tiles(keys), preferred_element_type=jnp.float32
        )
        * scale
    )
    probs = masked_softmax(scores, key_ok, land_query)
    outs = jnp.einsum(
        "abhqk,abhkd->abhqd", probs, tiles(values), preferred_element_type=jnp.float32
    )
    outs = outs * (1.0 - land_query)[..., None]
    outs = outs.astype(jnp.bfloat16).reshape(rows // 8, cols // 8, nh, 8, 8, hd)
    return outs.transpose(0, 3, 1, 4, 2, 5).reshape(rows, cols, width)


def row_attend(query, keys, values, flags):
    rows, length, width = query.shape
    nh = HEADS
    hd = width // nh
    scale = hd ** (-0.5)
    key_ok = (flags > 0)[:, None, :]
    land_query = (flags <= 0).astype(jnp.float32)

    def head(index):
        qh = lax.dynamic_slice_in_dim(query, index * hd, hd, 2)
        kh = lax.dynamic_slice_in_dim(keys, index * hd, hd, 2)
        vh = lax.dynamic_slice_in_dim(values, index * hd, hd, 2)
        scores = jnp.einsum("rqd,rkd->rqk", qh, kh, preferred_element_type=jnp.float32) * scale
        probs = masked_softmax(scores, key_ok, land_query)
        return jnp.einsum("rqk,rkd->rqd", probs, vh, preferred_element_type=jnp.float32)

    outs = lax.map(head, jnp.arange(nh, dtype=jnp.int32))
    outs = outs.transpose(1, 2, 0, 3).reshape(rows, length, width)
    return (outs * (1.0 - land_query)[..., None]).astype(jnp.bfloat16)


def attend_columns(columns, marks, w_query1, w_key1, w_value1):
    return window_attend(
        project(columns, w_query1), project(columns, w_key1), project(columns, w_value1), marks
    )


def spread_rows(
    fields, ocean, w_query1, w_key1, w_value1, w_out1, w_query2, w_key2, w_value2, w_out2
):
    rows, cols, width = fields.shape
    normed = norm_rows(fields)
    marks = ocean.astype(jnp.bfloat16)
    edge_feats, edge_marks = passed_along((normed[:, cols - 4 :], marks[:, cols - 4 :]), "lon", 1)
    columns = jnp.concatenate([edge_feats, normed[:, : cols - 4]], 1)
    column_marks = jnp.concatenate([edge_marks, marks[:, : cols - 4]], 1)
    extended = attend_columns(columns, column_marks, w_query1, w_key1, w_value1)
    returned = passed_along(extended[:, :4], "lon", -1)
    o1 = jnp.concatenate([extended[:, 4:], returned], 1)
    y1 = (
        fields.astype(jnp.float32) + jnp.dot(o1, w_out1, preferred_element_type=jnp.float32)
    ).astype(jnp.bfloat16)
    h2 = norm_rows(y1)
    q2 = project(h2, w_query2)
    k2 = project(h2, w_key2)
    v2 = project(h2, w_value2)
    row_q, row_k, row_v, row_marks = (
        lax.all_to_all(q2, "lon", split_axis=0, concat_axis=1, tiled=True),
        lax.all_to_all(k2, "lon", split_axis=0, concat_axis=1, tiled=True),
        lax.all_to_all(v2, "lon", split_axis=0, concat_axis=1, tiled=True),
        lax.all_to_all(marks, "lon", split_axis=0, concat_axis=1, tiled=True),
    )
    row_out = row_attend(row_q, row_k, row_v, row_marks)
    o2 = lax.all_to_all(row_out, "lon", split_axis=1, concat_axis=0, tiled=True)
    return (
        y1.astype(jnp.float32) + jnp.dot(o2, w_out2, preferred_element_type=jnp.float32)
    ).astype(jnp.bfloat16)


def normed_f32(a):
    mean = jnp.mean(a, -1, keepdims=True)
    centred = a - mean
    var = jnp.mean(centred * centred, -1, keepdims=True)
    return (centred * lax.rsqrt(var + EPS)).astype(jnp.bfloat16)


def dot_f32(a, b):
    return jnp.dot(a, b, preferred_element_type=jnp.float32)


def diagonal(n, m):
    return lax.broadcasted_iota(jnp.int32, (n, m), 0) == lax.broadcasted_iota(jnp.int32, (n, m), 1)


def low_columns(shape, axis):
    return lax.broadcasted_iota(jnp.int32, shape, axis) % 8 < 4


def key_bias_of(marks):
    n = marks.shape[0]
    land = (1.0 - marks[:, :n]) * NEG
    return jnp.sum(jnp.where(diagonal(n, n), land, 0.0), 0, keepdims=True)


def pair_attend(q, k, v, key_bias, land_query):
    n = q.shape[0]
    low = lax.broadcasted_iota(jnp.int32, (n, 128), 1) < 64
    zero = jnp.zeros_like(q)
    both = jnp.concatenate([jnp.where(low, q, zero), jnp.where(low, zero, q)], 0)
    scores = lax.dot_general(both, k, (((1,), (1,)), ((), ())), preferred_element_type=jnp.float32)
    scores = scores + key_bias
    top = jnp.max(scores, -1, keepdims=True)
    expo = jnp.exp(scores - top).astype(jnp.bfloat16)
    wide = jnp.concatenate([v, jnp.ones_like(v)], 1)
    sums = dot_f32(expo, wide)
    upper = jnp.where(low, sums[:n, :128], sums[n:, :128])
    total = jnp.where(low, sums[:n, 128:], sums[n:, 128:]) + land_query
    return (upper / total * (1.0 - land_query)).astype(jnp.bfloat16)


def pack_kernel(distances, me_ref, marks_ref, fields_ref, *refs):
    outs, (held, sems) = refs[: len(distances)], refs[len(distances) :]
    me = me_ref[0]
    tiles = fields_ref.shape[-1] // 128
    copies = []
    for i, d in enumerate(distances):
        there = jnp.bitwise_xor(me, d)
        copies.append(pltpu.make_async_copy(fields_ref.at[pl.ds(there * 8, 8)], held.at[i], sems.at[i]))
        copies[-1].start()
    for i, d in enumerate(distances):
        there = jnp.bitwise_xor(me, d)
        row = marks_ref[pl.ds(there, 1), :]
        outs[i][128 * tiles :, :] = jnp.broadcast_to(row, (16, 128)).astype(jnp.bfloat16)
        copies[i].wait()
        piece = held[i].reshape(128, 128 * tiles)
        for t in range(tiles):
            outs[i][128 * t : 128 * t + 128, :] = piece[:, 128 * t : 128 * t + 128]


def pack(distances, me, marks, fields):
    cols, width = fields.shape[1:]
    vmem = pl.BlockSpec(memory_space=pltpu.VMEM)
    piece = jax.ShapeDtypeStruct((width + 16, 128), jnp.bfloat16)
    n = len(distances)
    return pl.pallas_call(
        functools.partial(pack_kernel, distances),
        out_shape=(piece,) * n,
        in_specs=[pl.BlockSpec(memory_space=pltpu.SMEM), vmem, pl.BlockSpec(memory_space=pltpu.HBM)],
        out_specs=(vmem,) * n,
        scratch_shapes=[pltpu.VMEM((n, 8, cols, width), jnp.bfloat16), pltpu.SemaphoreType.DMA((n,))],
        compiler_params=pltpu.CompilerParams(vmem_limit_bytes=16 * 1024 * 1024),
        cost_estimate=pl.CostEstimate(flops=n * 200000, bytes_accessed=n * 400000, transcendentals=0),
        name="pack",
    )(me, marks, fields)


def unpacked(piece):
    tiles = (piece.shape[0] - 16) // 128
    lanes = [piece[128 * t : 128 * t + 128] for t in range(tiles)]
    row = piece[128 * tiles :].astype(jnp.float32)[:1]
    marks = jnp.sum(jnp.where(diagonal(128, 128), row, 0.0), 1, keepdims=True)
    marks = jnp.broadcast_to(marks, (128, 128)).astype(jnp.bfloat16)
    whole = jnp.concatenate(lanes + [marks], 1).astype(jnp.float32).reshape(8, 2, 8, 128 * tiles + 128)
    return whole[:, 0], whole[:, 1]


def window_kernel(stage, me_ref, *refs):
    if stage == 0:
        pieces, refs = refs[:4], refs[4:]
    else:
        (*pieces, edge0_ref, edge3_ref, tail_ref), refs = refs[:7], refs[7:]
    wq, wk, wv, wo, wq2, wk2, wv2 = refs[:7]
    if stage == 0:
        y_ref, q2_ref, k2_ref, v2_ref, m_ref, edge0_ref, edge3_ref, tail_ref = refs[7:15]
        refs = refs[15:]
    else:
        y_ref, q2_ref, k2_ref, v2_ref, m_ref = refs[7:12]
        refs = refs[12:]
    placed, q_s, k_s, v_s, o_s, rows_s = refs
    width = wq.shape[0]
    scale = (width // HEADS) ** (-0.5)
    low = jnp.bitwise_and(me_ref[0], 3)
    for d in range(4):
        placed[jnp.bitwise_xor(low, d)] = pieces[d][...]
    columns = [unpacked(placed[l]) for l in range(4)]
    mask = low_columns((8, 8, width + 128), 1)
    full = (64, width + 128)

    def whole_window(l):
        return jnp.where(mask, columns[l][1], columns[l][0]).reshape(full)

    def straddling_window(left, right):
        return jnp.where(mask, right, left).reshape(full)

    windows = [whole_window(0)]
    for l in range(1, 4):
        windows += [straddling_window(columns[l - 1][1], columns[l][0]), whole_window(l)]
    if stage == 0:
        edge0_ref[...] = columns[0][0].reshape(full)
        edge3_ref[...] = columns[3][1].reshape(full)
    else:
        windows = (
            [straddling_window(edge3_ref[...].reshape(8, 8, -1), columns[0][0])]
            + windows
            + [straddling_window(columns[3][1], edge0_ref[...].reshape(8, 8, -1))]
        )
    count = len(windows)
    x = jnp.concatenate([w[:, :width] for w in windows], 0)
    marks = [w[:, width:] for w in windows]
    h = normed_f32(x)
    q_s[...] = (dot_f32(h, wq[...]) * scale).astype(jnp.bfloat16)
    k_s[...] = dot_f32(h, wk[...]).astype(jnp.bfloat16)
    v_s[...] = dot_f32(h, wv[...]).astype(jnp.bfloat16)
    for w in range(count):
        here = slice(64 * w, 64 * w + 64)
        bias = key_bias_of(marks[w])
        land = 1.0 - marks[w]
        for p in range(HEADS // 2):
            lanes = slice(128 * p, 128 * p + 128)
            o_s[here, lanes] = pair_attend(q_s[here, lanes], k_s[here, lanes], v_s[here, lanes], bias, land)
    y = (x + dot_f32(o_s[...], wo[...])).astype(jnp.bfloat16).astype(jnp.float32)
    first = 0
    if stage == 1:
        first = 1
        rows_s[:, :8, :] = tail_ref[...]
    for w in range(count):
        for r in range(8):
            at = 64 * w + 8 * r
            to = 8 * (w + first)
            if stage == 0 and w == count - 1:
                tail_ref[r, :, :width] = y[at : at + 8]
                tail_ref[r, :, width:] = marks[w][8 * r : 8 * r + 8]
            else:
                rows_s[r, to : to + 8, :width] = y[at : at + 8]
                rows_s[r, to : to + 8, width:] = marks[w][8 * r : 8 * r + 8]
    tokens = rows_s.shape[0] * rows_s.shape[1]
    y = rows_s[:, :, :width].reshape(tokens, width)
    m_ref[...] = rows_s[:, :, width:].astype(jnp.bfloat16)
    y_ref[...] = y.astype(jnp.bfloat16).reshape(y_ref.shape)
    h = normed_f32(y)
    q2_ref[...] = (dot_f32(h, wq2[...]) * scale).astype(jnp.bfloat16).reshape(q2_ref.shape)
    k2_ref[...] = dot_f32(h, wk2[...]).astype(jnp.bfloat16).reshape(k2_ref.shape)
    v2_ref[...] = dot_f32(h, wv2[...]).astype(jnp.bfloat16).reshape(v2_ref.shape)


def window_layer(stage, me, pieces, carried, weights):
    width = weights[0].shape[0]
    tokens = 64 * (7, 9)[stage]
    columns = 8 * (6, 10)[stage]
    half = jax.ShapeDtypeStruct((8, columns, width), jnp.bfloat16)
    marks = jax.ShapeDtypeStruct((8, columns, 128), jnp.bfloat16)
    edge = jax.ShapeDtypeStruct((64, width + 128), jnp.float32)
    tail = jax.ShapeDtypeStruct((8, 8, width + 128), jnp.float32)
    outs = (half,) * 4 + (marks,) + ((edge, edge, tail) if stage == 0 else ())
    vmem = pl.BlockSpec(memory_space=pltpu.VMEM)
    work = pltpu.VMEM((tokens, width), jnp.bfloat16)
    inputs = [*pieces, *carried, *weights]
    return pl.pallas_call(
        functools.partial(window_kernel, stage),
        out_shape=outs,
        in_specs=[pl.BlockSpec(memory_space=pltpu.SMEM)] + [vmem] * len(inputs),
        out_specs=(vmem,) * len(outs),
        scratch_shapes=[
            pltpu.VMEM((4, width + 16, 128), jnp.bfloat16),
            work, work, work, work,
            pltpu.VMEM((8, columns, width + 128), jnp.float32),
        ],
        compiler_params=pltpu.CompilerParams(vmem_limit_bytes=36 * 1024 * 1024),
        cost_estimate=pl.CostEstimate(
            flops=2 * tokens * width * (7 * width + 512), bytes_accessed=16 << 20, transcendentals=tokens * 64 * HEADS
        ),
        name="window_layer",
    )(me, *inputs)


def row_kernel(rows, me_ref, *refs):
    (ya, qa, ka, va, ma, yb, qb, kb, vb, mb, wo), refs = refs[:11], refs[11:]
    outs, (o_s, placed) = refs[:8], refs[8:]
    width = wo.shape[0]
    length = ya.shape[1] + yb.shape[1]
    for r in range(rows):
        here = slice(length * r, length * r + length)
        marks = jnp.concatenate([ma[r], mb[r]], 0).astype(jnp.float32)
        bias = key_bias_of(marks)
        land = 1.0 - marks
        for p in range(HEADS // 2):
            lanes = slice(128 * p, 128 * p + 128)
            q = jnp.concatenate([qa[r, :, lanes], qb[r, :, lanes]], 0)
            k = jnp.concatenate([ka[r, :, lanes], kb[r, :, lanes]], 0)
            v = jnp.concatenate([va[r, :, lanes], vb[r, :, lanes]], 0)
            o_s[here, lanes] = pair_attend(q, k, v, bias, land)
    added = dot_f32(o_s[...], wo[...])
    mask = low_columns((8, width), 0)
    for r in range(rows):
        before = jnp.concatenate([ya[r], yb[r]], 0).astype(jnp.float32)
        f = before + added[length * r : length * r + length]
        tiles = [f[8 * w : 8 * w + 8] for w in range(16)]
        for l in range(8):
            placed[l, r] = jnp.concatenate(
                [
                    jnp.where(mask, tiles[(2 * l - 1) % 16], tiles[2 * l]),
                    jnp.where(mask, tiles[2 * l], tiles[2 * l + 1]),
                ],
                0,
            ).astype(jnp.bfloat16)
    low = jnp.bitwise_and(me_ref[0], 3)
    for d in range(8):
        outs[d][...] = placed[jnp.bitwise_xor(low, d)]


def row_layer(start, rows, me, halves, w_out):
    width = w_out.shape[0]
    step = start // rows
    length = 128

    def block(a):
        return pl.BlockSpec((rows,) + a.shape[1:], lambda i: (step, 0, 0))

    piece = jax.ShapeDtypeStruct((rows, 16, width), jnp.bfloat16)
    return pl.pallas_call(
        functools.partial(row_kernel, rows),
        out_shape=(piece,) * 8,
        grid=(1,),
        in_specs=[pl.BlockSpec(memory_space=pltpu.SMEM)]
        + [block(a) for a in halves]
        + [pl.BlockSpec((width, width), lambda i: (0, 0))],
        out_specs=(pl.BlockSpec(piece.shape, lambda i: (0, 0, 0)),) * 8,
        scratch_shapes=[
            pltpu.VMEM((rows * length, width), jnp.bfloat16),
            pltpu.VMEM((8, rows, 16, width), jnp.bfloat16),
        ],
        compiler_params=pltpu.CompilerParams(vmem_limit_bytes=32 * 1024 * 1024),
        cost_estimate=pl.CostEstimate(
            flops=2 * rows * length * width * (width + 1024), bytes_accessed=8 << 20,
            transcendentals=rows * length * length * HEADS,
        ),
        name="row_layer",
    )(me, *halves, w_out)


def place_kernel(start, rows, me_ref, *refs):
    pieces, out_ref, sems = refs[:8], refs[-2], refs[-1]
    copies = []
    for d in range(8):
        there = jnp.bitwise_xor(me_ref[0], d)
        copies.append(
            pltpu.make_async_copy(pieces[d], out_ref.at[pl.ds(there * 8 + start, rows)], sems.at[d])
        )
        copies[-1].start()
    for copy in copies:
        copy.wait()


def place(start, rows, me, pieces, so_far, shape):
    anywhere = pl.BlockSpec(memory_space=pl.ANY)
    hbm = pl.BlockSpec(memory_space=pltpu.HBM)
    more = () if so_far is None else (so_far,)
    return pl.pallas_call(
        functools.partial(place_kernel, start, rows),
        out_shape=jax.ShapeDtypeStruct(shape, jnp.bfloat16),
        in_specs=[pl.BlockSpec(memory_space=pltpu.SMEM)] + [anywhere] * 8 + [hbm] * len(more),
        out_specs=hbm,
        scratch_shapes=[pltpu.SemaphoreType.DMA((8,))],
        input_output_aliases={9: 0} if more else {},
        cost_estimate=pl.CostEstimate(flops=0, bytes_accessed=16 * rows * shape[1] * shape[2] * 2, transcendentals=0),
        name="place",
    )(me, *pieces, *more)


def exchanged(piece, distance):
    count = lax.axis_size("lon")
    return lax.ppermute(piece, "lon", [(s, s ^ distance) for s in range(count)])


def gathered_bands(
    fields, ocean, w_query1, w_key1, w_value1, w_out1, w_query2, w_key2, w_value2, w_out2
):
    me = lax.axis_index("lon").astype(jnp.int32).reshape(1)
    marks = ocean.reshape(8, 128).astype(jnp.float32)
    weights = (w_query1, w_key1, w_value1, w_out1, w_query2, w_key2, w_value2)

    order = (4, 5, 6, 7, 1, 2, 3, 0)
    packed = dict(zip(order, pack(order, me, marks, fields)))
    got = {d: exchanged(packed[d], d) if d else packed[d] for d in order}
    own = window_layer(0, me, [got[d] for d in range(4)], (), weights)
    other = window_layer(1, me, [got[d] for d in range(4, 8)], own[5:], weights)
    halves = (*own[:5], *other)
    start, out = 0, None
    for size in GROUPS:
        sent = row_layer(start, size, me, halves, w_out2)
        back = [exchanged(sent[d], d) if d else sent[d] for d in range(8)]
        out = place(start, size, me, back, out, fields.shape)
        start += size
    return out


def on_device(fields, *rest):
    rows, cols, width = fields.shape
    if lax.axis_size("lon") == 8 and rows == 64 and cols == 16 and width == 64 * HEADS:
        return gathered_bands(fields, *rest)
    return spread_rows(fields, *rest)


def solution(mesh):
    in_specs = (
        P(("grp", "lat"), "lon", None),
        P(("grp", "lat"), "lon"),
        P(),
        P(),
        P(),
        P(),
        P(),
        P(),
        P(),
        P(),
    )
    out_specs = P(("grp", "lat"), "lon", None)
    return jax.shard_map(
        on_device, mesh=mesh, in_specs=in_specs, out_specs=out_specs, check_vma=False
    )
```

```python
import functools

import jax
import jax.numpy as jnp
from jax import lax
from jax.experimental import pallas as pl
from jax.experimental.pallas import tpu as pltpu
from jax.sharding import PartitionSpec as P

HEADS = 12


EPS = 1e-05
NEG = -1e30

GROUPS = (4, 4)

PAIRS = [slice(128 * p, 128 * p + 128) for p in range(HEADS // 2)]


def passed_along(value, axis, steps):
    count = lax.axis_size(axis)
    pairs = [(source, (source + steps) % count) for source in range(count)]
    return lax.ppermute(value, axis, pairs)


def norm_rows(a):
    af = a.astype(jnp.float32)
    mean = jnp.mean(af, -1, keepdims=True)
    var = jnp.mean((af - mean) * (af - mean), -1, keepdims=True)
    return ((af - mean) * lax.rsqrt(var + EPS)).astype(jnp.bfloat16)


def project(h, weight):
    return jnp.dot(h, weight, preferred_element_type=jnp.float32).astype(jnp.bfloat16)


def masked_softmax(scores, key_ok, land_query):
    top = jnp.max(jnp.where(key_ok, scores, NEG), -1, keepdims=True)
    expo = jnp.where(key_ok, jnp.exp(scores - top), 0.0)
    total = jnp.sum(expo, -1, keepdims=True) + land_query[..., None]
    return (expo / total).astype(jnp.bfloat16)


def window_attend(query, keys, values, flags):
    rows, cols, width = query.shape
    nh = HEADS
    hd = width // nh
    scale = hd ** (-0.5)

    def tiles(a):
        a = a.reshape(rows // 8, 8, cols // 8, 8, nh, hd).transpose(0, 2, 4, 1, 3, 5)
        return a.reshape(rows // 8, cols // 8, nh, 64, hd)

    marks = (
        flags.reshape(rows // 8, 8, cols // 8, 8)
        .transpose(0, 2, 1, 3)
        .reshape(rows // 8, cols // 8, 64)
    )
    key_ok = (marks > 0)[:, :, None, None, :]
    land_query = (marks <= 0).astype(jnp.float32)[:, :, None, :]
    scores = (
        jnp.einsum(
            "abhqd,abhkd->abhqk", tiles(query), tiles(keys), preferred_element_type=jnp.float32
        )
        * scale
    )
    probs = masked_softmax(scores, key_ok, land_query)
    outs = jnp.einsum(
        "abhqk,abhkd->abhqd", probs, tiles(values), preferred_element_type=jnp.float32
    )
    outs = outs * (1.0 - land_query)[..., None]
    outs = outs.astype(jnp.bfloat16).reshape(rows // 8, cols // 8, nh, 8, 8, hd)
    return outs.transpose(0, 3, 1, 4, 2, 5).reshape(rows, cols, width)


def row_attend(query, keys, values, flags):
    rows, length, width = query.shape
    nh = HEADS
    hd = width // nh
    scale = hd ** (-0.5)
    key_ok = (flags > 0)[:, None, :]
    land_query = (flags <= 0).astype(jnp.float32)

    def head(index):
        qh = lax.dynamic_slice_in_dim(query, index * hd, hd, 2)
        kh = lax.dynamic_slice_in_dim(keys, index * hd, hd, 2)
        vh = lax.dynamic_slice_in_dim(values, index * hd, hd, 2)
        scores = jnp.einsum("rqd,rkd->rqk", qh, kh, preferred_element_type=jnp.float32) * scale
        probs = masked_softmax(scores, key_ok, land_query)
        return jnp.einsum("rqk,rkd->rqd", probs, vh, preferred_element_type=jnp.float32)

    outs = lax.map(head, jnp.arange(nh, dtype=jnp.int32))
    outs = outs.transpose(1, 2, 0, 3).reshape(rows, length, width)
    return (outs * (1.0 - land_query)[..., None]).astype(jnp.bfloat16)


def attend_columns(columns, marks, w_query1, w_key1, w_value1):
    return window_attend(
        project(columns, w_query1), project(columns, w_key1), project(columns, w_value1), marks
    )


def spread_rows(
    fields, ocean, w_query1, w_key1, w_value1, w_out1, w_query2, w_key2, w_value2, w_out2
):
    rows, cols, width = fields.shape
    normed = norm_rows(fields)
    marks = ocean.astype(jnp.bfloat16)
    edge_feats, edge_marks = passed_along((normed[:, cols - 4 :], marks[:, cols - 4 :]), "lon", 1)
    columns = jnp.concatenate([edge_feats, normed[:, : cols - 4]], 1)
    column_marks = jnp.concatenate([edge_marks, marks[:, : cols - 4]], 1)
    extended = attend_columns(columns, column_marks, w_query1, w_key1, w_value1)
    returned = passed_along(extended[:, :4], "lon", -1)
    o1 = jnp.concatenate([extended[:, 4:], returned], 1)
    y1 = (
        fields.astype(jnp.float32) + jnp.dot(o1, w_out1, preferred_element_type=jnp.float32)
    ).astype(jnp.bfloat16)
    h2 = norm_rows(y1)
    q2 = project(h2, w_query2)
    k2 = project(h2, w_key2)
    v2 = project(h2, w_value2)
    row_q, row_k, row_v, row_marks = (
        lax.all_to_all(q2, "lon", split_axis=0, concat_axis=1, tiled=True),
        lax.all_to_all(k2, "lon", split_axis=0, concat_axis=1, tiled=True),
        lax.all_to_all(v2, "lon", split_axis=0, concat_axis=1, tiled=True),
        lax.all_to_all(marks, "lon", split_axis=0, concat_axis=1, tiled=True),
    )
    row_out = row_attend(row_q, row_k, row_v, row_marks)
    o2 = lax.all_to_all(row_out, "lon", split_axis=1, concat_axis=0, tiled=True)
    return (
        y1.astype(jnp.float32) + jnp.dot(o2, w_out2, preferred_element_type=jnp.float32)
    ).astype(jnp.bfloat16)


def normed_f32(a):
    mean = jnp.mean(a, -1, keepdims=True)
    centred = a - mean
    var = jnp.mean(centred * centred, -1, keepdims=True)
    return (centred * lax.rsqrt(var + EPS)).astype(jnp.bfloat16)


def dot_f32(a, b):
    return jnp.dot(a, b, preferred_element_type=jnp.float32)


def diagonal(n, m):
    return lax.broadcasted_iota(jnp.int32, (n, m), 0) == lax.broadcasted_iota(jnp.int32, (n, m), 1)


def low_columns(shape, axis):
    return lax.broadcasted_iota(jnp.int32, shape, axis) % 8 < 4


def attend(queries, keys, values, marks):
    n = marks.shape[0]
    low = lax.broadcasted_iota(jnp.int32, (n, 128), 1) < 64
    land = 1.0 - marks
    bias = jnp.concatenate([land * NEG] * (2 * n // 128), 1)
    scores = []
    for q, k in zip(queries, keys):
        zero = jnp.zeros_like(q)
        both = jnp.concatenate([jnp.where(low, q, zero), jnp.where(low, zero, q)], 0)
        scores.append(lax.dot_general(k, both, (((1,), (1,)), ((), ())), preferred_element_type=jnp.float32) + bias)
    expos = [jnp.exp(s - jnp.max(s, 0, keepdims=True)).astype(jnp.bfloat16) for s in scores]
    outs = []
    for expo, v in zip(expos, values):
        wide = jnp.concatenate([v, jnp.ones_like(v)], 1)
        sums = lax.dot_general(expo, wide, (((0,), (0,)), ((), ())), preferred_element_type=jnp.float32)
        upper = jnp.where(low, sums[:n, :128], sums[n:, :128])
        total = jnp.where(low, sums[:n, 128:], sums[n:, 128:]) + land
        outs.append((upper / total * marks).astype(jnp.bfloat16))
    return outs


ORDER = (4, 5, 6, 7, 1, 2, 3, 0)


def pack_kernel(distances, me_ref, marks_ref, fields_ref, *refs):
    outs, (held, sems) = refs[: len(distances)], refs[len(distances) :]
    me = me_ref[0]
    tiles = fields_ref.shape[-1] // 128
    copies = []
    for i, d in enumerate(distances):
        there = jnp.bitwise_xor(me, d)
        copies.append(pltpu.make_async_copy(fields_ref.at[pl.ds(there * 8, 8)], held.at[i], sems.at[i]))
        copies[-1].start()
    for i, d in enumerate(distances):
        there = jnp.bitwise_xor(me, d)
        row = marks_ref[pl.ds(there, 1), :]
        outs[i][128 * tiles :, :] = jnp.broadcast_to(row, (16, 128)).astype(jnp.bfloat16)
        copies[i].wait()
        piece = held[i].reshape(128, 128 * tiles)
        for t in range(tiles):
            outs[i][128 * t : 128 * t + 128, :] = piece[:, 128 * t : 128 * t + 128]


def pack(distances, me, marks, fields):
    cols, width = fields.shape[1:]
    vmem = pl.BlockSpec(memory_space=pltpu.VMEM)
    piece = jax.ShapeDtypeStruct((width + 16, 128), jnp.bfloat16)
    n = len(distances)
    return pl.pallas_call(
        functools.partial(pack_kernel, distances),
        out_shape=(piece,) * n,
        in_specs=[pl.BlockSpec(memory_space=pltpu.SMEM), vmem, pl.BlockSpec(memory_space=pltpu.HBM)],
        out_specs=(vmem,) * n,
        scratch_shapes=[pltpu.VMEM((n, 8, cols, width), jnp.bfloat16), pltpu.SemaphoreType.DMA((n,))],
        compiler_params=pltpu.CompilerParams(vmem_limit_bytes=16 * 1024 * 1024),
        cost_estimate=pl.CostEstimate(flops=n * 200000, bytes_accessed=n * 400000, transcendentals=0),
        name="pack",
    )(me, marks, fields)


def unpacked(piece):
    tiles = (piece.shape[0] - 16) // 128
    lanes = [piece[128 * t : 128 * t + 128] for t in range(tiles)]
    row = piece[128 * tiles :].astype(jnp.float32)[:1]
    marks = jnp.sum(jnp.where(diagonal(128, 128), row, 0.0), 1, keepdims=True)
    marks = jnp.broadcast_to(marks, (128, 128)).astype(jnp.bfloat16)
    whole = jnp.concatenate(lanes + [marks], 1).astype(jnp.float32).reshape(8, 2, 8, 128 * tiles + 128)
    return whole[:, 0], whole[:, 1]


def window_kernel(stage, me_ref, *refs):
    if stage == 0:
        pieces, refs = refs[:4], refs[4:]
    else:
        (*pieces, edge0_ref, edge3_ref, tail_ref), refs = refs[:7], refs[7:]
    wq, wk, wv, wo, wq2, wk2, wv2 = refs[:7]
    if stage == 0:
        y_ref, q2_ref, k2_ref, v2_ref, m_ref, edge0_ref, edge3_ref, tail_ref = refs[7:15]
        refs = refs[15:]
    else:
        y_ref, q2_ref, k2_ref, v2_ref, m_ref = refs[7:12]
        refs = refs[12:]
    placed, q_s, k_s, v_s, o_s, rows_s = refs
    width = wq.shape[0]
    scale = (width // HEADS) ** (-0.5)
    low = jnp.bitwise_and(me_ref[0], 3)
    for d in range(4):
        placed[jnp.bitwise_xor(low, d)] = pieces[d][...]
    columns = [unpacked(placed[l]) for l in range(4)]
    mask = low_columns((8, 8, width + 128), 1)
    full = (64, width + 128)

    def whole_window(l):
        return jnp.where(mask, columns[l][1], columns[l][0]).reshape(full)

    def straddling_window(left, right):
        return jnp.where(mask, right, left).reshape(full)

    windows = [whole_window(0)]
    for l in range(1, 4):
        windows += [straddling_window(columns[l - 1][1], columns[l][0]), whole_window(l)]
    if stage == 0:
        edge0_ref[...] = columns[0][0].reshape(full)
        edge3_ref[...] = columns[3][1].reshape(full)
    else:
        windows = (
            [straddling_window(edge3_ref[...].reshape(8, 8, -1), columns[0][0])]
            + windows
            + [straddling_window(columns[3][1], edge0_ref[...].reshape(8, 8, -1))]
        )
    count = len(windows)
    x = jnp.concatenate([w[:, :width] for w in windows], 0)
    marks = [w[:, width:] for w in windows]
    h = normed_f32(x)
    q_s[...] = (dot_f32(h, wq[...]) * scale).astype(jnp.bfloat16)
    k_s[...] = dot_f32(h, wk[...]).astype(jnp.bfloat16)
    v_s[...] = dot_f32(h, wv[...]).astype(jnp.bfloat16)
    for w in range(count):
        here = slice(64 * w, 64 * w + 64)
        outs = attend(*([a[here, lanes] for lanes in PAIRS] for a in (q_s, k_s, v_s)), marks[w])
        for lanes, out in zip(PAIRS, outs):
            o_s[here, lanes] = out
    y = (x + dot_f32(o_s[...], wo[...])).astype(jnp.bfloat16).astype(jnp.float32)
    first = 0
    if stage == 1:
        first = 1
        rows_s[:, :8, :] = tail_ref[...]
    for w in range(count):
        for r in range(8):
            at = 64 * w + 8 * r
            to = 8 * (w + first)
            if stage == 0 and w == count - 1:
                tail_ref[r, :, :width] = y[at : at + 8]
                tail_ref[r, :, width:] = marks[w][8 * r : 8 * r + 8]
            else:
                rows_s[r, to : to + 8, :width] = y[at : at + 8]
                rows_s[r, to : to + 8, width:] = marks[w][8 * r : 8 * r + 8]
    tokens = rows_s.shape[0] * rows_s.shape[1]
    y = rows_s[:, :, :width].reshape(tokens, width)
    m_ref[...] = rows_s[:, :, width:].astype(jnp.bfloat16)
    y_ref[...] = y.astype(jnp.bfloat16).reshape(y_ref.shape)
    h = normed_f32(y)
    q2_ref[...] = (dot_f32(h, wq2[...]) * scale).astype(jnp.bfloat16).reshape(q2_ref.shape)
    k2_ref[...] = dot_f32(h, wk2[...]).astype(jnp.bfloat16).reshape(k2_ref.shape)
    v2_ref[...] = dot_f32(h, wv2[...]).astype(jnp.bfloat16).reshape(v2_ref.shape)


def window_layer(stage, me, pieces, carried, weights):
    width = weights[0].shape[0]
    tokens = 64 * (7, 9)[stage]
    columns = 8 * (6, 10)[stage]
    half = jax.ShapeDtypeStruct((8, columns, width), jnp.bfloat16)
    marks = jax.ShapeDtypeStruct((8, columns, 128), jnp.bfloat16)
    edge = jax.ShapeDtypeStruct((64, width + 128), jnp.float32)
    tail = jax.ShapeDtypeStruct((8, 8, width + 128), jnp.float32)
    outs = (half,) * 4 + (marks,) + ((edge, edge, tail) if stage == 0 else ())
    vmem = pl.BlockSpec(memory_space=pltpu.VMEM)
    work = pltpu.VMEM((tokens, width), jnp.bfloat16)
    inputs = [*pieces, *carried, *weights]
    return pl.pallas_call(
        functools.partial(window_kernel, stage),
        out_shape=outs,
        in_specs=[pl.BlockSpec(memory_space=pltpu.SMEM)] + [vmem] * len(inputs),
        out_specs=(vmem,) * len(outs),
        scratch_shapes=[
            pltpu.VMEM((4, width + 16, 128), jnp.bfloat16),
            work, work, work, work,
            pltpu.VMEM((8, columns, width + 128), jnp.float32),
        ],
        compiler_params=pltpu.CompilerParams(vmem_limit_bytes=36 * 1024 * 1024),
        cost_estimate=pl.CostEstimate(
            flops=2 * tokens * width * (7 * width + 512), bytes_accessed=16 << 20, transcendentals=tokens * 64 * HEADS
        ),
        name="window_layer",
    )(me, *inputs)


def row_kernel(rows, me_ref, *refs):
    (yb, qb, kb, vb, mb, ya, qa, ka, va, ma, wo), refs = refs[:11], refs[11:]
    outs, (o_s, placed) = refs[:8], refs[8:]
    width = wo.shape[0]
    length = ya.shape[1] + yb.shape[1]
    for r in range(rows):
        here = slice(length * r, length * r + length)
        marks = jnp.concatenate([ma[r], mb[r]], 0).astype(jnp.float32)
        heads = attend(
            *(
                [jnp.concatenate([a[r, :, lanes], b[r, :, lanes]], 0) for lanes in PAIRS]
                for a, b in ((qa, qb), (ka, kb), (va, vb))
            ),
            marks,
        )
        for lanes, out in zip(PAIRS, heads):
            o_s[here, lanes] = out
    added = dot_f32(o_s[...], wo[...])
    mask = low_columns((8, width), 0)
    for r in range(rows):
        before = jnp.concatenate([ya[r], yb[r]], 0).astype(jnp.float32)
        f = before + added[length * r : length * r + length]
        tiles = [f[8 * w : 8 * w + 8] for w in range(16)]
        for l in range(8):
            placed[l, r] = jnp.concatenate(
                [
                    jnp.where(mask, tiles[(2 * l - 1) % 16], tiles[2 * l]),
                    jnp.where(mask, tiles[2 * l], tiles[2 * l + 1]),
                ],
                0,
            ).astype(jnp.bfloat16)
    low = jnp.bitwise_and(me_ref[0], 3)
    for i, d in enumerate(ORDER):
        outs[i][...] = placed[jnp.bitwise_xor(low, d)]


def row_layer(start, rows, me, halves, w_out):
    width = w_out.shape[0]
    step = start // rows
    length = 128

    def block(a):
        return pl.BlockSpec((rows,) + a.shape[1:], lambda i: (step, 0, 0))

    piece = jax.ShapeDtypeStruct((rows, 16, width), jnp.bfloat16)
    return pl.pallas_call(
        functools.partial(row_kernel, rows),
        out_shape=(piece,) * 8,
        grid=(1,),
        in_specs=[pl.BlockSpec(memory_space=pltpu.SMEM)]
        + [block(a) for a in halves]
        + [pl.BlockSpec((width, width), lambda i: (0, 0))],
        out_specs=(pl.BlockSpec(piece.shape, lambda i: (0, 0, 0)),) * 8,
        scratch_shapes=[
            pltpu.VMEM((rows * length, width), jnp.bfloat16),
            pltpu.VMEM((8, rows, 16, width), jnp.bfloat16),
        ],
        compiler_params=pltpu.CompilerParams(vmem_limit_bytes=32 * 1024 * 1024),
        cost_estimate=pl.CostEstimate(
            flops=2 * rows * length * width * (width + 1024), bytes_accessed=8 << 20,
            transcendentals=rows * length * length * HEADS,
        ),
        name="row_layer",
    )(me, *halves, w_out)


def place_kernel(start, rows, me_ref, *refs):
    pieces, out_ref, sems = refs[:8], refs[-2], refs[-1]
    copies = []
    for i, d in enumerate(ORDER):
        there = jnp.bitwise_xor(me_ref[0], d)
        copies.append(
            pltpu.make_async_copy(pieces[i], out_ref.at[pl.ds(there * 8 + start, rows)], sems.at[i])
        )
        copies[-1].start()
    for copy in copies:
        copy.wait()


def place(start, rows, me, pieces, so_far, shape):
    vmem = pl.BlockSpec(memory_space=pltpu.VMEM)
    hbm = pl.BlockSpec(memory_space=pltpu.HBM)
    more = () if so_far is None else (so_far,)
    return pl.pallas_call(
        functools.partial(place_kernel, start, rows),
        out_shape=jax.ShapeDtypeStruct(shape, jnp.bfloat16),
        in_specs=[pl.BlockSpec(memory_space=pltpu.SMEM)] + [vmem] * 8 + [hbm] * len(more),
        out_specs=hbm,
        scratch_shapes=[pltpu.SemaphoreType.DMA((8,))],
        input_output_aliases={9: 0} if more else {},
        cost_estimate=pl.CostEstimate(flops=0, bytes_accessed=16 * rows * shape[1] * shape[2] * 2, transcendentals=0),
        name="place",
    )(me, *pieces, *more)


def exchanged(piece, distance):
    count = lax.axis_size("lon")
    return lax.ppermute(piece, "lon", [(s, s ^ distance) for s in range(count)])


def gathered_bands(
    fields, ocean, w_query1, w_key1, w_value1, w_out1, w_query2, w_key2, w_value2, w_out2
):
    me = lax.axis_index("lon").astype(jnp.int32).reshape(1)
    marks = ocean.reshape(8, 128).astype(jnp.float32)
    weights = (w_query1, w_key1, w_value1, w_out1, w_query2, w_key2, w_value2)

    packed = dict(zip(ORDER, pack(ORDER, me, marks, fields)))
    got = {d: exchanged(packed[d], d) if d else packed[d] for d in ORDER}
    own = window_layer(0, me, [got[d] for d in range(4)], (), weights)
    other = window_layer(1, me, [got[d] for d in range(4, 8)], own[5:], weights)
    halves = (*other, *own[:5])
    start, out, back = 0, None, None
    for size in GROUPS:
        sent = list(row_layer(start, size, me, halves, w_out2))
        if back is not None:
            for i in range(7):
                sent[i], back[i] = lax.optimization_barrier((sent[i], back[i]))
            out = place(start - size, size, me, back, out, fields.shape)
        back = [exchanged(piece, d) if d else piece for d, piece in zip(ORDER, sent)]
        start += size
    return place(start - size, size, me, back, out, fields.shape)


def on_device(fields, *rest):
    rows, cols, width = fields.shape
    if lax.axis_size("lon") == 8 and rows == 64 and cols == 16 and width == 64 * HEADS:
        return gathered_bands(fields, *rest)
    return spread_rows(fields, *rest)


def solution(mesh):
    in_specs = (
        P(("grp", "lat"), "lon", None),
        P(("grp", "lat"), "lon"),
        P(),
        P(),
        P(),
        P(),
        P(),
        P(),
        P(),
        P(),
    )
    out_specs = P(("grp", "lat"), "lon", None)
    return jax.shard_map(
        on_device, mesh=mesh, in_specs=in_specs, out_specs=out_specs, check_vma=False
    )
```

```python
import functools

import jax
import jax.numpy as jnp
from jax import lax
from jax.experimental import pallas as pl
from jax.experimental.pallas import tpu as pltpu
from jax.sharding import PartitionSpec as P

HEADS = 12


EPS = 1e-05
NEG = -1e30

GROUPS = (4, 4)

PAIRS = [slice(128 * p, 128 * p + 128) for p in range(HEADS // 2)]


def passed_along(value, axis, steps):
    count = lax.axis_size(axis)
    pairs = [(source, (source + steps) % count) for source in range(count)]
    return lax.ppermute(value, axis, pairs)


def norm_rows(a):
    af = a.astype(jnp.float32)
    mean = jnp.mean(af, -1, keepdims=True)
    var = jnp.mean((af - mean) * (af - mean), -1, keepdims=True)
    return ((af - mean) * lax.rsqrt(var + EPS)).astype(jnp.bfloat16)


def project(h, weight):
    return jnp.dot(h, weight, preferred_element_type=jnp.float32).astype(jnp.bfloat16)


def masked_softmax(scores, key_ok, land_query):
    top = jnp.max(jnp.where(key_ok, scores, NEG), -1, keepdims=True)
    expo = jnp.where(key_ok, jnp.exp(scores - top), 0.0)
    total = jnp.sum(expo, -1, keepdims=True) + land_query[..., None]
    return (expo / total).astype(jnp.bfloat16)


def window_attend(query, keys, values, flags):
    rows, cols, width = query.shape
    nh = HEADS
    hd = width // nh
    scale = hd ** (-0.5)

    def tiles(a):
        a = a.reshape(rows // 8, 8, cols // 8, 8, nh, hd).transpose(0, 2, 4, 1, 3, 5)
        return a.reshape(rows // 8, cols // 8, nh, 64, hd)

    marks = (
        flags.reshape(rows // 8, 8, cols // 8, 8)
        .transpose(0, 2, 1, 3)
        .reshape(rows // 8, cols // 8, 64)
    )
    key_ok = (marks > 0)[:, :, None, None, :]
    land_query = (marks <= 0).astype(jnp.float32)[:, :, None, :]
    scores = (
        jnp.einsum(
            "abhqd,abhkd->abhqk", tiles(query), tiles(keys), preferred_element_type=jnp.float32
        )
        * scale
    )
    probs = masked_softmax(scores, key_ok, land_query)
    outs = jnp.einsum(
        "abhqk,abhkd->abhqd", probs, tiles(values), preferred_element_type=jnp.float32
    )
    outs = outs * (1.0 - land_query)[..., None]
    outs = outs.astype(jnp.bfloat16).reshape(rows // 8, cols // 8, nh, 8, 8, hd)
    return outs.transpose(0, 3, 1, 4, 2, 5).reshape(rows, cols, width)


def row_attend(query, keys, values, flags):
    rows, length, width = query.shape
    nh = HEADS
    hd = width // nh
    scale = hd ** (-0.5)
    key_ok = (flags > 0)[:, None, :]
    land_query = (flags <= 0).astype(jnp.float32)

    def head(index):
        qh = lax.dynamic_slice_in_dim(query, index * hd, hd, 2)
        kh = lax.dynamic_slice_in_dim(keys, index * hd, hd, 2)
        vh = lax.dynamic_slice_in_dim(values, index * hd, hd, 2)
        scores = jnp.einsum("rqd,rkd->rqk", qh, kh, preferred_element_type=jnp.float32) * scale
        probs = masked_softmax(scores, key_ok, land_query)
        return jnp.einsum("rqk,rkd->rqd", probs, vh, preferred_element_type=jnp.float32)

    outs = lax.map(head, jnp.arange(nh, dtype=jnp.int32))
    outs = outs.transpose(1, 2, 0, 3).reshape(rows, length, width)
    return (outs * (1.0 - land_query)[..., None]).astype(jnp.bfloat16)


def attend_columns(columns, marks, w_query1, w_key1, w_value1):
    return window_attend(
        project(columns, w_query1), project(columns, w_key1), project(columns, w_value1), marks
    )


def spread_rows(
    fields, ocean, w_query1, w_key1, w_value1, w_out1, w_query2, w_key2, w_value2, w_out2
):
    rows, cols, width = fields.shape
    normed = norm_rows(fields)
    marks = ocean.astype(jnp.bfloat16)
    edge_feats, edge_marks = passed_along((normed[:, cols - 4 :], marks[:, cols - 4 :]), "lon", 1)
    columns = jnp.concatenate([edge_feats, normed[:, : cols - 4]], 1)
    column_marks = jnp.concatenate([edge_marks, marks[:, : cols - 4]], 1)
    extended = attend_columns(columns, column_marks, w_query1, w_key1, w_value1)
    returned = passed_along(extended[:, :4], "lon", -1)
    o1 = jnp.concatenate([extended[:, 4:], returned], 1)
    y1 = (
        fields.astype(jnp.float32) + jnp.dot(o1, w_out1, preferred_element_type=jnp.float32)
    ).astype(jnp.bfloat16)
    h2 = norm_rows(y1)
    q2 = project(h2, w_query2)
    k2 = project(h2, w_key2)
    v2 = project(h2, w_value2)
    row_q, row_k, row_v, row_marks = (
        lax.all_to_all(q2, "lon", split_axis=0, concat_axis=1, tiled=True),
        lax.all_to_all(k2, "lon", split_axis=0, concat_axis=1, tiled=True),
        lax.all_to_all(v2, "lon", split_axis=0, concat_axis=1, tiled=True),
        lax.all_to_all(marks, "lon", split_axis=0, concat_axis=1, tiled=True),
    )
    row_out = row_attend(row_q, row_k, row_v, row_marks)
    o2 = lax.all_to_all(row_out, "lon", split_axis=1, concat_axis=0, tiled=True)
    return (
        y1.astype(jnp.float32) + jnp.dot(o2, w_out2, preferred_element_type=jnp.float32)
    ).astype(jnp.bfloat16)


def normed_f32(a):
    mean = jnp.mean(a, -1, keepdims=True)
    centred = a - mean
    var = jnp.mean(centred * centred, -1, keepdims=True)
    return (centred * lax.rsqrt(var + EPS)).astype(jnp.bfloat16)


def dot_f32(a, b):
    return jnp.dot(a, b, preferred_element_type=jnp.float32)


def low_columns(shape, axis):
    return lax.broadcasted_iota(jnp.int32, shape, axis) % 8 < 4


def attend(queries, keys, values, marks):
    n = marks.shape[0]
    low = lax.broadcasted_iota(jnp.int32, (n, 128), 1) < 64
    land = 1.0 - marks
    bias = jnp.concatenate([land * NEG] * (2 * n // 128), 1)
    scores = []
    for q, k in zip(queries, keys):
        zero = jnp.zeros_like(q)
        both = jnp.concatenate([jnp.where(low, q, zero), jnp.where(low, zero, q)], 0)
        scores.append(lax.dot_general(k, both, (((1,), (1,)), ((), ())), preferred_element_type=jnp.float32) + bias)
    expos = [jnp.exp(s - jnp.max(s, 0, keepdims=True)).astype(jnp.bfloat16) for s in scores]
    outs = []
    for expo, v in zip(expos, values):
        wide = jnp.concatenate([v, jnp.ones_like(v)], 1)
        sums = lax.dot_general(expo, wide, (((0,), (0,)), ((), ())), preferred_element_type=jnp.float32)
        upper = jnp.where(low, sums[:n, :128], sums[n:, :128])
        total = jnp.where(low, sums[:n, 128:], sums[n:, 128:]) + land
        outs.append((upper / total * marks).astype(jnp.bfloat16))
    return outs


ORDER = (4, 5, 6, 7, 1, 2, 3, 0)


def pack_kernel(distances, me_ref, marks_ref, fields_ref, *outs):
    me = me_ref[0]
    tiles = fields_ref.shape[-1] // 128
    marks = marks_ref[...].astype(jnp.float32)
    marks = jnp.concatenate([marks, jnp.zeros((16, 128 - marks.shape[1]), jnp.float32)], 1).astype(jnp.bfloat16)
    for i, d in enumerate(distances):
        there = jnp.bitwise_xor(me, d)
        piece = fields_ref[pl.ds(there * 8, 8)].reshape(128, 128 * tiles)
        for t in range(tiles):
            outs[i][128 * t : 128 * t + 128, :] = piece[:, 128 * t : 128 * t + 128]
        outs[i][128 * tiles :, :] = marks


def pack(distances, me, marks, fields):
    width = fields.shape[-1]
    vmem = pl.BlockSpec(memory_space=pltpu.VMEM)
    piece = jax.ShapeDtypeStruct((width + 16, 128), jnp.bfloat16)
    n = len(distances)
    return pl.pallas_call(
        functools.partial(pack_kernel, distances),
        out_shape=(piece,) * n,
        in_specs=[pl.BlockSpec(memory_space=pltpu.SMEM), vmem, vmem],
        out_specs=(vmem,) * n,
        compiler_params=pltpu.CompilerParams(vmem_limit_bytes=16 * 1024 * 1024),
        cost_estimate=pl.CostEstimate(flops=n * 200000, bytes_accessed=n * 400000, transcendentals=0),
        name="pack",
    )(me, marks, fields)


def hold_kernel(*refs):
    *weights, out_ref, sems = refs
    copies = [pltpu.make_async_copy(w, out_ref.at[i], sems.at[i]) for i, w in enumerate(weights)]
    for copy in copies:
        copy.start()
    for copy in copies:
        copy.wait()


def hold(weights):
    width = weights[0].shape[0]
    return pl.pallas_call(
        hold_kernel,
        out_shape=jax.ShapeDtypeStruct((len(weights), width, width), jnp.bfloat16),
        in_specs=[pl.BlockSpec(memory_space=pl.ANY)] * len(weights),
        out_specs=pl.BlockSpec(memory_space=pltpu.VMEM),
        scratch_shapes=[pltpu.SemaphoreType.DMA((len(weights),))],
        compiler_params=pltpu.CompilerParams(vmem_limit_bytes=16 * 1024 * 1024),
        cost_estimate=pl.CostEstimate(flops=0, bytes_accessed=32 << 20, transcendentals=0),
        name="hold",
    )(*weights)


def unpacked(me, piece):
    tiles = (piece.shape[0] - 16) // 128
    lanes = [piece[128 * t : 128 * t + 128] for t in range(tiles)]
    marks = pltpu.roll(piece[128 * tiles :].astype(jnp.float32), jnp.bitwise_and(128 - 8 * me, 127), 1)
    marks = jnp.concatenate([jnp.broadcast_to(marks[:, r : r + 1], (16, 128)) for r in range(8)], 0)
    whole = jnp.concatenate(lanes + [marks.astype(jnp.bfloat16)], 1).astype(jnp.float32)
    whole = whole.reshape(8, 2, 8, 128 * tiles + 128)
    return whole[:, 0], whole[:, 1]


STAGES = ((3, 2), (8, 8), (5, 6))


def window_kernel(stage, me_ref, *refs):
    pieces = refs[: (2, 4, 2)[stage]]
    refs = refs[len(pieces) :]
    carried = refs[: (0, 2, 5)[stage]]
    refs = refs[len(carried) :]
    weights, y_ref, q2_ref, k2_ref, v2_ref, m_ref = refs[:6]
    wq, wk, wv, wo, wq2, wk2, wv2 = (weights.at[i] for i in range(7))
    refs = refs[6:]
    passed = refs[: (3, 2, 0)[stage]]
    placed, q_s, k_s, v_s, o_s, rows_s = refs[len(passed) :]
    width = wq.shape[0]
    scale = (width // HEADS) ** (-0.5)
    me = me_ref[0]
    upper = jnp.bitwise_and(me, 2) > 0
    low = jnp.bitwise_and(me, len(pieces) - 1)
    for d, piece in enumerate(pieces):
        placed[jnp.bitwise_xor(low, d)] = piece[...]
    columns = [unpacked(me, placed[l]) for l in range(len(pieces))]
    mask = low_columns((8, 8, width + 128), 1)
    full = (64, width + 128)

    def whole_window(l):
        return jnp.where(mask, columns[l][1], columns[l][0]).reshape(full)

    def straddling_window(left, right):
        return jnp.where(mask, right, left).reshape(full)

    def either(if_upper, if_lower):
        return jnp.where(upper, if_upper, if_lower)

    windows = [whole_window(0)]
    for l in range(1, len(pieces)):
        windows += [straddling_window(columns[l - 1][1], columns[l][0]), whole_window(l)]
    first, last = columns[0][0], columns[-1][1]
    edges = [a[...].reshape(8, 8, width + 128) for a in carried[:4]]
    if stage < 2:
        passed[0][...] = first.reshape(full)
        passed[1][...] = last.reshape(full)
    if stage == 1:
        second_first, second_last = edges
        windows.append(straddling_window(either(second_last, last), either(first, second_first)))
    if stage == 2:
        second_first, second_last, own_first, own_last = edges
        windows = (
            [straddling_window(either(last, second_last), either(second_first, first))]
            + windows
            + [straddling_window(either(own_last, last), either(first, own_first))]
        )
    count = len(windows)
    x = jnp.concatenate([w[:, :width] for w in windows], 0)
    marks = [w[:, width:] for w in windows]
    h = normed_f32(x)
    q_s[...] = (dot_f32(h, wq[...]) * scale).astype(jnp.bfloat16)
    k_s[...] = dot_f32(h, wk[...]).astype(jnp.bfloat16)
    v_s[...] = dot_f32(h, wv[...]).astype(jnp.bfloat16)
    for w in range(count):
        here = slice(64 * w, 64 * w + 64)
        outs = attend(*([a[here, lanes] for lanes in PAIRS] for a in (q_s, k_s, v_s)), marks[w])
        for lanes, out in zip(PAIRS, outs):
            o_s[here, lanes] = out
    y = (x + dot_f32(o_s[...], wo[...])).astype(jnp.bfloat16).astype(jnp.float32)
    skip = 0
    if stage == 2:
        skip = 1
        rows_s[:, :8, :] = carried[4][...]
    for w in range(count):
        for r in range(8):
            at = 64 * w + 8 * r
            to = 8 * (w + skip)
            if stage == 0 and w == count - 1:
                passed[2][r, :, :width] = y[at : at + 8]
                passed[2][r, :, width:] = marks[w][8 * r : 8 * r + 8]
            else:
                rows_s[r, to : to + 8, :width] = y[at : at + 8]
                rows_s[r, to : to + 8, width:] = marks[w][8 * r : 8 * r + 8]
    tokens = rows_s.shape[0] * rows_s.shape[1]
    y = rows_s[:, :, :width].reshape(tokens, width)
    m_ref[...] = rows_s[:, :, width:].astype(jnp.bfloat16)
    y_ref[...] = y.astype(jnp.bfloat16).reshape(y_ref.shape)
    h = normed_f32(y)
    q2_ref[...] = (dot_f32(h, wq2[...]) * scale).astype(jnp.bfloat16).reshape(q2_ref.shape)
    k2_ref[...] = dot_f32(h, wk2[...]).astype(jnp.bfloat16).reshape(k2_ref.shape)
    v2_ref[...] = dot_f32(h, wv2[...]).astype(jnp.bfloat16).reshape(v2_ref.shape)


def window_layer(stage, me, pieces, carried, weights):
    width = weights.shape[1]
    tokens = 64 * STAGES[stage][0]
    columns = 8 * STAGES[stage][1]
    part = jax.ShapeDtypeStruct((8, columns, width), jnp.bfloat16)
    marks = jax.ShapeDtypeStruct((8, columns, 128), jnp.bfloat16)
    edge = jax.ShapeDtypeStruct((64, width + 128), jnp.float32)
    tail = jax.ShapeDtypeStruct((8, 8, width + 128), jnp.float32)
    outs = (part,) * 4 + (marks,) + ((edge, edge, tail), (edge, edge), ())[stage]
    vmem = pl.BlockSpec(memory_space=pltpu.VMEM)
    work = pltpu.VMEM((tokens, width), jnp.bfloat16)
    inputs = [*pieces, *carried, weights]
    return pl.pallas_call(
        functools.partial(window_kernel, stage),
        out_shape=outs,
        in_specs=[pl.BlockSpec(memory_space=pltpu.SMEM)] + [vmem] * len(inputs),
        out_specs=(vmem,) * len(outs),
        scratch_shapes=[
            pltpu.VMEM((len(pieces), width + 16, 128), jnp.bfloat16),
            work, work, work, work,
            pltpu.VMEM((8, columns, width + 128), jnp.float32),
        ],
        compiler_params=pltpu.CompilerParams(vmem_limit_bytes=36 * 1024 * 1024),
        cost_estimate=pl.CostEstimate(
            flops=2 * tokens * width * (7 * width + 512), bytes_accessed=16 << 20, transcendentals=tokens * 64 * HEADS
        ),
        name="window_layer",
    )(me, *inputs)


def row_kernel(start, rows, me_ref, *refs):
    parts, wo, refs = (refs[:5], refs[5:10], refs[10:15]), refs[15].at[7], refs[16:]
    outs, (o_s, placed) = refs[:8], refs[8:]
    width = wo.shape[0]
    length = 128

    def row(i, r, lanes=slice(None)):
        return jnp.concatenate([part[i][start + r, :, lanes] for part in parts], 0)

    for r in range(rows):
        here = slice(length * r, length * r + length)
        heads = attend(*([row(i, r, lanes) for lanes in PAIRS] for i in (1, 2, 3)), row(4, r).astype(jnp.float32))
        for lanes, out in zip(PAIRS, heads):
            o_s[here, lanes] = out
    added = dot_f32(o_s[...], wo[...])
    mask = low_columns((8, width), 0)
    me = me_ref[0]
    upper = jnp.bitwise_and(me, 2) > 0
    for r in range(rows):
        f = row(0, r).astype(jnp.float32) + added[length * r : length * r + length]
        tiles = [f[8 * w : 8 * w + 8] for w in range(16)]
        own = tiles[2:9]
        second, third = (tiles[0], tiles[1], tiles[10]), tiles[12:15]
        at_second, middle, at_third = tiles[9], tiles[11], tiles[15]
        after_own = jnp.where(upper, at_third, at_second)
        before_own = jnp.where(upper, at_second, at_third)
        whole = [before_own, *own, after_own]
        whole += [jnp.where(upper, middle, after_own), *second, jnp.where(upper, before_own, middle)]
        whole += [jnp.where(upper, after_own, middle), *third, jnp.where(upper, middle, before_own)]
        for l in range(8):
            at = 2 * l if l < 4 else (9, 11, 14, 16)[l - 4]
            before, a, after = whole[at : at + 3]
            piece = jnp.concatenate([jnp.where(mask, before, a), jnp.where(mask, a, after)], 0)
            placed[l, r] = piece.astype(jnp.bfloat16)
    for i, d in enumerate(ORDER):
        if d < 4:
            outs[i][...] = placed[jnp.bitwise_xor(jnp.bitwise_and(me, 3), d)]
        else:
            outs[i][...] = placed[jnp.bitwise_xor(jnp.bitwise_and(me, 1), d)]


def row_layer(start, rows, me, parts, weights):
    width = weights.shape[1]
    length = 128
    piece = jax.ShapeDtypeStruct((rows, 16, width), jnp.bfloat16)
    vmem = pl.BlockSpec(memory_space=pltpu.VMEM)
    return pl.pallas_call(
        functools.partial(row_kernel, start, rows),
        out_shape=(piece,) * 8,
        in_specs=[pl.BlockSpec(memory_space=pltpu.SMEM)] + [vmem] * (len(parts) + 1),
        out_specs=(vmem,) * 8,
        scratch_shapes=[
            pltpu.VMEM((rows * length, width), jnp.bfloat16),
            pltpu.VMEM((8, rows, 16, width), jnp.bfloat16),
        ],
        compiler_params=pltpu.CompilerParams(vmem_limit_bytes=36 * 1024 * 1024),
        cost_estimate=pl.CostEstimate(
            flops=2 * rows * length * width * (width + 1024), bytes_accessed=8 << 20,
            transcendentals=rows * length * length * HEADS,
        ),
        name="row_layer",
    )(me, *parts, weights)


def place_kernel(start, rows, me_ref, *refs):
    pieces, out_ref, sems = refs[:8], refs[-2], refs[-1]
    copies = []
    for i, d in enumerate(ORDER):
        there = jnp.bitwise_xor(me_ref[0], d)
        copies.append(
            pltpu.make_async_copy(pieces[i], out_ref.at[pl.ds(there * 8 + start, rows)], sems.at[i])
        )
        copies[-1].start()
    for copy in copies:
        copy.wait()


def place(start, rows, me, pieces, so_far, shape):
    vmem = pl.BlockSpec(memory_space=pltpu.VMEM)
    hbm = pl.BlockSpec(memory_space=pltpu.HBM)
    more = () if so_far is None else (so_far,)
    return pl.pallas_call(
        functools.partial(place_kernel, start, rows),
        out_shape=jax.ShapeDtypeStruct(shape, jnp.bfloat16),
        in_specs=[pl.BlockSpec(memory_space=pltpu.SMEM)] + [vmem] * 8 + [hbm] * len(more),
        out_specs=hbm,
        scratch_shapes=[pltpu.SemaphoreType.DMA((8,))],
        input_output_aliases={9: 0} if more else {},
        cost_estimate=pl.CostEstimate(flops=0, bytes_accessed=16 * rows * shape[1] * shape[2] * 2, transcendentals=0),
        name="place",
    )(me, *pieces, *more)


def exchanged(piece, distance):
    count = lax.axis_size("lon")
    return lax.ppermute(piece, "lon", [(s, s ^ distance) for s in range(count)])


def gathered_bands(
    fields, ocean, w_query1, w_key1, w_value1, w_out1, w_query2, w_key2, w_value2, w_out2
):
    me = lax.axis_index("lon").astype(jnp.int32).reshape(1)
    weights = hold((w_query1, w_key1, w_value1, w_out1, w_query2, w_key2, w_value2, w_out2))

    packed = dict(zip(ORDER, pack(ORDER, me, ocean.T, fields)))
    got = {d: exchanged(packed[d], d) if d else packed[d] for d in ORDER}
    second = window_layer(0, me, [got[4], got[5]], (), weights)
    own = window_layer(1, me, [got[d] for d in range(4)], second[5:7], weights)
    third = window_layer(2, me, [got[6], got[7]], (*second[5:7], *own[5:], second[7]), weights)
    parts = (*second[:5], *own[:5], *third)
    start, out, back = 0, None, None
    for size in GROUPS:
        sent = list(row_layer(start, size, me, parts, weights))
        if back is not None:
            for i in range(7):
                sent[i], back[i] = lax.optimization_barrier((sent[i], back[i]))
            out = place(start - before, before, me, back, out, fields.shape)
        back = [exchanged(piece, d) if d else piece for d, piece in zip(ORDER, sent)]
        start, before = start + size, size
    return place(start - before, before, me, back, out, fields.shape)


def on_device(fields, *rest):
    rows, cols, width = fields.shape
    if lax.axis_size("lon") == 8 and rows == 64 and cols == 16 and width == 64 * HEADS:
        return gathered_bands(fields, *rest)
    return spread_rows(fields, *rest)


def solution(mesh):
    in_specs = (
        P(("grp", "lat"), "lon", None),
        P(("grp", "lat"), "lon"),
        P(),
        P(),
        P(),
        P(),
        P(),
        P(),
        P(),
        P(),
    )
    out_specs = P(("grp", "lat"), "lon", None)
    return jax.shard_map(
        on_device, mesh=mesh, in_specs=in_specs, out_specs=out_specs, check_vma=False
    )
```

```python
import functools

import jax
import jax.numpy as jnp
from jax import lax
from jax.experimental import pallas as pl
from jax.experimental.pallas import tpu as pltpu
from jax.sharding import PartitionSpec as P

HEADS = 12


EPS = 1e-05
NEG = -1e30

ROWS_FIRST = 4

PACK_VMEM = 52 * 1024 * 1024

PAIRS = [slice(128 * p, 128 * p + 128) for p in range(HEADS // 2)]


def passed_along(value, axis, steps):
    count = lax.axis_size(axis)
    pairs = [(source, (source + steps) % count) for source in range(count)]
    return lax.ppermute(value, axis, pairs)


def norm_rows(a):
    af = a.astype(jnp.float32)
    mean = jnp.mean(af, -1, keepdims=True)
    var = jnp.mean((af - mean) * (af - mean), -1, keepdims=True)
    return ((af - mean) * lax.rsqrt(var + EPS)).astype(jnp.bfloat16)


def project(h, weight):
    return jnp.dot(h, weight, preferred_element_type=jnp.float32).astype(jnp.bfloat16)


def masked_softmax(scores, key_ok, land_query):
    top = jnp.max(jnp.where(key_ok, scores, NEG), -1, keepdims=True)
    expo = jnp.where(key_ok, jnp.exp(scores - top), 0.0)
    total = jnp.sum(expo, -1, keepdims=True) + land_query[..., None]
    return (expo / total).astype(jnp.bfloat16)


def window_attend(query, keys, values, flags):
    rows, cols, width = query.shape
    nh = HEADS
    hd = width // nh
    scale = hd ** (-0.5)

    def tiles(a):
        a = a.reshape(rows // 8, 8, cols // 8, 8, nh, hd).transpose(0, 2, 4, 1, 3, 5)
        return a.reshape(rows // 8, cols // 8, nh, 64, hd)

    marks = (
        flags.reshape(rows // 8, 8, cols // 8, 8)
        .transpose(0, 2, 1, 3)
        .reshape(rows // 8, cols // 8, 64)
    )
    key_ok = (marks > 0)[:, :, None, None, :]
    land_query = (marks <= 0).astype(jnp.float32)[:, :, None, :]
    scores = (
        jnp.einsum(
            "abhqd,abhkd->abhqk", tiles(query), tiles(keys), preferred_element_type=jnp.float32
        )
        * scale
    )
    probs = masked_softmax(scores, key_ok, land_query)
    outs = jnp.einsum(
        "abhqk,abhkd->abhqd", probs, tiles(values), preferred_element_type=jnp.float32
    )
    outs = outs * (1.0 - land_query)[..., None]
    outs = outs.astype(jnp.bfloat16).reshape(rows // 8, cols // 8, nh, 8, 8, hd)
    return outs.transpose(0, 3, 1, 4, 2, 5).reshape(rows, cols, width)


def row_attend(query, keys, values, flags):
    rows, length, width = query.shape
    nh = HEADS
    hd = width // nh
    scale = hd ** (-0.5)
    key_ok = (flags > 0)[:, None, :]
    land_query = (flags <= 0).astype(jnp.float32)

    def head(index):
        qh = lax.dynamic_slice_in_dim(query, index * hd, hd, 2)
        kh = lax.dynamic_slice_in_dim(keys, index * hd, hd, 2)
        vh = lax.dynamic_slice_in_dim(values, index * hd, hd, 2)
        scores = jnp.einsum("rqd,rkd->rqk", qh, kh, preferred_element_type=jnp.float32) * scale
        probs = masked_softmax(scores, key_ok, land_query)
        return jnp.einsum("rqk,rkd->rqd", probs, vh, preferred_element_type=jnp.float32)

    outs = lax.map(head, jnp.arange(nh, dtype=jnp.int32))
    outs = outs.transpose(1, 2, 0, 3).reshape(rows, length, width)
    return (outs * (1.0 - land_query)[..., None]).astype(jnp.bfloat16)


def attend_columns(columns, marks, w_query1, w_key1, w_value1):
    return window_attend(
        project(columns, w_query1), project(columns, w_key1), project(columns, w_value1), marks
    )


def spread_rows(
    fields, ocean, w_query1, w_key1, w_value1, w_out1, w_query2, w_key2, w_value2, w_out2
):
    rows, cols, width = fields.shape
    normed = norm_rows(fields)
    marks = ocean.astype(jnp.bfloat16)
    edge_feats, edge_marks = passed_along((normed[:, cols - 4 :], marks[:, cols - 4 :]), "lon", 1)
    columns = jnp.concatenate([edge_feats, normed[:, : cols - 4]], 1)
    column_marks = jnp.concatenate([edge_marks, marks[:, : cols - 4]], 1)
    extended = attend_columns(columns, column_marks, w_query1, w_key1, w_value1)
    returned = passed_along(extended[:, :4], "lon", -1)
    o1 = jnp.concatenate([extended[:, 4:], returned], 1)
    y1 = (
        fields.astype(jnp.float32) + jnp.dot(o1, w_out1, preferred_element_type=jnp.float32)
    ).astype(jnp.bfloat16)
    h2 = norm_rows(y1)
    q2 = project(h2, w_query2)
    k2 = project(h2, w_key2)
    v2 = project(h2, w_value2)
    row_q, row_k, row_v, row_marks = (
        lax.all_to_all(q2, "lon", split_axis=0, concat_axis=1, tiled=True),
        lax.all_to_all(k2, "lon", split_axis=0, concat_axis=1, tiled=True),
        lax.all_to_all(v2, "lon", split_axis=0, concat_axis=1, tiled=True),
        lax.all_to_all(marks, "lon", split_axis=0, concat_axis=1, tiled=True),
    )
    row_out = row_attend(row_q, row_k, row_v, row_marks)
    o2 = lax.all_to_all(row_out, "lon", split_axis=1, concat_axis=0, tiled=True)
    return (
        y1.astype(jnp.float32) + jnp.dot(o2, w_out2, preferred_element_type=jnp.float32)
    ).astype(jnp.bfloat16)


def normed_f32(a):
    mean = jnp.mean(a, -1, keepdims=True)
    centred = a - mean
    var = jnp.mean(centred * centred, -1, keepdims=True)
    return (centred * lax.rsqrt(var + EPS)).astype(jnp.bfloat16)


def dot_f32(a, b):
    return jnp.dot(a, b, preferred_element_type=jnp.float32)


def low_columns(shape, axis):
    return lax.broadcasted_iota(jnp.int32, shape, axis) % 8 < 4


def attend(queries, keys, values, marks):
    n = marks.shape[0]
    low = lax.broadcasted_iota(jnp.int32, (n, 128), 1) < 64
    land = 1.0 - marks
    bias = jnp.concatenate([land * NEG] * (2 * n // 128), 1)
    scores = []
    for q, k in zip(queries, keys):
        zero = jnp.zeros_like(q)
        both = jnp.concatenate([jnp.where(low, q, zero), jnp.where(low, zero, q)], 0)
        scores.append(lax.dot_general(k, both, (((1,), (1,)), ((), ())), preferred_element_type=jnp.float32) + bias)
    expos = [jnp.exp(s - jnp.max(s, 0, keepdims=True)).astype(jnp.bfloat16) for s in scores]
    outs = []
    for expo, v in zip(expos, values):
        wide = jnp.concatenate([v, jnp.ones_like(v)], 1)
        sums = lax.dot_general(expo, wide, (((0,), (0,)), ((), ())), preferred_element_type=jnp.float32)
        upper = jnp.where(low, sums[:n, :128], sums[n:, :128])
        total = jnp.where(low, sums[:n, 128:], sums[n:, 128:]) + land
        outs.append((upper / total * marks).astype(jnp.bfloat16))
    return outs


ORDER = (4, 5, 6, 7, 1, 2, 3, 0)


def pack_kernel(distances, me_ref, marks_ref, fields_ref, *refs):
    outs, (held, held_marks, sems) = refs[: len(distances)], refs[len(distances) :]
    me = me_ref[0]
    tiles = fields_ref.shape[-1] // 128
    copies = [pltpu.make_async_copy(marks_ref, held_marks, sems.at[len(distances)])]
    for i, d in enumerate(distances):
        there = jnp.bitwise_xor(me, d)
        copies.append(pltpu.make_async_copy(fields_ref.at[pl.ds(there * 8, 8)], held.at[i], sems.at[i]))
    for copy in copies:
        copy.start()
    copies[0].wait()
    marks = held_marks[...].astype(jnp.float32)
    marks = jnp.concatenate([marks, jnp.zeros((16, 128 - marks.shape[1]), jnp.float32)], 1).astype(jnp.bfloat16)
    for i in range(len(distances)):
        copies[i + 1].wait()
        piece = held[i].reshape(128, 128 * tiles)
        for t in range(tiles):
            outs[i][128 * t : 128 * t + 128, :] = piece[:, 128 * t : 128 * t + 128]
        outs[i][128 * tiles :, :] = marks


def pack(distances, me, marks, fields):
    cols, width = fields.shape[1:]
    vmem = pl.BlockSpec(memory_space=pltpu.VMEM)
    anywhere = pl.BlockSpec(memory_space=pl.ANY)
    piece = jax.ShapeDtypeStruct((width + 16, 128), jnp.bfloat16)
    n = len(distances)
    return pl.pallas_call(
        functools.partial(pack_kernel, distances),
        out_shape=(piece,) * n,
        in_specs=[pl.BlockSpec(memory_space=pltpu.SMEM), anywhere, anywhere],
        out_specs=(vmem,) * n,
        scratch_shapes=[
            pltpu.VMEM((n, 8, cols, width), jnp.bfloat16),
            pltpu.VMEM(marks.shape, marks.dtype),
            pltpu.SemaphoreType.DMA((n + 1,)),
        ],
        compiler_params=pltpu.CompilerParams(vmem_limit_bytes=PACK_VMEM),
        cost_estimate=pl.CostEstimate(flops=n * 200000, bytes_accessed=n * 400000, transcendentals=0),
        name="pack",
    )(me, marks, fields)


def ready_kernel(*refs):
    refs[-1][...] = jnp.zeros_like(refs[-1])


def ready(weights):
    vmem = pl.BlockSpec(memory_space=pltpu.VMEM)
    return pl.pallas_call(
        ready_kernel,
        out_shape=jax.ShapeDtypeStruct((8, 128), jnp.float32),
        in_specs=[vmem] * len(weights),
        out_specs=vmem,
        compiler_params=pltpu.CompilerParams(vmem_limit_bytes=16 * 1024 * 1024),
        cost_estimate=pl.CostEstimate(flops=0, bytes_accessed=32 << 20, transcendentals=0),
        name="ready",
    )(*weights)


def unpacked(me, piece):
    tiles = (piece.shape[0] - 16) // 128
    lanes = [piece[128 * t : 128 * t + 128] for t in range(tiles)]
    marks = pltpu.roll(piece[128 * tiles :].astype(jnp.float32), jnp.bitwise_and(128 - 8 * me, 127), 1)
    marks = jnp.concatenate([jnp.broadcast_to(marks[:, r : r + 1], (16, 128)) for r in range(8)], 0)
    whole = jnp.concatenate(lanes + [marks.astype(jnp.bfloat16)], 1).astype(jnp.float32)
    whole = whole.reshape(8, 2, 8, 128 * tiles + 128)
    return whole[:, 0], whole[:, 1]


STAGES = ((7, 6), (4, 4), (5, 6))


def window_kernel(stage, me_ref, *refs):
    pieces = refs[: (4, 2, 2)[stage]]
    refs = refs[len(pieces) :]
    carried = refs[: (0, 3, 5)[stage]]
    refs = refs[len(carried) :]
    _, wq, wk, wv, wo, wq2, wk2, wv2, y_ref, q2_ref, k2_ref, v2_ref, m_ref = refs[:13]
    refs = refs[13:]
    passed = refs[: (3, 3, 0)[stage]]
    placed, q_s, k_s, v_s, o_s, rows_s = refs[len(passed) :]
    width = wq.shape[0]
    scale = (width // HEADS) ** (-0.5)
    me = me_ref[0]
    upper = jnp.bitwise_and(me, 2) > 0
    low = jnp.bitwise_and(me, len(pieces) - 1)
    for d, piece in enumerate(pieces):
        placed[jnp.bitwise_xor(low, d)] = piece[...]
    columns = [unpacked(me, placed[l]) for l in range(len(pieces))]
    mask = low_columns((8, 8, width + 128), 1)
    full = (64, width + 128)

    def whole_window(l):
        return jnp.where(mask, columns[l][1], columns[l][0]).reshape(full)

    def straddling_window(left, right):
        return jnp.where(mask, right, left).reshape(full)

    def either(if_upper, if_lower):
        return jnp.where(upper, if_upper, if_lower)

    windows = [whole_window(0)]
    for l in range(1, len(pieces)):
        windows += [straddling_window(columns[l - 1][1], columns[l][0]), whole_window(l)]
    first, last = columns[0][0], columns[-1][1]
    if stage < 2:
        passed[0][...] = first.reshape(full)
        passed[1][...] = last.reshape(full)
    edges = [a[...].reshape(8, 8, width + 128) for a in carried[:-1]]
    if stage == 1:
        own_first, own_last = edges
        windows = [straddling_window(either(last, own_last), either(own_first, first))] + windows
    if stage == 2:
        own_first, own_last, second_first, second_last = edges
        windows = (
            [straddling_window(either(last, second_last), either(second_first, first))]
            + windows
            + [straddling_window(either(own_last, last), either(first, own_first))]
        )
    count = len(windows)
    x = jnp.concatenate([w[:, :width] for w in windows], 0)
    marks = [w[:, width:] for w in windows]
    h = normed_f32(x)
    q_s[...] = (dot_f32(h, wq[...]) * scale).astype(jnp.bfloat16)
    k_s[...] = dot_f32(h, wk[...]).astype(jnp.bfloat16)
    v_s[...] = dot_f32(h, wv[...]).astype(jnp.bfloat16)
    for w in range(count):
        here = slice(64 * w, 64 * w + 64)
        outs = attend(*([a[here, lanes] for lanes in PAIRS] for a in (q_s, k_s, v_s)), marks[w])
        for lanes, out in zip(PAIRS, outs):
            o_s[here, lanes] = out
    y = (x + dot_f32(o_s[...], wo[...])).astype(jnp.bfloat16).astype(jnp.float32)
    skip = 0
    if stage > 0:
        skip = 1
        rows_s[:, :8, :] = carried[-1][...]
    for w in range(count):
        for r in range(8):
            at = 64 * w + 8 * r
            to = 8 * (w + skip)
            if stage < 2 and w == count - 1:
                passed[2][r, :, :width] = y[at : at + 8]
                passed[2][r, :, width:] = marks[w][8 * r : 8 * r + 8]
            else:
                rows_s[r, to : to + 8, :width] = y[at : at + 8]
                rows_s[r, to : to + 8, width:] = marks[w][8 * r : 8 * r + 8]
    tokens = rows_s.shape[0] * rows_s.shape[1]
    y = rows_s[:, :, :width].reshape(tokens, width)
    m_ref[...] = rows_s[:, :, width:].astype(jnp.bfloat16)
    y_ref[...] = y.astype(jnp.bfloat16).reshape(y_ref.shape)
    h = normed_f32(y)
    q2_ref[...] = (dot_f32(h, wq2[...]) * scale).astype(jnp.bfloat16).reshape(q2_ref.shape)
    k2_ref[...] = dot_f32(h, wk2[...]).astype(jnp.bfloat16).reshape(k2_ref.shape)
    v2_ref[...] = dot_f32(h, wv2[...]).astype(jnp.bfloat16).reshape(v2_ref.shape)


def window_layer(stage, me, pieces, carried, weights):
    width = weights[1].shape[0]
    tokens = 64 * STAGES[stage][0]
    columns = 8 * STAGES[stage][1]
    part = jax.ShapeDtypeStruct((8, columns, width), jnp.bfloat16)
    marks = jax.ShapeDtypeStruct((8, columns, 128), jnp.bfloat16)
    edge = jax.ShapeDtypeStruct((64, width + 128), jnp.float32)
    tail = jax.ShapeDtypeStruct((8, 8, width + 128), jnp.float32)
    outs = (part,) * 4 + (marks,) + ((edge, edge, tail), (edge, edge, tail), ())[stage]
    vmem = pl.BlockSpec(memory_space=pltpu.VMEM)
    work = pltpu.VMEM((tokens, width), jnp.bfloat16)
    inputs = [*pieces, *carried, *weights]
    return pl.pallas_call(
        functools.partial(window_kernel, stage),
        out_shape=outs,
        in_specs=[pl.BlockSpec(memory_space=pltpu.SMEM)] + [vmem] * len(inputs),
        out_specs=(vmem,) * len(outs),
        scratch_shapes=[
            pltpu.VMEM((len(pieces), width + 16, 128), jnp.bfloat16),
            work, work, work, work,
            pltpu.VMEM((8, columns, width + 128), jnp.float32),
        ],
        compiler_params=pltpu.CompilerParams(vmem_limit_bytes=36 * 1024 * 1024),
        cost_estimate=pl.CostEstimate(
            flops=2 * tokens * width * (7 * width + 512), bytes_accessed=16 << 20, transcendentals=tokens * 64 * HEADS
        ),
        name="window_layer",
    )(me, *inputs)


def row_kernel(start, rows, me_ref, *refs):
    parts, wo, refs = (refs[:5], refs[5:10], refs[10:15]), refs[15], refs[16:]
    earlier, refs = (refs[:4], refs[4:]) if start else ((), refs)
    outs, (o_s, placed) = refs[:8], refs[8:]
    width = wo.shape[0]
    length = 128

    def row(i, r, lanes=slice(None)):
        return jnp.concatenate([part[i][start + r, :, lanes] for part in parts], 0)

    for r in range(rows):
        here = slice(length * r, length * r + length)
        heads = attend(*([row(i, r, lanes) for lanes in PAIRS] for i in (1, 2, 3)), row(4, r).astype(jnp.float32))
        for lanes, out in zip(PAIRS, heads):
            o_s[here, lanes] = out
    added = dot_f32(o_s[...], wo[...])
    mask = low_columns((8, width), 0)
    me = me_ref[0]
    upper = jnp.bitwise_and(me, 2) > 0
    for r in range(rows):
        f = row(0, r).astype(jnp.float32) + added[length * r : length * r + length]
        tiles = [f[8 * w : 8 * w + 8] for w in range(16)]
        own, second, third = tiles[:7], tiles[8:11], tiles[12:15]
        own_second, middle, third_own = tiles[7], tiles[11], tiles[15]
        after_own = jnp.where(upper, third_own, own_second)
        before_own = jnp.where(upper, own_second, third_own)
        whole = [before_own, *own, after_own]
        whole += [jnp.where(upper, middle, after_own), *second, jnp.where(upper, before_own, middle)]
        whole += [jnp.where(upper, after_own, middle), *third, jnp.where(upper, middle, before_own)]
        for l in range(8):
            at = 2 * l if l < 4 else (9, 11, 14, 16)[l - 4]
            before, a, after = whole[at : at + 3]
            piece = jnp.concatenate([jnp.where(mask, before, a), jnp.where(mask, a, after)], 0)
            placed[l, r] = piece.astype(jnp.bfloat16)
    for i, d in enumerate(ORDER):
        if d < 4:
            if start:
                outs[i][:start] = earlier[i - 4][...]
            outs[i][start:] = placed[jnp.bitwise_xor(jnp.bitwise_and(me, 3), d)]
        else:
            outs[i][...] = placed[d // 2 * 2 + jnp.bitwise_xor(jnp.bitwise_and(me, 1), d % 2)]


def row_layer(start, rows, me, parts, w_out, earlier):
    width = w_out.shape[0]
    length = 128
    far = jax.ShapeDtypeStruct((rows, 16, width), jnp.bfloat16)
    near = jax.ShapeDtypeStruct((start + rows, 16, width), jnp.bfloat16)
    vmem = pl.BlockSpec(memory_space=pltpu.VMEM)
    inputs = [*parts, w_out, *earlier]
    return pl.pallas_call(
        functools.partial(row_kernel, start, rows),
        out_shape=(far,) * 4 + (near,) * 4,
        in_specs=[pl.BlockSpec(memory_space=pltpu.SMEM)] + [vmem] * len(inputs),
        out_specs=(vmem,) * 8,
        scratch_shapes=[
            pltpu.VMEM((rows * length, width), jnp.bfloat16),
            pltpu.VMEM((8, rows, 16, width), jnp.bfloat16),
        ],
        compiler_params=pltpu.CompilerParams(vmem_limit_bytes=36 * 1024 * 1024),
        cost_estimate=pl.CostEstimate(
            flops=0, bytes_accessed=1 << 16, transcendentals=0
        ),
        name="row_layer",
    )(me, *inputs)


def place_kernel(spots, me_ref, *refs):
    pieces, out_ref, sems = refs[: len(spots)], refs[-2], refs[-1]
    copies = []
    for i, (d, start) in enumerate(spots):
        at = jnp.bitwise_xor(me_ref[0], d) * 8 + start
        copies.append(pltpu.make_async_copy(pieces[i], out_ref.at[pl.ds(at, pieces[i].shape[0])], sems.at[i]))
        copies[-1].start()
    for copy in copies:
        copy.wait()


def place(spots, me, pieces, so_far, shape):
    vmem = pl.BlockSpec(memory_space=pltpu.VMEM)
    hbm = pl.BlockSpec(memory_space=pltpu.HBM)
    n = len(pieces)
    more = () if so_far is None else (so_far,)
    return pl.pallas_call(
        functools.partial(place_kernel, spots),
        out_shape=jax.ShapeDtypeStruct(shape, jnp.bfloat16),
        in_specs=[pl.BlockSpec(memory_space=pltpu.SMEM)] + [vmem] * n + [hbm] * len(more),
        out_specs=hbm,
        scratch_shapes=[pltpu.SemaphoreType.DMA((n,))],
        input_output_aliases={n + 1: 0} if more else {},
        compiler_params=pltpu.CompilerParams(vmem_limit_bytes=8 * 1024 * 1024),
        cost_estimate=pl.CostEstimate(flops=0, bytes_accessed=4 << 20, transcendentals=0),
        name="place",
    )(me, *pieces, *more)


def exchanged(piece, distance):
    count = lax.axis_size("lon")
    return lax.ppermute(piece, "lon", [(s, s ^ distance) for s in range(count)])


def gathered_bands(
    fields, ocean, w_query1, w_key1, w_value1, w_out1, w_query2, w_key2, w_value2, w_out2
):
    me = lax.axis_index("lon").astype(jnp.int32).reshape(1)
    weights = (w_query1, w_key1, w_value1, w_out1, w_query2, w_key2, w_value2)
    weights = (ready(weights), *weights)

    packed = dict(zip(ORDER, pack(ORDER, me, ocean.T, fields)))
    got = {d: exchanged(packed[d], d) if d else packed[d] for d in ORDER}
    got[4], *near = lax.optimization_barrier((got[4], got[2], got[3], got[1]))
    got[2], got[3], got[1] = near
    own = window_layer(0, me, [got[d] for d in range(4)], (), weights)
    second = window_layer(1, me, [got[4], got[5]], own[5:], weights)
    third = window_layer(2, me, [got[6], got[7]], (*own[5:7], *second[5:]), weights)
    parts = (*own[:5], *second[:5], *third)
    first = row_layer(0, ROWS_FIRST, me, parts, w_out2, ())
    last = row_layer(ROWS_FIRST, 8 - ROWS_FIRST, me, parts, w_out2, first[4:])
    far = [exchanged(piece, d) for d, piece in zip(ORDER[:4], first)]
    last = list(last)
    for i in range(4):
        last[i], last[4 + i], far[i] = lax.optimization_barrier((last[i], last[4 + i], far[i]))
    far_last = [exchanged(piece, d) for d, piece in zip(ORDER[:4], last)]
    near = [exchanged(piece, d) if d else piece for d, piece in zip(ORDER[4:], last[4:])]
    out = place([(d, 0) for d in ORDER], me, far + near, None, fields.shape)
    return place([(d, ROWS_FIRST) for d in ORDER[:4]], me, far_last, out, fields.shape)


def on_device(fields, *rest):
    rows, cols, width = fields.shape
    if lax.axis_size("lon") == 8 and rows == 64 and cols == 16 and width == 64 * HEADS:
        return gathered_bands(fields, *rest)
    return spread_rows(fields, *rest)


def solution(mesh):
    in_specs = (
        P(("grp", "lat"), "lon", None),
        P(("grp", "lat"), "lon"),
        P(),
        P(),
        P(),
        P(),
        P(),
        P(),
        P(),
        P(),
    )
    out_specs = P(("grp", "lat"), "lon", None)
    return jax.shard_map(
        on_device, mesh=mesh, in_specs=in_specs, out_specs=out_specs, check_vma=False
    )
```

```python
import functools

import jax
import jax.numpy as jnp
from jax import lax
from jax.experimental import pallas as pl
from jax.experimental.pallas import tpu as pltpu
from jax.sharding import PartitionSpec as P

HEADS = 12


EPS = 1e-05
NEG = -1e30

PACK_VMEM = 52 * 1024 * 1024

PAIRS = [slice(128 * p, 128 * p + 128) for p in range(HEADS // 2)]


def passed_along(value, axis, steps):
    count = lax.axis_size(axis)
    pairs = [(source, (source + steps) % count) for source in range(count)]
    return lax.ppermute(value, axis, pairs)


def norm_rows(a):
    af = a.astype(jnp.float32)
    mean = jnp.mean(af, -1, keepdims=True)
    var = jnp.mean((af - mean) * (af - mean), -1, keepdims=True)
    return ((af - mean) * lax.rsqrt(var + EPS)).astype(jnp.bfloat16)


def project(h, weight):
    return jnp.dot(h, weight, preferred_element_type=jnp.float32).astype(jnp.bfloat16)


def masked_softmax(scores, key_ok, land_query):
    top = jnp.max(jnp.where(key_ok, scores, NEG), -1, keepdims=True)
    expo = jnp.where(key_ok, jnp.exp(scores - top), 0.0)
    total = jnp.sum(expo, -1, keepdims=True) + land_query[..., None]
    return (expo / total).astype(jnp.bfloat16)


def window_attend(query, keys, values, flags):
    rows, cols, width = query.shape
    nh = HEADS
    hd = width // nh
    scale = hd ** (-0.5)

    def tiles(a):
        a = a.reshape(rows // 8, 8, cols // 8, 8, nh, hd).transpose(0, 2, 4, 1, 3, 5)
        return a.reshape(rows // 8, cols // 8, nh, 64, hd)

    marks = (
        flags.reshape(rows // 8, 8, cols // 8, 8)
        .transpose(0, 2, 1, 3)
        .reshape(rows // 8, cols // 8, 64)
    )
    key_ok = (marks > 0)[:, :, None, None, :]
    land_query = (marks <= 0).astype(jnp.float32)[:, :, None, :]
    scores = (
        jnp.einsum(
            "abhqd,abhkd->abhqk", tiles(query), tiles(keys), preferred_element_type=jnp.float32
        )
        * scale
    )
    probs = masked_softmax(scores, key_ok, land_query)
    outs = jnp.einsum(
        "abhqk,abhkd->abhqd", probs, tiles(values), preferred_element_type=jnp.float32
    )
    outs = outs * (1.0 - land_query)[..., None]
    outs = outs.astype(jnp.bfloat16).reshape(rows // 8, cols // 8, nh, 8, 8, hd)
    return outs.transpose(0, 3, 1, 4, 2, 5).reshape(rows, cols, width)


def row_attend(query, keys, values, flags):
    rows, length, width = query.shape
    nh = HEADS
    hd = width // nh
    scale = hd ** (-0.5)
    key_ok = (flags > 0)[:, None, :]
    land_query = (flags <= 0).astype(jnp.float32)

    def head(index):
        qh = lax.dynamic_slice_in_dim(query, index * hd, hd, 2)
        kh = lax.dynamic_slice_in_dim(keys, index * hd, hd, 2)
        vh = lax.dynamic_slice_in_dim(values, index * hd, hd, 2)
        scores = jnp.einsum("rqd,rkd->rqk", qh, kh, preferred_element_type=jnp.float32) * scale
        probs = masked_softmax(scores, key_ok, land_query)
        return jnp.einsum("rqk,rkd->rqd", probs, vh, preferred_element_type=jnp.float32)

    outs = lax.map(head, jnp.arange(nh, dtype=jnp.int32))
    outs = outs.transpose(1, 2, 0, 3).reshape(rows, length, width)
    return (outs * (1.0 - land_query)[..., None]).astype(jnp.bfloat16)


def attend_columns(columns, marks, w_query1, w_key1, w_value1):
    return window_attend(
        project(columns, w_query1), project(columns, w_key1), project(columns, w_value1), marks
    )


def spread_rows(
    fields, ocean, w_query1, w_key1, w_value1, w_out1, w_query2, w_key2, w_value2, w_out2
):
    rows, cols, width = fields.shape
    normed = norm_rows(fields)
    marks = ocean.astype(jnp.bfloat16)
    edge_feats, edge_marks = passed_along((normed[:, cols - 4 :], marks[:, cols - 4 :]), "lon", 1)
    columns = jnp.concatenate([edge_feats, normed[:, : cols - 4]], 1)
    column_marks = jnp.concatenate([edge_marks, marks[:, : cols - 4]], 1)
    extended = attend_columns(columns, column_marks, w_query1, w_key1, w_value1)
    returned = passed_along(extended[:, :4], "lon", -1)
    o1 = jnp.concatenate([extended[:, 4:], returned], 1)
    y1 = (
        fields.astype(jnp.float32) + jnp.dot(o1, w_out1, preferred_element_type=jnp.float32)
    ).astype(jnp.bfloat16)
    h2 = norm_rows(y1)
    q2 = project(h2, w_query2)
    k2 = project(h2, w_key2)
    v2 = project(h2, w_value2)
    row_q, row_k, row_v, row_marks = (
        lax.all_to_all(q2, "lon", split_axis=0, concat_axis=1, tiled=True),
        lax.all_to_all(k2, "lon", split_axis=0, concat_axis=1, tiled=True),
        lax.all_to_all(v2, "lon", split_axis=0, concat_axis=1, tiled=True),
        lax.all_to_all(marks, "lon", split_axis=0, concat_axis=1, tiled=True),
    )
    row_out = row_attend(row_q, row_k, row_v, row_marks)
    o2 = lax.all_to_all(row_out, "lon", split_axis=1, concat_axis=0, tiled=True)
    return (
        y1.astype(jnp.float32) + jnp.dot(o2, w_out2, preferred_element_type=jnp.float32)
    ).astype(jnp.bfloat16)


def normed_f32(a):
    mean = jnp.mean(a, -1, keepdims=True)
    centred = a - mean
    var = jnp.mean(centred * centred, -1, keepdims=True)
    return (centred * lax.rsqrt(var + EPS)).astype(jnp.bfloat16)


def dot_f32(a, b):
    return jnp.dot(a, b, preferred_element_type=jnp.float32)


def low_columns(shape, axis):
    return lax.broadcasted_iota(jnp.int32, shape, axis) % 8 < 4


def attend(queries, keys, values, query_marks, key_marks):
    n = query_marks.shape[0]
    low = lax.broadcasted_iota(jnp.int32, (n, 128), 1) < 64
    land = 1.0 - query_marks
    bias = (1.0 - key_marks) * NEG
    scores = []
    for q, k in zip(queries, keys):
        zero = jnp.zeros_like(q)
        both = jnp.concatenate([jnp.where(low, q, zero), jnp.where(low, zero, q)], 0)
        scores.append(lax.dot_general(k, both, (((1,), (1,)), ((), ())), preferred_element_type=jnp.float32) + bias)
    expos = [jnp.exp(s - jnp.max(s, 0, keepdims=True)).astype(jnp.bfloat16) for s in scores]
    outs = []
    for expo, v in zip(expos, values):
        wide = jnp.concatenate([v, jnp.ones_like(v)], 1)
        sums = lax.dot_general(expo, wide, (((0,), (0,)), ((), ())), preferred_element_type=jnp.float32)
        upper = jnp.where(low, sums[:n, :128], sums[n:, :128])
        total = jnp.where(low, sums[:n, 128:], sums[n:, 128:]) + land
        outs.append((upper / total * query_marks).astype(jnp.bfloat16))
    return outs


ORDER = (4, 5, 6, 7, 2, 3, 1, 0)


def pack_kernel(distances, me_ref, marks_ref, fields_ref, *refs):
    outs, (held, held_marks, sems) = refs[: len(distances)], refs[len(distances) :]
    me = me_ref[0]
    tiles = fields_ref.shape[-1] // 128
    copies = [pltpu.make_async_copy(marks_ref, held_marks, sems.at[len(distances)])]
    for i, d in enumerate(distances):
        there = jnp.bitwise_xor(me, d)
        copies.append(pltpu.make_async_copy(fields_ref.at[pl.ds(there * 8, 8)], held.at[i], sems.at[i]))
    for copy in copies:
        copy.start()
    copies[0].wait()
    marks = held_marks[...].astype(jnp.float32)
    marks = jnp.concatenate([marks, jnp.zeros((16, 128 - marks.shape[1]), jnp.float32)], 1).astype(jnp.bfloat16)
    for i in range(len(distances)):
        copies[i + 1].wait()
        piece = held[i].reshape(128, 128 * tiles)
        for t in range(tiles):
            outs[i][128 * t : 128 * t + 128, :] = piece[:, 128 * t : 128 * t + 128]
        outs[i][128 * tiles :, :] = marks


def pack(distances, me, marks, fields):
    cols, width = fields.shape[1:]
    vmem = pl.BlockSpec(memory_space=pltpu.VMEM)
    anywhere = pl.BlockSpec(memory_space=pl.ANY)
    piece = jax.ShapeDtypeStruct((width + 16, 128), jnp.bfloat16)
    n = len(distances)
    return pl.pallas_call(
        functools.partial(pack_kernel, distances),
        out_shape=(piece,) * n,
        in_specs=[pl.BlockSpec(memory_space=pltpu.SMEM), anywhere, anywhere],
        out_specs=(vmem,) * n,
        scratch_shapes=[
            pltpu.VMEM((n, 8, cols, width), jnp.bfloat16),
            pltpu.VMEM(marks.shape, marks.dtype),
            pltpu.SemaphoreType.DMA((n + 1,)),
        ],
        compiler_params=pltpu.CompilerParams(vmem_limit_bytes=PACK_VMEM),
        cost_estimate=pl.CostEstimate(flops=n * 200000, bytes_accessed=n * 400000, transcendentals=0),
        name="pack",
    )(me, marks, fields)


def ready_kernel(*refs):
    refs[-1][...] = jnp.zeros_like(refs[-1])


def ready(weights):
    vmem = pl.BlockSpec(memory_space=pltpu.VMEM)
    return pl.pallas_call(
        ready_kernel,
        out_shape=jax.ShapeDtypeStruct((8, 128), jnp.float32),
        in_specs=[vmem] * len(weights),
        out_specs=vmem,
        compiler_params=pltpu.CompilerParams(vmem_limit_bytes=16 * 1024 * 1024),
        cost_estimate=pl.CostEstimate(flops=0, bytes_accessed=32 << 20, transcendentals=0),
        name="ready",
    )(*weights)


def unpacked(me, piece):
    tiles = (piece.shape[0] - 16) // 128
    lanes = [piece[128 * t : 128 * t + 128] for t in range(tiles)]
    marks = pltpu.roll(piece[128 * tiles :].astype(jnp.float32), jnp.bitwise_and(128 - 8 * me, 127), 1)
    marks = jnp.concatenate([jnp.broadcast_to(marks[:, r : r + 1], (16, 128)) for r in range(8)], 0)
    whole = jnp.concatenate(lanes + [marks.astype(jnp.bfloat16)], 1).astype(jnp.float32)
    whole = whole.reshape(8, 2, 8, 128 * tiles + 128)
    return whole[:, 0], whole[:, 1]


STAGES = ((7, 6), (4, 4), (5, 6))


def window_kernel(stage, me_ref, *refs):
    pieces = refs[: (4, 2, 2)[stage]]
    refs = refs[len(pieces) :]
    carried = refs[: (0, 3, 5)[stage]]
    refs = refs[len(carried) :]
    _, wq, wk, wv, wo, wq2, wk2, wv2, y_ref, q2_ref, k2_ref, v2_ref, m_ref = refs[:13]
    refs = refs[13:]
    passed = refs[: (3, 3, 0)[stage]]
    placed, q_s, k_s, v_s, o_s, rows_s = refs[len(passed) :]
    width = wq.shape[0]
    scale = (width // HEADS) ** (-0.5)
    me = me_ref[0]
    upper = jnp.bitwise_and(me, 2) > 0
    low = jnp.bitwise_and(me, len(pieces) - 1)
    for d, piece in enumerate(pieces):
        placed[jnp.bitwise_xor(low, d)] = piece[...]
    columns = [unpacked(me, placed[l]) for l in range(len(pieces))]
    mask = low_columns((8, 8, width + 128), 1)
    full = (64, width + 128)

    def whole_window(l):
        return jnp.where(mask, columns[l][1], columns[l][0]).reshape(full)

    def straddling_window(left, right):
        return jnp.where(mask, right, left).reshape(full)

    def either(if_upper, if_lower):
        return jnp.where(upper, if_upper, if_lower)

    windows = [whole_window(0)]
    for l in range(1, len(pieces)):
        windows += [straddling_window(columns[l - 1][1], columns[l][0]), whole_window(l)]
    first, last = columns[0][0], columns[-1][1]
    if stage < 2:
        passed[0][...] = first.reshape(full)
        passed[1][...] = last.reshape(full)
    edges = [a[...].reshape(8, 8, width + 128) for a in carried[:-1]]
    if stage == 1:
        own_first, own_last = edges
        windows = [straddling_window(either(last, own_last), either(own_first, first))] + windows
    if stage == 2:
        own_first, own_last, second_first, second_last = edges
        windows = (
            [straddling_window(either(last, second_last), either(second_first, first))]
            + windows
            + [straddling_window(either(own_last, last), either(first, own_first))]
        )
    count = len(windows)
    x = jnp.concatenate([w[:, :width] for w in windows], 0)
    marks = [w[:, width:] for w in windows]
    h = normed_f32(x)
    q_s[...] = (dot_f32(h, wq[...]) * scale).astype(jnp.bfloat16)
    k_s[...] = dot_f32(h, wk[...]).astype(jnp.bfloat16)
    v_s[...] = dot_f32(h, wv[...]).astype(jnp.bfloat16)
    for w in range(count):
        here = slice(64 * w, 64 * w + 64)
        outs = attend(*([a[here, lanes] for lanes in PAIRS] for a in (q_s, k_s, v_s)), marks[w], marks[w])
        for lanes, out in zip(PAIRS, outs):
            o_s[here, lanes] = out
    y = (x + dot_f32(o_s[...], wo[...])).astype(jnp.bfloat16).astype(jnp.float32)
    for r in range(8):
        tiles = [
            jnp.concatenate([y[64 * w + 8 * r : 64 * w + 8 * r + 8], marks[w][8 * r : 8 * r + 8]], 1)
            for w in range(count)
        ]
        if stage == 0:
            *tiles, passed[2][r] = tiles
        if stage == 1:
            passed[2][r] = tiles[0]
            tiles = [tiles[1], tiles[2], carried[-1][r], tiles[3]]
        if stage == 2:
            one, other = carried[-1][r], tiles.pop()
            tiles += [
                jnp.where(mask[0], either(one, other), either(other, one)),
                jnp.where(mask[0], either(other, one), either(one, other)),
            ]
        for w, tile in enumerate(tiles):
            rows_s[r, 8 * w : 8 * w + 8, :] = tile
    tokens = rows_s.shape[0] * rows_s.shape[1]
    y = rows_s[:, :, :width].reshape(tokens, width)
    m_ref[...] = rows_s[:, :, width:].astype(jnp.bfloat16)
    y_ref[...] = y.astype(jnp.bfloat16).reshape(y_ref.shape)
    h = normed_f32(y)
    q2_ref[...] = (dot_f32(h, wq2[...]) * scale).astype(jnp.bfloat16).reshape(q2_ref.shape)
    k2_ref[...] = dot_f32(h, wk2[...]).astype(jnp.bfloat16).reshape(k2_ref.shape)
    v2_ref[...] = dot_f32(h, wv2[...]).astype(jnp.bfloat16).reshape(v2_ref.shape)


def window_layer(stage, me, pieces, carried, weights):
    width = weights[1].shape[0]
    tokens = 64 * STAGES[stage][0]
    columns = 8 * STAGES[stage][1]
    part = jax.ShapeDtypeStruct((8, columns, width), jnp.bfloat16)
    marks = jax.ShapeDtypeStruct((8, columns, 128), jnp.bfloat16)
    edge = jax.ShapeDtypeStruct((64, width + 128), jnp.float32)
    tail = jax.ShapeDtypeStruct((8, 8, width + 128), jnp.float32)
    outs = (part,) * 4 + (marks,) + ((edge, edge, tail), (edge, edge, tail), ())[stage]
    vmem = pl.BlockSpec(memory_space=pltpu.VMEM)
    work = pltpu.VMEM((tokens, width), jnp.bfloat16)
    inputs = [*pieces, *carried, *weights]
    return pl.pallas_call(
        functools.partial(window_kernel, stage),
        out_shape=outs,
        in_specs=[pl.BlockSpec(memory_space=pltpu.SMEM)] + [vmem] * len(inputs),
        out_specs=(vmem,) * len(outs),
        scratch_shapes=[
            pltpu.VMEM((len(pieces), width + 16, 128), jnp.bfloat16),
            work, work, work, work,
            pltpu.VMEM((8, columns, width + 128), jnp.float32),
        ],
        compiler_params=pltpu.CompilerParams(vmem_limit_bytes=36 * 1024 * 1024),
        cost_estimate=pl.CostEstimate(
            flops=2 * tokens * width * (7 * width + 512), bytes_accessed=16 << 20, transcendentals=tokens * 64 * HEADS
        ),
        name="window_layer",
    )(me, *inputs)


def row_kernel(far, me_ref, *refs):
    parts, wo, refs = (refs[:5], refs[5:10], refs[10:15]), refs[15], refs[16:]
    (*outs, o_s, placed) = refs if far else refs[1:]
    width = wo.shape[0]
    count = 64

    def keys(i, r, lanes=slice(None)):
        return jnp.concatenate([part[i][r, :, lanes] for part in parts], 0)

    def queries(i, r, lanes=slice(None)):
        mixed = [parts[1][i][r, 16:, lanes], parts[2][i][r, 32:, lanes]]
        mixed = [a.astype(jnp.float32)[8:] if far else a.astype(jnp.float32)[:8] for a in mixed]
        mixed = jnp.concatenate(mixed, 0).astype(jnp.bfloat16)
        whole = [parts[1][i][r, :16, lanes], parts[2][i][r, :32, lanes]] if far else [parts[0][i][r, :, lanes]]
        return jnp.concatenate([*whole, mixed], 0)

    for r in range(8):
        heads = attend(
            [queries(1, r, lanes) for lanes in PAIRS],
            [keys(2, r, lanes) for lanes in PAIRS],
            [keys(3, r, lanes) for lanes in PAIRS],
            queries(4, r).astype(jnp.float32),
            keys(4, r).astype(jnp.float32),
        )
        for lanes, out in zip(PAIRS, heads):
            o_s[count * r : count * r + count, lanes] = out
    added = dot_f32(o_s[...], wo[...])
    mask = low_columns((8, width), 0)
    me = me_ref[0]
    upper = jnp.bitwise_and(me, 2) > 0
    for r in range(8):
        f = queries(0, r).astype(jnp.float32) + added[count * r : count * r + count]
        tiles = [f[8 * w : 8 * w + 8] for w in range(8)]
        if far:
            second, middle, third, edge = (tiles[0], tiles[1], tiles[6]), tiles[2], tiles[3:6], tiles[7]
            start, end = jnp.where(upper, middle, edge), jnp.where(upper, edge, middle)
            whole = ((start, *second, end), (end, *third, start))
            pieces = [side[at : at + 3] for side in whole for at in (0, 2)]
        else:
            whole = (tiles[7], *tiles[:7], tiles[7])
            pieces = [whole[at : at + 3] for at in (0, 2, 4, 6)]
        for l, (before, a, after) in enumerate(pieces):
            piece = jnp.concatenate([jnp.where(mask, before, a), jnp.where(mask, a, after)], 0)
            placed[l, r] = piece.astype(jnp.bfloat16)
    for out, d in zip(outs, ORDER[:4] if far else ORDER[4:]):
        if far:
            out[...] = placed[(d - 4) // 2 * 2 + jnp.bitwise_xor(jnp.bitwise_and(me, 1), d % 2)]
        else:
            out[...] = placed[jnp.bitwise_xor(jnp.bitwise_and(me, 3), d)]


def row_layer(far, me, parts, w_out, after=()):
    width = w_out.shape[0]
    piece = jax.ShapeDtypeStruct((8, 16, width), jnp.bfloat16)
    vmem = pl.BlockSpec(memory_space=pltpu.VMEM)
    return pl.pallas_call(
        functools.partial(row_kernel, far),
        out_shape=(piece,) * 4,
        in_specs=[pl.BlockSpec(memory_space=pltpu.SMEM)] + [vmem] * (len(parts) + 1) + [pl.BlockSpec(memory_space=pl.ANY)] * len(after),
        out_specs=(vmem,) * 4,
        scratch_shapes=[pltpu.VMEM((8 * 64, width), jnp.bfloat16), pltpu.VMEM((4, 8, 16, width), jnp.bfloat16)],
        compiler_params=pltpu.CompilerParams(vmem_limit_bytes=36 * 1024 * 1024),
        cost_estimate=pl.CostEstimate(
            flops=0, bytes_accessed=1 << 10, transcendentals=0
        ),
        name="row_layer",
    )(me, *parts, w_out, *after)


def place_kernel(distances, me_ref, *refs):
    pieces, out_ref, sems = refs[: len(distances)], refs[-2], refs[-1]
    copies = []
    for i, d in enumerate(distances):
        at = jnp.bitwise_xor(me_ref[0], d) * 8
        copies.append(pltpu.make_async_copy(pieces[i], out_ref.at[pl.ds(at, 8)], sems.at[i]))
        copies[-1].start()
    for copy in copies:
        copy.wait()


def place(distances, me, pieces, so_far, shape):
    vmem = pl.BlockSpec(memory_space=pltpu.VMEM)
    hbm = pl.BlockSpec(memory_space=pltpu.HBM)
    n = len(pieces)
    more = () if so_far is None else (so_far,)
    return pl.pallas_call(
        functools.partial(place_kernel, distances),
        out_shape=jax.ShapeDtypeStruct(shape, jnp.bfloat16),
        in_specs=[pl.BlockSpec(memory_space=pltpu.SMEM)] + [vmem] * n + [hbm] * len(more),
        out_specs=hbm,
        scratch_shapes=[pltpu.SemaphoreType.DMA((n,))],
        input_output_aliases={n + 1: 0} if more else {},
        compiler_params=pltpu.CompilerParams(vmem_limit_bytes=8 * 1024 * 1024),
        cost_estimate=pl.CostEstimate(flops=0, bytes_accessed=4 << 20, transcendentals=0),
        name="place",
    )(me, *pieces, *more)


def exchanged(piece, distance):
    count = lax.axis_size("lon")
    return lax.ppermute(piece, "lon", [(s, s ^ distance) for s in range(count)])


def gathered_bands(
    fields, ocean, w_query1, w_key1, w_value1, w_out1, w_query2, w_key2, w_value2, w_out2
):
    me = lax.axis_index("lon").astype(jnp.int32).reshape(1)
    weights = (w_query1, w_key1, w_value1, w_out1, w_query2, w_key2, w_value2)
    weights = (ready(weights), *weights)

    packed = dict(zip(ORDER, pack(ORDER, me, ocean.T, fields)))
    got = {d: exchanged(packed[d], d) if d else packed[d] for d in ORDER}
    early = (4, 2, 5, 3, 1)
    got.update(zip(early, lax.optimization_barrier(tuple(got[d] for d in early))))
    own = window_layer(0, me, [got[d] for d in range(4)], (), weights)
    second = window_layer(1, me, [got[4], got[5]], own[5:], weights)
    third = window_layer(2, me, [got[6], got[7]], (*own[5:7], *second[5:]), weights)
    parts = (*own[:5], *second[:5], *third)
    far = row_layer(True, me, parts, w_out2)
    near = row_layer(False, me, parts, w_out2, far[:1])
    far = [exchanged(piece, d) for d, piece in zip(ORDER[:4], far)]
    near = [exchanged(piece, d) if d else piece for d, piece in zip(ORDER[4:], near)]
    out = place(ORDER[:4], me, far, None, fields.shape)
    return place(ORDER[4:], me, near, out, fields.shape)


def on_device(fields, *rest):
    rows, cols, width = fields.shape
    if lax.axis_size("lon") == 8 and rows == 64 and cols == 16 and width == 64 * HEADS:
        return gathered_bands(fields, *rest)
    return spread_rows(fields, *rest)


def solution(mesh):
    in_specs = (
        P(("grp", "lat"), "lon", None),
        P(("grp", "lat"), "lon"),
        P(),
        P(),
        P(),
        P(),
        P(),
        P(),
        P(),
        P(),
    )
    out_specs = P(("grp", "lat"), "lon", None)
    return jax.shard_map(
        on_device, mesh=mesh, in_specs=in_specs, out_specs=out_specs, check_vma=False
    )
```

```python
import functools

import jax
import jax.numpy as jnp
from jax import lax
from jax.experimental import pallas as pl
from jax.experimental.pallas import tpu as pltpu
from jax.sharding import PartitionSpec as P

HEADS = 12


EPS = 1e-05
NEG = -1e30

ROWS_FIRST = 4

PACK_VMEM = 52 * 1024 * 1024

PAIRS = [slice(128 * p, 128 * p + 128) for p in range(HEADS // 2)]


def passed_along(value, axis, steps):
    count = lax.axis_size(axis)
    pairs = [(source, (source + steps) % count) for source in range(count)]
    return lax.ppermute(value, axis, pairs)


def norm_rows(a):
    af = a.astype(jnp.float32)
    mean = jnp.mean(af, -1, keepdims=True)
    var = jnp.mean((af - mean) * (af - mean), -1, keepdims=True)
    return ((af - mean) * lax.rsqrt(var + EPS)).astype(jnp.bfloat16)


def project(h, weight):
    return jnp.dot(h, weight, preferred_element_type=jnp.float32).astype(jnp.bfloat16)


def masked_softmax(scores, key_ok, land_query):
    top = jnp.max(jnp.where(key_ok, scores, NEG), -1, keepdims=True)
    expo = jnp.where(key_ok, jnp.exp(scores - top), 0.0)
    total = jnp.sum(expo, -1, keepdims=True) + land_query[..., None]
    return (expo / total).astype(jnp.bfloat16)


def window_attend(query, keys, values, flags):
    rows, cols, width = query.shape
    nh = HEADS
    hd = width // nh
    scale = hd ** (-0.5)

    def tiles(a):
        a = a.reshape(rows // 8, 8, cols // 8, 8, nh, hd).transpose(0, 2, 4, 1, 3, 5)
        return a.reshape(rows // 8, cols // 8, nh, 64, hd)

    marks = (
        flags.reshape(rows // 8, 8, cols // 8, 8)
        .transpose(0, 2, 1, 3)
        .reshape(rows // 8, cols // 8, 64)
    )
    key_ok = (marks > 0)[:, :, None, None, :]
    land_query = (marks <= 0).astype(jnp.float32)[:, :, None, :]
    scores = (
        jnp.einsum(
            "abhqd,abhkd->abhqk", tiles(query), tiles(keys), preferred_element_type=jnp.float32
        )
        * scale
    )
    probs = masked_softmax(scores, key_ok, land_query)
    outs = jnp.einsum(
        "abhqk,abhkd->abhqd", probs, tiles(values), preferred_element_type=jnp.float32
    )
    outs = outs * (1.0 - land_query)[..., None]
    outs = outs.astype(jnp.bfloat16).reshape(rows // 8, cols // 8, nh, 8, 8, hd)
    return outs.transpose(0, 3, 1, 4, 2, 5).reshape(rows, cols, width)


def row_attend(query, keys, values, flags):
    rows, length, width = query.shape
    nh = HEADS
    hd = width // nh
    scale = hd ** (-0.5)
    key_ok = (flags > 0)[:, None, :]
    land_query = (flags <= 0).astype(jnp.float32)

    def head(index):
        qh = lax.dynamic_slice_in_dim(query, index * hd, hd, 2)
        kh = lax.dynamic_slice_in_dim(keys, index * hd, hd, 2)
        vh = lax.dynamic_slice_in_dim(values, index * hd, hd, 2)
        scores = jnp.einsum("rqd,rkd->rqk", qh, kh, preferred_element_type=jnp.float32) * scale
        probs = masked_softmax(scores, key_ok, land_query)
        return jnp.einsum("rqk,rkd->rqd", probs, vh, preferred_element_type=jnp.float32)

    outs = lax.map(head, jnp.arange(nh, dtype=jnp.int32))
    outs = outs.transpose(1, 2, 0, 3).reshape(rows, length, width)
    return (outs * (1.0 - land_query)[..., None]).astype(jnp.bfloat16)


def attend_columns(columns, marks, w_query1, w_key1, w_value1):
    return window_attend(
        project(columns, w_query1), project(columns, w_key1), project(columns, w_value1), marks
    )


def spread_rows(
    fields, ocean, w_query1, w_key1, w_value1, w_out1, w_query2, w_key2, w_value2, w_out2
):
    rows, cols, width = fields.shape
    normed = norm_rows(fields)
    marks = ocean.astype(jnp.bfloat16)
    edge_feats, edge_marks = passed_along((normed[:, cols - 4 :], marks[:, cols - 4 :]), "lon", 1)
    columns = jnp.concatenate([edge_feats, normed[:, : cols - 4]], 1)
    column_marks = jnp.concatenate([edge_marks, marks[:, : cols - 4]], 1)
    extended = attend_columns(columns, column_marks, w_query1, w_key1, w_value1)
    returned = passed_along(extended[:, :4], "lon", -1)
    o1 = jnp.concatenate([extended[:, 4:], returned], 1)
    y1 = (
        fields.astype(jnp.float32) + jnp.dot(o1, w_out1, preferred_element_type=jnp.float32)
    ).astype(jnp.bfloat16)
    h2 = norm_rows(y1)
    q2 = project(h2, w_query2)
    k2 = project(h2, w_key2)
    v2 = project(h2, w_value2)
    row_q, row_k, row_v, row_marks = (
        lax.all_to_all(q2, "lon", split_axis=0, concat_axis=1, tiled=True),
        lax.all_to_all(k2, "lon", split_axis=0, concat_axis=1, tiled=True),
        lax.all_to_all(v2, "lon", split_axis=0, concat_axis=1, tiled=True),
        lax.all_to_all(marks, "lon", split_axis=0, concat_axis=1, tiled=True),
    )
    row_out = row_attend(row_q, row_k, row_v, row_marks)
    o2 = lax.all_to_all(row_out, "lon", split_axis=1, concat_axis=0, tiled=True)
    return (
        y1.astype(jnp.float32) + jnp.dot(o2, w_out2, preferred_element_type=jnp.float32)
    ).astype(jnp.bfloat16)


def normed_f32(a):
    mean = jnp.mean(a, -1, keepdims=True)
    centred = a - mean
    var = jnp.mean(centred * centred, -1, keepdims=True)
    return (centred * lax.rsqrt(var + EPS)).astype(jnp.bfloat16)


def dot_f32(a, b):
    return jnp.dot(a, b, preferred_element_type=jnp.float32)


def low_columns(shape, axis):
    return lax.broadcasted_iota(jnp.int32, shape, axis) % 8 < 4


def attend(queries, keys, values, marks):
    n = marks.shape[0]
    low = lax.broadcasted_iota(jnp.int32, (n, 128), 1) < 64
    land = 1.0 - marks
    bias = jnp.concatenate([land * NEG] * (2 * n // 128), 1)
    scores = []
    for q, k in zip(queries, keys):
        zero = jnp.zeros_like(q)
        both = jnp.concatenate([jnp.where(low, q, zero), jnp.where(low, zero, q)], 0)
        scores.append(lax.dot_general(k, both, (((1,), (1,)), ((), ())), preferred_element_type=jnp.float32) + bias)
    expos = [jnp.exp(s - jnp.max(s, 0, keepdims=True)).astype(jnp.bfloat16) for s in scores]
    outs = []
    for expo, v in zip(expos, values):
        wide = jnp.concatenate([v, jnp.ones_like(v)], 1)
        sums = lax.dot_general(expo, wide, (((0,), (0,)), ((), ())), preferred_element_type=jnp.float32)
        upper = jnp.where(low, sums[:n, :128], sums[n:, :128])
        total = jnp.where(low, sums[:n, 128:], sums[n:, 128:]) + land
        outs.append((upper / total * marks).astype(jnp.bfloat16))
    return outs


ORDER = (4, 5, 6, 7, 1, 2, 3, 0)


def pack_kernel(distances, me_ref, marks_ref, fields_ref, *refs):
    outs, (held, held_marks, sems) = refs[: len(distances)], refs[len(distances) :]
    me = me_ref[0]
    tiles = fields_ref.shape[-1] // 128
    copies = [pltpu.make_async_copy(marks_ref, held_marks, sems.at[len(distances)])]
    for i, d in enumerate(distances):
        there = jnp.bitwise_xor(me, d)
        copies.append(pltpu.make_async_copy(fields_ref.at[pl.ds(there * 8, 8)], held.at[i], sems.at[i]))
    for copy in copies:
        copy.start()
    copies[0].wait()
    marks = held_marks[...].astype(jnp.float32)
    marks = jnp.concatenate([marks, jnp.zeros((16, 128 - marks.shape[1]), jnp.float32)], 1).astype(jnp.bfloat16)
    for i in range(len(distances)):
        copies[i + 1].wait()
        piece = held[i].reshape(128, 128 * tiles)
        for t in range(tiles):
            outs[i][128 * t : 128 * t + 128, :] = piece[:, 128 * t : 128 * t + 128]
        outs[i][128 * tiles :, :] = marks


def pack(distances, me, marks, fields):
    cols, width = fields.shape[1:]
    vmem = pl.BlockSpec(memory_space=pltpu.VMEM)
    anywhere = pl.BlockSpec(memory_space=pl.ANY)
    piece = jax.ShapeDtypeStruct((width + 16, 128), jnp.bfloat16)
    n = len(distances)
    return pl.pallas_call(
        functools.partial(pack_kernel, distances),
        out_shape=(piece,) * n,
        in_specs=[pl.BlockSpec(memory_space=pltpu.SMEM), anywhere, anywhere],
        out_specs=(vmem,) * n,
        scratch_shapes=[
            pltpu.VMEM((n, 8, cols, width), jnp.bfloat16),
            pltpu.VMEM(marks.shape, marks.dtype),
            pltpu.SemaphoreType.DMA((n + 1,)),
        ],
        compiler_params=pltpu.CompilerParams(vmem_limit_bytes=PACK_VMEM),
        cost_estimate=pl.CostEstimate(flops=n * 200000, bytes_accessed=n * 400000, transcendentals=0),
        name="pack",
    )(me, marks, fields)


def ready_kernel(*refs):
    refs[-1][...] = jnp.zeros_like(refs[-1])


def ready(weights):
    vmem = pl.BlockSpec(memory_space=pltpu.VMEM)
    return pl.pallas_call(
        ready_kernel,
        out_shape=jax.ShapeDtypeStruct((8, 128), jnp.float32),
        in_specs=[vmem] * len(weights),
        out_specs=vmem,
        compiler_params=pltpu.CompilerParams(vmem_limit_bytes=16 * 1024 * 1024),
        cost_estimate=pl.CostEstimate(flops=0, bytes_accessed=32 << 20, transcendentals=0),
        name="ready",
    )(*weights)


def unpacked(me, piece):
    tiles = (piece.shape[0] - 16) // 128
    lanes = [piece[128 * t : 128 * t + 128] for t in range(tiles)]
    marks = pltpu.roll(piece[128 * tiles :].astype(jnp.float32), jnp.bitwise_and(128 - 8 * me, 127), 1)
    marks = jnp.concatenate([jnp.broadcast_to(marks[:, r : r + 1], (16, 128)) for r in range(8)], 0)
    whole = jnp.concatenate(lanes + [marks.astype(jnp.bfloat16)], 1).astype(jnp.float32)
    whole = whole.reshape(8, 2, 8, 128 * tiles + 128)
    return whole[:, 0], whole[:, 1]


STAGES = ((7, 6), (4, 4), (5, 6))


def window_kernel(stage, me_ref, *refs):
    pieces = refs[: (4, 2, 2)[stage]]
    refs = refs[len(pieces) :]
    carried = refs[: (0, 3, 5)[stage]]
    refs = refs[len(carried) :]
    _, wq, wk, wv, wo, wq2, wk2, wv2, y_ref, q2_ref, k2_ref, v2_ref, m_ref = refs[:13]
    refs = refs[13:]
    passed = refs[: (3, 3, 0)[stage]]
    placed, q_s, k_s, v_s, o_s, rows_s = refs[len(passed) :]
    width = wq.shape[0]
    scale = (width // HEADS) ** (-0.5)
    me = me_ref[0]
    upper = jnp.bitwise_and(me, 2) > 0
    low = jnp.bitwise_and(me, len(pieces) - 1)
    for d, piece in enumerate(pieces):
        placed[jnp.bitwise_xor(low, d)] = piece[...]
    columns = [unpacked(me, placed[l]) for l in range(len(pieces))]
    mask = low_columns((8, 8, width + 128), 1)
    full = (64, width + 128)

    def whole_window(l):
        return jnp.where(mask, columns[l][1], columns[l][0]).reshape(full)

    def straddling_window(left, right):
        return jnp.where(mask, right, left).reshape(full)

    def either(if_upper, if_lower):
        return jnp.where(upper, if_upper, if_lower)

    windows = [whole_window(0)]
    for l in range(1, len(pieces)):
        windows += [straddling_window(columns[l - 1][1], columns[l][0]), whole_window(l)]
    first, last = columns[0][0], columns[-1][1]
    if stage < 2:
        passed[0][...] = first.reshape(full)
        passed[1][...] = last.reshape(full)
    edges = [a[...].reshape(8, 8, width + 128) for a in carried[:-1]]
    if stage == 1:
        own_first, own_last = edges
        windows = [straddling_window(either(last, own_last), either(own_first, first))] + windows
    if stage == 2:
        own_first, own_last, second_first, second_last = edges
        windows = (
            [straddling_window(either(last, second_last), either(second_first, first))]
            + windows
            + [straddling_window(either(own_last, last), either(first, own_first))]
        )
    count = len(windows)
    x = jnp.concatenate([w[:, :width] for w in windows], 0)
    marks = [w[:, width:] for w in windows]
    h = normed_f32(x)
    q_s[...] = (dot_f32(h, wq[...]) * scale).astype(jnp.bfloat16)
    k_s[...] = dot_f32(h, wk[...]).astype(jnp.bfloat16)
    v_s[...] = dot_f32(h, wv[...]).astype(jnp.bfloat16)
    for w in range(count):
        here = slice(64 * w, 64 * w + 64)
        outs = attend(*([a[here, lanes] for lanes in PAIRS] for a in (q_s, k_s, v_s)), marks[w])
        for lanes, out in zip(PAIRS, outs):
            o_s[here, lanes] = out
    y = (x + dot_f32(o_s[...], wo[...])).astype(jnp.bfloat16).astype(jnp.float32)
    skip = 0
    if stage > 0:
        skip = 1
        rows_s[:, :8, :] = carried[-1][...]
    for w in range(count):
        for r in range(8):
            at = 64 * w + 8 * r
            to = 8 * (w + skip)
            if stage < 2 and w == count - 1:
                passed[2][r, :, :width] = y[at : at + 8]
                passed[2][r, :, width:] = marks[w][8 * r : 8 * r + 8]
            else:
                rows_s[r, to : to + 8, :width] = y[at : at + 8]
                rows_s[r, to : to + 8, width:] = marks[w][8 * r : 8 * r + 8]
    tokens = rows_s.shape[0] * rows_s.shape[1]
    y = rows_s[:, :, :width].reshape(tokens, width)
    m_ref[...] = rows_s[:, :, width:].astype(jnp.bfloat16)
    y_ref[...] = y.astype(jnp.bfloat16).reshape(y_ref.shape)
    h = normed_f32(y)
    q2_ref[...] = (dot_f32(h, wq2[...]) * scale).astype(jnp.bfloat16).reshape(q2_ref.shape)
    k2_ref[...] = dot_f32(h, wk2[...]).astype(jnp.bfloat16).reshape(k2_ref.shape)
    v2_ref[...] = dot_f32(h, wv2[...]).astype(jnp.bfloat16).reshape(v2_ref.shape)


def window_layer(stage, me, pieces, carried, weights):
    width = weights[1].shape[0]
    tokens = 64 * STAGES[stage][0]
    columns = 8 * STAGES[stage][1]
    part = jax.ShapeDtypeStruct((8, columns, width), jnp.bfloat16)
    marks = jax.ShapeDtypeStruct((8, columns, 128), jnp.bfloat16)
    edge = jax.ShapeDtypeStruct((64, width + 128), jnp.float32)
    tail = jax.ShapeDtypeStruct((8, 8, width + 128), jnp.float32)
    outs = (part,) * 4 + (marks,) + ((edge, edge, tail), (edge, edge, tail), ())[stage]
    vmem = pl.BlockSpec(memory_space=pltpu.VMEM)
    work = pltpu.VMEM((tokens, width), jnp.bfloat16)
    inputs = [*pieces, *carried, *weights]
    return pl.pallas_call(
        functools.partial(window_kernel, stage),
        out_shape=outs,
        in_specs=[pl.BlockSpec(memory_space=pltpu.SMEM)] + [vmem] * len(inputs),
        out_specs=(vmem,) * len(outs),
        scratch_shapes=[
            pltpu.VMEM((len(pieces), width + 16, 128), jnp.bfloat16),
            work, work, work, work,
            pltpu.VMEM((8, columns, width + 128), jnp.float32),
        ],
        compiler_params=pltpu.CompilerParams(vmem_limit_bytes=36 * 1024 * 1024),
        cost_estimate=pl.CostEstimate(
            flops=2 * tokens * width * (7 * width + 512), bytes_accessed=16 << 20, transcendentals=tokens * 64 * HEADS
        ),
        name="window_layer",
    )(me, *inputs)


def row_kernel(start, rows, me_ref, *refs):
    parts, wo, refs = (refs[:5], refs[5:10], refs[10:15]), refs[15], refs[16:]
    earlier, refs = (refs[:4], refs[4:]) if start else ((), refs)
    outs, (o_s, placed) = refs[:8], refs[8:]
    width = wo.shape[0]
    length = 128

    def row(i, r, lanes=slice(None)):
        return jnp.concatenate([part[i][start + r, :, lanes] for part in parts], 0)

    for r in range(rows):
        here = slice(length * r, length * r + length)
        heads = attend(*([row(i, r, lanes) for lanes in PAIRS] for i in (1, 2, 3)), row(4, r).astype(jnp.float32))
        for lanes, out in zip(PAIRS, heads):
            o_s[here, lanes] = out
    added = dot_f32(o_s[...], wo[...])
    mask = low_columns((8, width), 0)
    me = me_ref[0]
    upper = jnp.bitwise_and(me, 2) > 0
    for r in range(rows):
        f = row(0, r).astype(jnp.float32) + added[length * r : length * r + length]
        tiles = [f[8 * w : 8 * w + 8] for w in range(16)]
        own, second, third = tiles[:7], tiles[8:11], tiles[12:15]
        own_second, middle, third_own = tiles[7], tiles[11], tiles[15]
        after_own = jnp.where(upper, third_own, own_second)
        before_own = jnp.where(upper, own_second, third_own)
        whole = [before_own, *own, after_own]
        whole += [jnp.where(upper, middle, after_own), *second, jnp.where(upper, before_own, middle)]
        whole += [jnp.where(upper, after_own, middle), *third, jnp.where(upper, middle, before_own)]
        for l in range(8):
            at = 2 * l if l < 4 else (9, 11, 14, 16)[l - 4]
            before, a, after = whole[at : at + 3]
            piece = jnp.concatenate([jnp.where(mask, before, a), jnp.where(mask, a, after)], 0)
            placed[l, r] = piece.astype(jnp.bfloat16)
    for i, d in enumerate(ORDER):
        if d < 4:
            if start:
                outs[i][:start] = earlier[i - 4][...]
            outs[i][start:] = placed[jnp.bitwise_xor(jnp.bitwise_and(me, 3), d)]
        else:
            outs[i][...] = placed[d // 2 * 2 + jnp.bitwise_xor(jnp.bitwise_and(me, 1), d % 2)]


def row_layer(start, rows, me, parts, w_out, earlier):
    width = w_out.shape[0]
    length = 128
    far = jax.ShapeDtypeStruct((rows, 16, width), jnp.bfloat16)
    near = jax.ShapeDtypeStruct((start + rows, 16, width), jnp.bfloat16)
    vmem = pl.BlockSpec(memory_space=pltpu.VMEM)
    inputs = [*parts, w_out, *earlier]
    return pl.pallas_call(
        functools.partial(row_kernel, start, rows),
        out_shape=(far,) * 4 + (near,) * 4,
        in_specs=[pl.BlockSpec(memory_space=pltpu.SMEM)] + [vmem] * len(inputs),
        out_specs=(vmem,) * 8,
        scratch_shapes=[
            pltpu.VMEM((rows * length, width), jnp.bfloat16),
            pltpu.VMEM((8, rows, 16, width), jnp.bfloat16),
        ],
        compiler_params=pltpu.CompilerParams(vmem_limit_bytes=36 * 1024 * 1024),
        cost_estimate=pl.CostEstimate(
            flops=0, bytes_accessed=1 << 16, transcendentals=0
        ),
        name="row_layer",
    )(me, *inputs)


def place_kernel(spots, me_ref, *refs):
    pieces, out_ref, sems = refs[: len(spots)], refs[-2], refs[-1]
    copies = []
    for i, (d, start) in enumerate(spots):
        at = jnp.bitwise_xor(me_ref[0], d) * 8 + start
        copies.append(pltpu.make_async_copy(pieces[i], out_ref.at[pl.ds(at, pieces[i].shape[0])], sems.at[i]))
        copies[-1].start()
    for copy in copies:
        copy.wait()


def place(spots, me, pieces, so_far, shape):
    vmem = pl.BlockSpec(memory_space=pltpu.VMEM)
    hbm = pl.BlockSpec(memory_space=pltpu.HBM)
    n = len(pieces)
    more = () if so_far is None else (so_far,)
    return pl.pallas_call(
        functools.partial(place_kernel, spots),
        out_shape=jax.ShapeDtypeStruct(shape, jnp.bfloat16),
        in_specs=[pl.BlockSpec(memory_space=pltpu.SMEM)] + [vmem] * n + [hbm] * len(more),
        out_specs=hbm,
        scratch_shapes=[pltpu.SemaphoreType.DMA((n,))],
        input_output_aliases={n + 1: 0} if more else {},
        compiler_params=pltpu.CompilerParams(vmem_limit_bytes=8 * 1024 * 1024),
        cost_estimate=pl.CostEstimate(flops=0, bytes_accessed=4 << 20, transcendentals=0),
        name="place",
    )(me, *pieces, *more)


def exchanged(piece, distance):
    count = lax.axis_size("lon")
    return lax.ppermute(piece, "lon", [(s, s ^ distance) for s in range(count)])


def gathered_bands(
    fields, ocean, w_query1, w_key1, w_value1, w_out1, w_query2, w_key2, w_value2, w_out2
):
    me = lax.axis_index("lon").astype(jnp.int32).reshape(1)
    weights = (w_query1, w_key1, w_value1, w_out1, w_query2, w_key2, w_value2)
    weights = (ready(weights[:3]), *weights)

    packed = dict(zip(ORDER, pack(ORDER, me, ocean.T, fields)))
    got = {d: exchanged(packed[d], d) if d else packed[d] for d in ORDER}
    early = (2, 4, 3, 5, 1)
    got.update(zip(early, lax.optimization_barrier(tuple(got[d] for d in early))))
    own = window_layer(0, me, [got[d] for d in range(4)], (), weights)
    second = window_layer(1, me, [got[4], got[5]], own[5:], weights)
    third = window_layer(2, me, [got[6], got[7]], (*own[5:7], *second[5:]), weights)
    parts = (*own[:5], *second[:5], *third)
    first = row_layer(0, ROWS_FIRST, me, parts, w_out2, ())
    last = row_layer(ROWS_FIRST, 8 - ROWS_FIRST, me, parts, w_out2, first[4:])
    far = [exchanged(piece, d) for d, piece in zip(ORDER[:4], first)]
    last = list(last)
    for i in range(4):
        last[i], last[4 + i], far[i] = lax.optimization_barrier((last[i], last[4 + i], far[i]))
    far_last = [exchanged(piece, d) for d, piece in zip(ORDER[:4], last)]
    near = [exchanged(piece, d) if d else piece for d, piece in zip(ORDER[4:], last[4:])]
    out = place([(d, 0) for d in ORDER], me, far + near, None, fields.shape)
    return place([(d, ROWS_FIRST) for d in ORDER[:4]], me, far_last, out, fields.shape)


def on_device(fields, *rest):
    rows, cols, width = fields.shape
    if lax.axis_size("lon") == 8 and rows == 64 and cols == 16 and width == 64 * HEADS:
        return gathered_bands(fields, *rest)
    return spread_rows(fields, *rest)


def solution(mesh):
    in_specs = (
        P(("grp", "lat"), "lon", None),
        P(("grp", "lat"), "lon"),
        P(),
        P(),
        P(),
        P(),
        P(),
        P(),
        P(),
        P(),
    )
    out_specs = P(("grp", "lat"), "lon", None)
    return jax.shard_map(
        on_device, mesh=mesh, in_specs=in_specs, out_specs=out_specs, check_vma=False
    )
```

```python
import functools

import jax
import jax.numpy as jnp
from jax import lax
from jax.experimental import pallas as pl
from jax.experimental.pallas import tpu as pltpu
from jax.sharding import PartitionSpec as P

HEADS = 12


EPS = 1e-05
NEG = -1e30

ROWS_FIRST = 4

PACK_VMEM = 52 * 1024 * 1024

PAIRS = [slice(128 * p, 128 * p + 128) for p in range(HEADS // 2)]


def passed_along(value, axis, steps):
    count = lax.axis_size(axis)
    pairs = [(source, (source + steps) % count) for source in range(count)]
    return lax.ppermute(value, axis, pairs)


def norm_rows(a):
    af = a.astype(jnp.float32)
    mean = jnp.mean(af, -1, keepdims=True)
    var = jnp.mean((af - mean) * (af - mean), -1, keepdims=True)
    return ((af - mean) * lax.rsqrt(var + EPS)).astype(jnp.bfloat16)


def project(h, weight):
    return jnp.dot(h, weight, preferred_element_type=jnp.float32).astype(jnp.bfloat16)


def masked_softmax(scores, key_ok, land_query):
    top = jnp.max(jnp.where(key_ok, scores, NEG), -1, keepdims=True)
    expo = jnp.where(key_ok, jnp.exp(scores - top), 0.0)
    total = jnp.sum(expo, -1, keepdims=True) + land_query[..., None]
    return (expo / total).astype(jnp.bfloat16)


def window_attend(query, keys, values, flags):
    rows, cols, width = query.shape
    nh = HEADS
    hd = width // nh
    scale = hd ** (-0.5)

    def tiles(a):
        a = a.reshape(rows // 8, 8, cols // 8, 8, nh, hd).transpose(0, 2, 4, 1, 3, 5)
        return a.reshape(rows // 8, cols // 8, nh, 64, hd)

    marks = (
        flags.reshape(rows // 8, 8, cols // 8, 8)
        .transpose(0, 2, 1, 3)
        .reshape(rows // 8, cols // 8, 64)
    )
    key_ok = (marks > 0)[:, :, None, None, :]
    land_query = (marks <= 0).astype(jnp.float32)[:, :, None, :]
    scores = (
        jnp.einsum(
            "abhqd,abhkd->abhqk", tiles(query), tiles(keys), preferred_element_type=jnp.float32
        )
        * scale
    )
    probs = masked_softmax(scores, key_ok, land_query)
    outs = jnp.einsum(
        "abhqk,abhkd->abhqd", probs, tiles(values), preferred_element_type=jnp.float32
    )
    outs = outs * (1.0 - land_query)[..., None]
    outs = outs.astype(jnp.bfloat16).reshape(rows // 8, cols // 8, nh, 8, 8, hd)
    return outs.transpose(0, 3, 1, 4, 2, 5).reshape(rows, cols, width)


def row_attend(query, keys, values, flags):
    rows, length, width = query.shape
    nh = HEADS
    hd = width // nh
    scale = hd ** (-0.5)
    key_ok = (flags > 0)[:, None, :]
    land_query = (flags <= 0).astype(jnp.float32)

    def head(index):
        qh = lax.dynamic_slice_in_dim(query, index * hd, hd, 2)
        kh = lax.dynamic_slice_in_dim(keys, index * hd, hd, 2)
        vh = lax.dynamic_slice_in_dim(values, index * hd, hd, 2)
        scores = jnp.einsum("rqd,rkd->rqk", qh, kh, preferred_element_type=jnp.float32) * scale
        probs = masked_softmax(scores, key_ok, land_query)
        return jnp.einsum("rqk,rkd->rqd", probs, vh, preferred_element_type=jnp.float32)

    outs = lax.map(head, jnp.arange(nh, dtype=jnp.int32))
    outs = outs.transpose(1, 2, 0, 3).reshape(rows, length, width)
    return (outs * (1.0 - land_query)[..., None]).astype(jnp.bfloat16)


def attend_columns(columns, marks, w_query1, w_key1, w_value1):
    return window_attend(
        project(columns, w_query1), project(columns, w_key1), project(columns, w_value1), marks
    )


def spread_rows(
    fields, ocean, w_query1, w_key1, w_value1, w_out1, w_query2, w_key2, w_value2, w_out2
):
    rows, cols, width = fields.shape
    normed = norm_rows(fields)
    marks = ocean.astype(jnp.bfloat16)
    edge_feats, edge_marks = passed_along((normed[:, cols - 4 :], marks[:, cols - 4 :]), "lon", 1)
    columns = jnp.concatenate([edge_feats, normed[:, : cols - 4]], 1)
    column_marks = jnp.concatenate([edge_marks, marks[:, : cols - 4]], 1)
    extended = attend_columns(columns, column_marks, w_query1, w_key1, w_value1)
    returned = passed_along(extended[:, :4], "lon", -1)
    o1 = jnp.concatenate([extended[:, 4:], returned], 1)
    y1 = (
        fields.astype(jnp.float32) + jnp.dot(o1, w_out1, preferred_element_type=jnp.float32)
    ).astype(jnp.bfloat16)
    h2 = norm_rows(y1)
    q2 = project(h2, w_query2)
    k2 = project(h2, w_key2)
    v2 = project(h2, w_value2)
    row_q, row_k, row_v, row_marks = (
        lax.all_to_all(q2, "lon", split_axis=0, concat_axis=1, tiled=True),
        lax.all_to_all(k2, "lon", split_axis=0, concat_axis=1, tiled=True),
        lax.all_to_all(v2, "lon", split_axis=0, concat_axis=1, tiled=True),
        lax.all_to_all(marks, "lon", split_axis=0, concat_axis=1, tiled=True),
    )
    row_out = row_attend(row_q, row_k, row_v, row_marks)
    o2 = lax.all_to_all(row_out, "lon", split_axis=1, concat_axis=0, tiled=True)
    return (
        y1.astype(jnp.float32) + jnp.dot(o2, w_out2, preferred_element_type=jnp.float32)
    ).astype(jnp.bfloat16)


def normed_f32(a):
    mean = jnp.mean(a, -1, keepdims=True)
    centred = a - mean
    var = jnp.mean(centred * centred, -1, keepdims=True)
    return (centred * lax.rsqrt(var + EPS)).astype(jnp.bfloat16)


def dot_f32(a, b):
    return jnp.dot(a, b, preferred_element_type=jnp.float32)


def low_columns(shape, axis):
    return lax.broadcasted_iota(jnp.int32, shape, axis) % 8 < 4


def attend(queries, keys, values, marks):
    n = marks.shape[0]
    low = lax.broadcasted_iota(jnp.int32, (n, 128), 1) < 64
    land = 1.0 - marks
    bias = jnp.concatenate([land * NEG] * (2 * n // 128), 1)
    scores = []
    for q, k in zip(queries, keys):
        zero = jnp.zeros_like(q)
        both = jnp.concatenate([jnp.where(low, q, zero), jnp.where(low, zero, q)], 0)
        scores.append(lax.dot_general(k, both, (((1,), (1,)), ((), ())), preferred_element_type=jnp.float32) + bias)
    expos = [jnp.exp(s - jnp.max(s, 0, keepdims=True)).astype(jnp.bfloat16) for s in scores]
    outs = []
    for expo, v in zip(expos, values):
        wide = jnp.concatenate([v, jnp.ones_like(v)], 1)
        sums = lax.dot_general(expo, wide, (((0,), (0,)), ((), ())), preferred_element_type=jnp.float32)
        upper = jnp.where(low, sums[:n, :128], sums[n:, :128])
        total = jnp.where(low, sums[:n, 128:], sums[n:, 128:]) + land
        outs.append((upper / total * marks).astype(jnp.bfloat16))
    return outs


ORDER = (4, 5, 6, 7, 1, 2, 3, 0)


def pack_kernel(distances, me_ref, marks_ref, fields_ref, *refs):
    outs, (held, held_marks, sems) = refs[: len(distances)], refs[len(distances) :]
    me = me_ref[0]
    tiles = fields_ref.shape[-1] // 128
    copies = [pltpu.make_async_copy(marks_ref, held_marks, sems.at[len(distances)])]
    for i, d in enumerate(distances):
        there = jnp.bitwise_xor(me, d)
        copies.append(pltpu.make_async_copy(fields_ref.at[pl.ds(there * 8, 8)], held.at[i], sems.at[i]))
    for copy in copies:
        copy.start()
    copies[0].wait()
    marks = held_marks[...].astype(jnp.float32)
    marks = jnp.concatenate([marks, jnp.zeros((16, 128 - marks.shape[1]), jnp.float32)], 1).astype(jnp.bfloat16)
    for i in range(len(distances)):
        copies[i + 1].wait()
        piece = held[i].reshape(128, 128 * tiles)
        for t in range(tiles):
            outs[i][128 * t : 128 * t + 128, :] = piece[:, 128 * t : 128 * t + 128]
        outs[i][128 * tiles :, :] = marks


def pack(distances, me, marks, fields):
    cols, width = fields.shape[1:]
    vmem = pl.BlockSpec(memory_space=pltpu.VMEM)
    anywhere = pl.BlockSpec(memory_space=pl.ANY)
    piece = jax.ShapeDtypeStruct((width + 16, 128), jnp.bfloat16)
    n = len(distances)
    return pl.pallas_call(
        functools.partial(pack_kernel, distances),
        out_shape=(piece,) * n,
        in_specs=[pl.BlockSpec(memory_space=pltpu.SMEM), anywhere, anywhere],
        out_specs=(vmem,) * n,
        scratch_shapes=[
            pltpu.VMEM((n, 8, cols, width), jnp.bfloat16),
            pltpu.VMEM(marks.shape, marks.dtype),
            pltpu.SemaphoreType.DMA((n + 1,)),
        ],
        compiler_params=pltpu.CompilerParams(vmem_limit_bytes=PACK_VMEM),
        cost_estimate=pl.CostEstimate(flops=n * 200000, bytes_accessed=n * 400000, transcendentals=0),
        name="pack",
    )(me, marks, fields)


def ready_kernel(*refs):
    refs[-1][...] = jnp.zeros_like(refs[-1])


def ready(weights):
    vmem = pl.BlockSpec(memory_space=pltpu.VMEM)
    return pl.pallas_call(
        ready_kernel,
        out_shape=jax.ShapeDtypeStruct((8, 128), jnp.float32),
        in_specs=[vmem] * len(weights),
        out_specs=vmem,
        compiler_params=pltpu.CompilerParams(vmem_limit_bytes=16 * 1024 * 1024),
        cost_estimate=pl.CostEstimate(flops=0, bytes_accessed=32 << 20, transcendentals=0),
        name="ready",
    )(*weights)


def unpacked(me, piece):
    tiles = (piece.shape[0] - 16) // 128
    lanes = [piece[128 * t : 128 * t + 128] for t in range(tiles)]
    marks = pltpu.roll(piece[128 * tiles :].astype(jnp.float32), jnp.bitwise_and(128 - 8 * me, 127), 1)
    marks = jnp.concatenate([jnp.broadcast_to(marks[:, r : r + 1], (16, 128)) for r in range(8)], 0)
    whole = jnp.concatenate(lanes + [marks.astype(jnp.bfloat16)], 1).astype(jnp.float32)
    whole = whole.reshape(8, 2, 8, 128 * tiles + 128)
    return whole[:, 0], whole[:, 1]


STAGES = ((7, 6), (4, 4), (5, 6))


def window_kernel(stage, me_ref, *refs):
    pieces = refs[: (4, 2, 2)[stage]]
    refs = refs[len(pieces) :]
    if stage > 0:
        others, refs = refs[:2], refs[2:]
    carried = refs[: (0, 3, 5)[stage]]
    refs = refs[len(carried) :]
    _, wq, wk, wv, wo, wq2, wk2, wv2, y_ref, q2_ref, k2_ref, v2_ref, m_ref = refs[:13]
    refs = refs[13:]
    passed = refs[: (3, 3, 0)[stage]]
    placed, q_s, k_s, v_s, o_s, rows_s = refs[len(passed) :]
    width = wq.shape[0]
    scale = (width // HEADS) ** (-0.5)
    me = me_ref[0]
    upper = jnp.bitwise_and(me, 2) > 0
    low = jnp.bitwise_and(me, len(pieces) - 1)
    for d, piece in enumerate(pieces):
        placed[jnp.bitwise_xor(low, d)] = piece[...] if stage == 0 else jnp.where(me_ref[1] > 0, piece[...], others[d][...])
    columns = [unpacked(me, placed[l]) for l in range(len(pieces))]
    mask = low_columns((8, 8, width + 128), 1)
    full = (64, width + 128)

    def whole_window(l):
        return jnp.where(mask, columns[l][1], columns[l][0]).reshape(full)

    def straddling_window(left, right):
        return jnp.where(mask, right, left).reshape(full)

    def either(if_upper, if_lower):
        return jnp.where(upper, if_upper, if_lower)

    windows = [whole_window(0)]
    for l in range(1, len(pieces)):
        windows += [straddling_window(columns[l - 1][1], columns[l][0]), whole_window(l)]
    first, last = columns[0][0], columns[-1][1]
    if stage < 2:
        passed[0][...] = first.reshape(full)
        passed[1][...] = last.reshape(full)
    edges = [a[...].reshape(8, 8, width + 128) for a in carried[:-1]]
    if stage == 1:
        own_first, own_last = edges
        windows = [straddling_window(either(last, own_last), either(own_first, first))] + windows
    if stage == 2:
        own_first, own_last, second_first, second_last = edges
        windows = (
            [straddling_window(either(last, second_last), either(second_first, first))]
            + windows
            + [straddling_window(either(own_last, last), either(first, own_first))]
        )
    count = len(windows)
    x = jnp.concatenate([w[:, :width] for w in windows], 0)
    marks = [w[:, width:] for w in windows]
    h = normed_f32(x)
    q_s[...] = (dot_f32(h, wq[...]) * scale).astype(jnp.bfloat16)
    k_s[...] = dot_f32(h, wk[...]).astype(jnp.bfloat16)
    v_s[...] = dot_f32(h, wv[...]).astype(jnp.bfloat16)
    for w in range(count):
        here = slice(64 * w, 64 * w + 64)
        outs = attend(*([a[here, lanes] for lanes in PAIRS] for a in (q_s, k_s, v_s)), marks[w])
        for lanes, out in zip(PAIRS, outs):
            o_s[here, lanes] = out
    y = (x + dot_f32(o_s[...], wo[...])).astype(jnp.bfloat16).astype(jnp.float32)
    skip = 0
    if stage > 0:
        skip = 1
        rows_s[:, :8, :] = carried[-1][...]
    for w in range(count):
        for r in range(8):
            at = 64 * w + 8 * r
            to = 8 * (w + skip)
            if stage < 2 and w == count - 1:
                passed[2][r, :, :width] = y[at : at + 8]
                passed[2][r, :, width:] = marks[w][8 * r : 8 * r + 8]
            else:
                rows_s[r, to : to + 8, :width] = y[at : at + 8]
                rows_s[r, to : to + 8, width:] = marks[w][8 * r : 8 * r + 8]
    tokens = rows_s.shape[0] * rows_s.shape[1]
    y = rows_s[:, :, :width].reshape(tokens, width)
    m_ref[...] = rows_s[:, :, width:].astype(jnp.bfloat16)
    y_ref[...] = y.astype(jnp.bfloat16).reshape(y_ref.shape)
    h = normed_f32(y)
    q2_ref[...] = (dot_f32(h, wq2[...]) * scale).astype(jnp.bfloat16).reshape(q2_ref.shape)
    k2_ref[...] = dot_f32(h, wk2[...]).astype(jnp.bfloat16).reshape(k2_ref.shape)
    v2_ref[...] = dot_f32(h, wv2[...]).astype(jnp.bfloat16).reshape(v2_ref.shape)


def window_layer(stage, me, pieces, others, carried, weights):
    width = weights[1].shape[0]
    tokens = 64 * STAGES[stage][0]
    columns = 8 * STAGES[stage][1]
    part = jax.ShapeDtypeStruct((8, columns, width), jnp.bfloat16)
    marks = jax.ShapeDtypeStruct((8, columns, 128), jnp.bfloat16)
    edge = jax.ShapeDtypeStruct((64, width + 128), jnp.float32)
    tail = jax.ShapeDtypeStruct((8, 8, width + 128), jnp.float32)
    outs = (part,) * 4 + (marks,) + ((edge, edge, tail), (edge, edge, tail), ())[stage]
    vmem = pl.BlockSpec(memory_space=pltpu.VMEM)
    work = pltpu.VMEM((tokens, width), jnp.bfloat16)
    inputs = [*pieces, *others, *carried, *weights]
    return pl.pallas_call(
        functools.partial(window_kernel, stage),
        out_shape=outs,
        in_specs=[pl.BlockSpec(memory_space=pltpu.SMEM)] + [vmem] * len(inputs),
        out_specs=(vmem,) * len(outs),
        scratch_shapes=[
            pltpu.VMEM((len(pieces), width + 16, 128), jnp.bfloat16),
            work, work, work, work,
            pltpu.VMEM((8, columns, width + 128), jnp.float32),
        ],
        compiler_params=pltpu.CompilerParams(vmem_limit_bytes=36 * 1024 * 1024),
        cost_estimate=pl.CostEstimate(
            flops=2 * tokens * width * (7 * width + 512), bytes_accessed=16 << 20, transcendentals=tokens * 64 * HEADS
        ),
        name="window_layer",
    )(me, *inputs)


def row_kernel(start, rows, me_ref, *refs):
    parts, wo, refs = (refs[:5], refs[5:10], refs[10:15]), refs[15], refs[16:]
    earlier, refs = (refs[:4], refs[4:]) if start else ((), refs)
    outs, (o_s, placed) = refs[:8], refs[8:]
    width = wo.shape[0]
    length = 128

    def row(i, r, lanes=slice(None)):
        return jnp.concatenate([part[i][start + r, :, lanes] for part in parts], 0)

    for r in range(rows):
        here = slice(length * r, length * r + length)
        heads = attend(*([row(i, r, lanes) for lanes in PAIRS] for i in (1, 2, 3)), row(4, r).astype(jnp.float32))
        for lanes, out in zip(PAIRS, heads):
            o_s[here, lanes] = out
    added = dot_f32(o_s[...], wo[...])
    mask = low_columns((8, width), 0)
    me = me_ref[0]
    upper = jnp.bitwise_and(me, 2) > 0
    for r in range(rows):
        f = row(0, r).astype(jnp.float32) + added[length * r : length * r + length]
        tiles = [f[8 * w : 8 * w + 8] for w in range(16)]
        own, second, third = tiles[:7], tiles[8:11], tiles[12:15]
        own_second, middle, third_own = tiles[7], tiles[11], tiles[15]
        after_own = jnp.where(upper, third_own, own_second)
        before_own = jnp.where(upper, own_second, third_own)
        whole = [before_own, *own, after_own]
        whole += [jnp.where(upper, middle, after_own), *second, jnp.where(upper, before_own, middle)]
        whole += [jnp.where(upper, after_own, middle), *third, jnp.where(upper, middle, before_own)]
        for l in range(8):
            at = 2 * l if l < 4 else (9, 11, 14, 16)[l - 4]
            before, a, after = whole[at : at + 3]
            piece = jnp.concatenate([jnp.where(mask, before, a), jnp.where(mask, a, after)], 0)
            placed[l, r] = piece.astype(jnp.bfloat16)
    for i, d in enumerate(ORDER):
        if d < 4:
            if start:
                outs[i][:start] = earlier[i - 4][...]
            outs[i][start:] = placed[jnp.bitwise_xor(jnp.bitwise_and(me, 3), d)]
        else:
            outs[i][...] = placed[d // 2 * 2 + jnp.bitwise_xor(jnp.bitwise_and(me, 1), d % 2)]


def row_layer(start, rows, me, parts, w_out, earlier):
    width = w_out.shape[0]
    length = 128
    far = jax.ShapeDtypeStruct((rows, 16, width), jnp.bfloat16)
    near = jax.ShapeDtypeStruct((start + rows, 16, width), jnp.bfloat16)
    vmem = pl.BlockSpec(memory_space=pltpu.VMEM)
    inputs = [*parts, w_out, *earlier]
    return pl.pallas_call(
        functools.partial(row_kernel, start, rows),
        out_shape=(far,) * 4 + (near,) * 4,
        in_specs=[pl.BlockSpec(memory_space=pltpu.SMEM)] + [vmem] * len(inputs),
        out_specs=(vmem,) * 8,
        scratch_shapes=[
            pltpu.VMEM((rows * length, width), jnp.bfloat16),
            pltpu.VMEM((8, rows, 16, width), jnp.bfloat16),
        ],
        compiler_params=pltpu.CompilerParams(vmem_limit_bytes=36 * 1024 * 1024),
        cost_estimate=pl.CostEstimate(
            flops=0, bytes_accessed=1 << 16, transcendentals=0
        ),
        name="row_layer",
    )(me, *inputs)


def place_kernel(spots, me_ref, *refs):
    pieces, out_ref, sems = refs[: len(spots)], refs[-2], refs[-1]
    copies = []
    for i, (d, start) in enumerate(spots):
        at = jnp.bitwise_xor(me_ref[0], d) * 8 + start
        copies.append(pltpu.make_async_copy(pieces[i], out_ref.at[pl.ds(at, pieces[i].shape[0])], sems.at[i]))
        copies[-1].start()
    for copy in copies:
        copy.wait()


def place(spots, me, pieces, so_far, shape):
    vmem = pl.BlockSpec(memory_space=pltpu.VMEM)
    hbm = pl.BlockSpec(memory_space=pltpu.HBM)
    n = len(pieces)
    more = () if so_far is None else (so_far,)
    return pl.pallas_call(
        functools.partial(place_kernel, spots),
        out_shape=jax.ShapeDtypeStruct(shape, jnp.bfloat16),
        in_specs=[pl.BlockSpec(memory_space=pltpu.SMEM)] + [vmem] * n + [hbm] * len(more),
        out_specs=hbm,
        scratch_shapes=[pltpu.SemaphoreType.DMA((n,))],
        input_output_aliases={n + 1: 0} if more else {},
        compiler_params=pltpu.CompilerParams(vmem_limit_bytes=8 * 1024 * 1024),
        cost_estimate=pl.CostEstimate(flops=0, bytes_accessed=4 << 20, transcendentals=0),
        name="place",
    )(me, *pieces, *more)


def exchanged(piece, distance):
    count = lax.axis_size("lon")
    return lax.ppermute(piece, "lon", [(s, s ^ distance) for s in range(count)])


def exchanged_of(lat, piece, distance):
    count = lax.axis_size("lon")
    pairs = [(lat * count + s, lat * count + (s ^ distance)) for s in range(count)]
    return lax.ppermute(piece, ("lat", "lon"), pairs)


def gathered_bands(
    fields, ocean, w_query1, w_key1, w_value1, w_out1, w_query2, w_key2, w_value2, w_out2
):
    me = jnp.stack([lax.axis_index("lon"), lax.axis_index("lat")]).astype(jnp.int32)
    weights = (w_query1, w_key1, w_value1, w_out1, w_query2, w_key2, w_value2)
    weights = (ready(weights), *weights)

    packed = dict(zip(ORDER, pack(ORDER, me, ocean.T, fields)))
    got = {0: packed[0], 2: exchanged(packed[2], 2), 3: exchanged(packed[3], 3)}
    last, got[2] = lax.optimization_barrier((packed[7], got[2]))
    packed[1], got[3] = lax.optimization_barrier((packed[1], got[3]))
    got[1] = exchanged(packed[1], 1)
    far = {d: exchanged_of(1, last if d == 7 else packed[d], d) for d in ORDER[:4]}
    far_other = {}
    for d in ORDER[:4]:
        packed[d], far[d] = lax.optimization_barrier((packed[d], far[d]))
        far_other[d] = exchanged_of(0, packed[d], d)
    own = window_layer(0, me, [got[d] for d in range(4)], (), (), weights)
    second = window_layer(1, me, [far[4], far[5]], [far_other[4], far_other[5]], own[5:], weights)
    third = window_layer(2, me, [far[6], far[7]], [far_other[6], far_other[7]], (*own[5:7], *second[5:]), weights)
    parts = (*own[:5], *second[:5], *third)
    first = row_layer(0, ROWS_FIRST, me, parts, w_out2, ())
    last = row_layer(ROWS_FIRST, 8 - ROWS_FIRST, me, parts, w_out2, first[4:])
    far = [exchanged(piece, d) for d, piece in zip(ORDER[:4], first)]
    last = list(last)
    for i in range(4):
        last[i], last[4 + i], far[i] = lax.optimization_barrier((last[i], last[4 + i], far[i]))
    far_last = [exchanged(piece, d) for d, piece in zip(ORDER[:4], last)]
    near = [exchanged(piece, d) if d else piece for d, piece in zip(ORDER[4:], last[4:])]
    out = place([(d, 0) for d in ORDER], me, far + near, None, fields.shape)
    return place([(d, ROWS_FIRST) for d in ORDER[:4]], me, far_last, out, fields.shape)


def on_device(fields, *rest):
    rows, cols, width = fields.shape
    if lax.axis_size("lon") == 8 and rows == 64 and cols == 16 and width == 64 * HEADS:
        return gathered_bands(fields, *rest)
    return spread_rows(fields, *rest)


def solution(mesh):
    in_specs = (
        P(("grp", "lat"), "lon", None),
        P(("grp", "lat"), "lon"),
        P(),
        P(),
        P(),
        P(),
        P(),
        P(),
        P(),
        P(),
    )
    out_specs = P(("grp", "lat"), "lon", None)
    return jax.shard_map(
        on_device, mesh=mesh, in_specs=in_specs, out_specs=out_specs, check_vma=False
    )
```

```python
import functools

import jax
import jax.numpy as jnp
from jax import lax
from jax.experimental import pallas as pl
from jax.experimental.pallas import tpu as pltpu
from jax.sharding import PartitionSpec as P

HEADS = 12


EPS = 1e-05
NEG = -1e30

PACK_VMEM = 52 * 1024 * 1024

PAIRS = [slice(128 * p, 128 * p + 128) for p in range(HEADS // 2)]


def passed_along(value, axis, steps):
    count = lax.axis_size(axis)
    pairs = [(source, (source + steps) % count) for source in range(count)]
    return lax.ppermute(value, axis, pairs)


def norm_rows(a):
    af = a.astype(jnp.float32)
    mean = jnp.mean(af, -1, keepdims=True)
    var = jnp.mean((af - mean) * (af - mean), -1, keepdims=True)
    return ((af - mean) * lax.rsqrt(var + EPS)).astype(jnp.bfloat16)


def project(h, weight):
    return jnp.dot(h, weight, preferred_element_type=jnp.float32).astype(jnp.bfloat16)


def masked_softmax(scores, key_ok, land_query):
    top = jnp.max(jnp.where(key_ok, scores, NEG), -1, keepdims=True)
    expo = jnp.where(key_ok, jnp.exp(scores - top), 0.0)
    total = jnp.sum(expo, -1, keepdims=True) + land_query[..., None]
    return (expo / total).astype(jnp.bfloat16)


def window_attend(query, keys, values, flags):
    rows, cols, width = query.shape
    nh = HEADS
    hd = width // nh
    scale = hd ** (-0.5)

    def tiles(a):
        a = a.reshape(rows // 8, 8, cols // 8, 8, nh, hd).transpose(0, 2, 4, 1, 3, 5)
        return a.reshape(rows // 8, cols // 8, nh, 64, hd)

    marks = (
        flags.reshape(rows // 8, 8, cols // 8, 8)
        .transpose(0, 2, 1, 3)
        .reshape(rows // 8, cols // 8, 64)
    )
    key_ok = (marks > 0)[:, :, None, None, :]
    land_query = (marks <= 0).astype(jnp.float32)[:, :, None, :]
    scores = (
        jnp.einsum(
            "abhqd,abhkd->abhqk", tiles(query), tiles(keys), preferred_element_type=jnp.float32
        )
        * scale
    )
    probs = masked_softmax(scores, key_ok, land_query)
    outs = jnp.einsum(
        "abhqk,abhkd->abhqd", probs, tiles(values), preferred_element_type=jnp.float32
    )
    outs = outs * (1.0 - land_query)[..., None]
    outs = outs.astype(jnp.bfloat16).reshape(rows // 8, cols // 8, nh, 8, 8, hd)
    return outs.transpose(0, 3, 1, 4, 2, 5).reshape(rows, cols, width)


def row_attend(query, keys, values, flags):
    rows, length, width = query.shape
    nh = HEADS
    hd = width // nh
    scale = hd ** (-0.5)
    key_ok = (flags > 0)[:, None, :]
    land_query = (flags <= 0).astype(jnp.float32)

    def head(index):
        qh = lax.dynamic_slice_in_dim(query, index * hd, hd, 2)
        kh = lax.dynamic_slice_in_dim(keys, index * hd, hd, 2)
        vh = lax.dynamic_slice_in_dim(values, index * hd, hd, 2)
        scores = jnp.einsum("rqd,rkd->rqk", qh, kh, preferred_element_type=jnp.float32) * scale
        probs = masked_softmax(scores, key_ok, land_query)
        return jnp.einsum("rqk,rkd->rqd", probs, vh, preferred_element_type=jnp.float32)

    outs = lax.map(head, jnp.arange(nh, dtype=jnp.int32))
    outs = outs.transpose(1, 2, 0, 3).reshape(rows, length, width)
    return (outs * (1.0 - land_query)[..., None]).astype(jnp.bfloat16)


def attend_columns(columns, marks, w_query1, w_key1, w_value1):
    return window_attend(
        project(columns, w_query1), project(columns, w_key1), project(columns, w_value1), marks
    )


def spread_rows(
    fields, ocean, w_query1, w_key1, w_value1, w_out1, w_query2, w_key2, w_value2, w_out2
):
    rows, cols, width = fields.shape
    normed = norm_rows(fields)
    marks = ocean.astype(jnp.bfloat16)
    edge_feats, edge_marks = passed_along((normed[:, cols - 4 :], marks[:, cols - 4 :]), "lon", 1)
    columns = jnp.concatenate([edge_feats, normed[:, : cols - 4]], 1)
    column_marks = jnp.concatenate([edge_marks, marks[:, : cols - 4]], 1)
    extended = attend_columns(columns, column_marks, w_query1, w_key1, w_value1)
    returned = passed_along(extended[:, :4], "lon", -1)
    o1 = jnp.concatenate([extended[:, 4:], returned], 1)
    y1 = (
        fields.astype(jnp.float32) + jnp.dot(o1, w_out1, preferred_element_type=jnp.float32)
    ).astype(jnp.bfloat16)
    h2 = norm_rows(y1)
    q2 = project(h2, w_query2)
    k2 = project(h2, w_key2)
    v2 = project(h2, w_value2)
    row_q, row_k, row_v, row_marks = (
        lax.all_to_all(q2, "lon", split_axis=0, concat_axis=1, tiled=True),
        lax.all_to_all(k2, "lon", split_axis=0, concat_axis=1, tiled=True),
        lax.all_to_all(v2, "lon", split_axis=0, concat_axis=1, tiled=True),
        lax.all_to_all(marks, "lon", split_axis=0, concat_axis=1, tiled=True),
    )
    row_out = row_attend(row_q, row_k, row_v, row_marks)
    o2 = lax.all_to_all(row_out, "lon", split_axis=1, concat_axis=0, tiled=True)
    return (
        y1.astype(jnp.float32) + jnp.dot(o2, w_out2, preferred_element_type=jnp.float32)
    ).astype(jnp.bfloat16)


def normed_f32(a):
    mean = jnp.mean(a, -1, keepdims=True)
    centred = a - mean
    var = jnp.mean(centred * centred, -1, keepdims=True)
    return (centred * lax.rsqrt(var + EPS)).astype(jnp.bfloat16)


def dot_f32(a, b):
    return jnp.dot(a, b, preferred_element_type=jnp.float32)


def low_columns(shape, axis):
    return lax.broadcasted_iota(jnp.int32, shape, axis) % 8 < 4


def attend(queries, keys, values, marks):
    n = marks.shape[0]
    low = lax.broadcasted_iota(jnp.int32, (n, 128), 1) < 64
    land = 1.0 - marks
    bias = jnp.concatenate([land * NEG] * (2 * n // 128), 1)
    scores = []
    for q, k in zip(queries, keys):
        zero = jnp.zeros_like(q)
        both = jnp.concatenate([jnp.where(low, q, zero), jnp.where(low, zero, q)], 0)
        scores.append(lax.dot_general(k, both, (((1,), (1,)), ((), ())), preferred_element_type=jnp.float32) + bias)
    expos = [jnp.exp(s - jnp.max(s, 0, keepdims=True)).astype(jnp.bfloat16) for s in scores]
    outs = []
    for expo, v in zip(expos, values):
        wide = jnp.concatenate([v, jnp.ones_like(v)], 1)
        sums = lax.dot_general(expo, wide, (((0,), (0,)), ((), ())), preferred_element_type=jnp.float32)
        upper = jnp.where(low, sums[:n, :128], sums[n:, :128])
        total = jnp.where(low, sums[:n, 128:], sums[n:, 128:]) + land
        outs.append((upper / total * marks).astype(jnp.bfloat16))
    return outs


ORDER = (4, 5, 6, 7, 1, 2, 3, 0)


def pack_kernel(distances, me_ref, marks_ref, fields_ref, *refs):
    outs, (held, held_marks, sems) = refs[: len(distances)], refs[len(distances) :]
    me = me_ref[0]
    tiles = fields_ref.shape[-1] // 128
    copies = [pltpu.make_async_copy(marks_ref, held_marks, sems.at[len(distances)])]
    for i, d in enumerate(distances):
        there = jnp.bitwise_xor(me, d)
        copies.append(pltpu.make_async_copy(fields_ref.at[pl.ds(there * 8, 8)], held.at[i], sems.at[i]))
    for copy in copies:
        copy.start()
    copies[0].wait()
    marks = held_marks[...].astype(jnp.float32)
    marks = jnp.concatenate([marks, jnp.zeros((16, 128 - marks.shape[1]), jnp.float32)], 1).astype(jnp.bfloat16)
    for i in range(len(distances)):
        copies[i + 1].wait()
        piece = held[i].reshape(128, 128 * tiles)
        for t in range(tiles):
            outs[i][128 * t : 128 * t + 128, :] = piece[:, 128 * t : 128 * t + 128]
        outs[i][128 * tiles :, :] = marks


def pack(distances, me, marks, fields):
    cols, width = fields.shape[1:]
    vmem = pl.BlockSpec(memory_space=pltpu.VMEM)
    anywhere = pl.BlockSpec(memory_space=pl.ANY)
    piece = jax.ShapeDtypeStruct((width + 16, 128), jnp.bfloat16)
    n = len(distances)
    return pl.pallas_call(
        functools.partial(pack_kernel, distances),
        out_shape=(piece,) * n,
        in_specs=[pl.BlockSpec(memory_space=pltpu.SMEM), anywhere, anywhere],
        out_specs=(vmem,) * n,
        scratch_shapes=[
            pltpu.VMEM((n, 8, cols, width), jnp.bfloat16),
            pltpu.VMEM(marks.shape, marks.dtype),
            pltpu.SemaphoreType.DMA((n + 1,)),
        ],
        compiler_params=pltpu.CompilerParams(vmem_limit_bytes=PACK_VMEM),
        cost_estimate=pl.CostEstimate(flops=n * 200000, bytes_accessed=n * 400000, transcendentals=0),
        name="pack",
    )(me, marks, fields)


def ready_kernel(*refs):
    refs[-1][...] = jnp.zeros_like(refs[-1])


def ready(weights):
    vmem = pl.BlockSpec(memory_space=pltpu.VMEM)
    return pl.pallas_call(
        ready_kernel,
        out_shape=jax.ShapeDtypeStruct((8, 128), jnp.float32),
        in_specs=[vmem] * len(weights),
        out_specs=vmem,
        compiler_params=pltpu.CompilerParams(vmem_limit_bytes=16 * 1024 * 1024),
        cost_estimate=pl.CostEstimate(flops=0, bytes_accessed=32 << 20, transcendentals=0),
        name="ready",
    )(*weights)


def unpacked(me, piece):
    tiles = (piece.shape[0] - 16) // 128
    lanes = [piece[128 * t : 128 * t + 128] for t in range(tiles)]
    marks = pltpu.roll(piece[128 * tiles :].astype(jnp.float32), jnp.bitwise_and(128 - 8 * me, 127), 1)
    marks = jnp.concatenate([jnp.broadcast_to(marks[:, r : r + 1], (16, 128)) for r in range(8)], 0)
    whole = jnp.concatenate(lanes + [marks.astype(jnp.bfloat16)], 1).astype(jnp.float32)
    whole = whole.reshape(8, 2, 8, 128 * tiles + 128)
    return whole[:, 0], whole[:, 1]


STAGES = ((7, 6), (4, 4), (2, 2), (3, 4))

ROWS_FIRST = 4


def window_kernel(stage, me_ref, *refs):
    pieces = refs[: (4, 2, 1, 1)[stage]]
    refs = refs[len(pieces) :]
    carried = refs[: (0, 3, 5, 7)[stage]]
    refs = refs[len(carried) :]
    _, wq, wk, wv, wo, wq2, wk2, wv2, y_ref, q2_ref, k2_ref, v2_ref, m_ref = refs[:13]
    refs = refs[13:]
    passed = refs[: 3 if stage < 3 else 0]
    placed, q_s, k_s, v_s, o_s, rows_s = refs[len(passed) :]
    width = wq.shape[0]
    scale = (width // HEADS) ** (-0.5)
    me = me_ref[0]
    upper = jnp.bitwise_and(me, 2) > 0
    odd = jnp.bitwise_and(me, 1) > 0
    low = jnp.bitwise_and(me, len(pieces) - 1)
    for d, piece in enumerate(pieces):
        placed[jnp.bitwise_xor(low, d)] = piece[...]
    columns = [unpacked(me, placed[l]) for l in range(len(pieces))]
    mask = low_columns((8, 8, width + 128), 1)
    full = (64, width + 128)

    def whole_window(l):
        return jnp.where(mask, columns[l][1], columns[l][0]).reshape(full)

    def straddling_window(left, right):
        return jnp.where(mask, right, left).reshape(full)

    def either(if_upper, if_lower):
        return jnp.where(upper, if_upper, if_lower)

    windows = [whole_window(0)]
    for l in range(1, len(pieces)):
        windows += [straddling_window(columns[l - 1][1], columns[l][0]), whole_window(l)]
    first, last = columns[0][0], columns[-1][1]
    if stage < 3:
        passed[0][...] = first.reshape(full)
        passed[1][...] = last.reshape(full)
    edges = [a[...].reshape(8, 8, width + 128) for a in carried[:-1]]
    if stage == 1:
        own_first, own_last = edges
        windows = [straddling_window(either(last, own_last), either(own_first, first))] + windows
    if stage >= 2:
        own_first, own_last, second_first, second_last = edges[:4]
        before, after = either(own_last, second_last), either(second_first, own_first)
    if stage == 2:
        windows.append(straddling_window(jnp.where(odd, last, before), jnp.where(odd, after, first)))
    if stage == 3:
        one_first, one_last = edges[4:]
        windows.append(straddling_window(jnp.where(odd, last, one_last), jnp.where(odd, one_first, first)))
        windows.append(straddling_window(jnp.where(odd, before, last), jnp.where(odd, first, after)))
    count = len(windows)
    x = jnp.concatenate([w[:, :width] for w in windows], 0)
    marks = [w[:, width:] for w in windows]
    h = normed_f32(x)
    q_s[...] = (dot_f32(h, wq[...]) * scale).astype(jnp.bfloat16)
    k_s[...] = dot_f32(h, wk[...]).astype(jnp.bfloat16)
    v_s[...] = dot_f32(h, wv[...]).astype(jnp.bfloat16)
    for w in range(count):
        here = slice(64 * w, 64 * w + 64)
        outs = attend(*([a[here, lanes] for lanes in PAIRS] for a in (q_s, k_s, v_s)), marks[w])
        for lanes, out in zip(PAIRS, outs):
            o_s[here, lanes] = out
    y = (x + dot_f32(o_s[...], wo[...])).astype(jnp.bfloat16).astype(jnp.float32)
    skip = 0
    if stage > 0:
        skip = 1
        rows_s[:, :8, :] = carried[-1][...]
    for w in range(count):
        for r in range(8):
            at = 64 * w + 8 * r
            to = 8 * (w + skip)
            if stage < 3 and w == count - 1:
                passed[2][r, :, :width] = y[at : at + 8]
                passed[2][r, :, width:] = marks[w][8 * r : 8 * r + 8]
            else:
                rows_s[r, to : to + 8, :width] = y[at : at + 8]
                rows_s[r, to : to + 8, width:] = marks[w][8 * r : 8 * r + 8]
    m_ref[...] = rows_s[:, :, width:].astype(jnp.bfloat16)
    y_ref[...] = rows_s[:, :, :width].astype(jnp.bfloat16)
    rows = q2_ref.shape[0]
    h = normed_f32(rows_s[:rows, :, :width].reshape(rows * rows_s.shape[1], width))
    q2_ref[...] = (dot_f32(h, wq2[...]) * scale).astype(jnp.bfloat16).reshape(q2_ref.shape)
    k2_ref[...] = dot_f32(h, wk2[...]).astype(jnp.bfloat16).reshape(k2_ref.shape)
    v2_ref[...] = dot_f32(h, wv2[...]).astype(jnp.bfloat16).reshape(v2_ref.shape)


def window_layer(stage, me, pieces, carried, weights):
    width = weights[1].shape[0]
    tokens = 64 * STAGES[stage][0]
    columns = 8 * STAGES[stage][1]
    part = jax.ShapeDtypeStruct((8, columns, width), jnp.bfloat16)
    marks = jax.ShapeDtypeStruct((8, columns, 128), jnp.bfloat16)
    edge = jax.ShapeDtypeStruct((64, width + 128), jnp.float32)
    tail = jax.ShapeDtypeStruct((8, 8, width + 128), jnp.float32)
    projected = part if stage < 3 else jax.ShapeDtypeStruct((ROWS_FIRST, columns, width), jnp.bfloat16)
    outs = (part, projected, projected, projected, marks) + ((edge, edge, tail) if stage < 3 else ())
    vmem = pl.BlockSpec(memory_space=pltpu.VMEM)
    work = pltpu.VMEM((tokens, width), jnp.bfloat16)
    inputs = [*pieces, *carried, *weights]
    return pl.pallas_call(
        functools.partial(window_kernel, stage),
        out_shape=outs,
        in_specs=[pl.BlockSpec(memory_space=pltpu.SMEM)] + [vmem] * len(inputs),
        out_specs=(vmem,) * len(outs),
        scratch_shapes=[
            pltpu.VMEM((len(pieces), width + 16, 128), jnp.bfloat16),
            work, work, work, work,
            pltpu.VMEM((8, columns, width + 128), jnp.float32),
        ],
        compiler_params=pltpu.CompilerParams(vmem_limit_bytes=36 * 1024 * 1024),
        cost_estimate=pl.CostEstimate(
            flops=2 * tokens * width * (7 * width + 512), bytes_accessed=16 << 20, transcendentals=tokens * 64 * HEADS
        ),
        name="window_layer",
    )(me, *inputs)


def row_kernel(start, rows, me_ref, *refs):
    parts, wo, refs = [refs[at : at + 5] for at in range(0, 20, 5)], refs[20], refs[21:]
    width = wo.shape[0]
    length = 128
    earlier = ()
    if start:
        earlier, weights, refs = refs[:4], refs[4:7], refs[7:]
        *refs, q_s, k_s, v_s = refs
        y = parts[3][0][start:].astype(jnp.float32)
        h = normed_f32(y.reshape(rows * y.shape[1], width))
        for to, weight, factor in zip((q_s, k_s, v_s), weights, ((width // HEADS) ** (-0.5), 1.0, 1.0)):
            to[...] = (dot_f32(h, weight[...]) * factor).astype(jnp.bfloat16).reshape(to.shape)
    outs, (o_s, placed) = refs[:8], refs[8:]

    def row(i, r, lanes=slice(None)):
        pieces = [part[i][start + r, :, lanes] for part in parts[:3]]
        if 1 <= i <= 3:
            pieces.append((q_s, k_s, v_s)[i - 1][r, :, lanes] if start else parts[3][i][r, :, lanes])
        else:
            pieces.append(parts[3][i][start + r, :, lanes])
        return jnp.concatenate(pieces, 0)

    for r in range(rows):
        here = slice(length * r, length * r + length)
        heads = attend(*([row(i, r, lanes) for lanes in PAIRS] for i in (1, 2, 3)), row(4, r).astype(jnp.float32))
        for lanes, out in zip(PAIRS, heads):
            o_s[here, lanes] = out
    added = dot_f32(o_s[...], wo[...])
    mask = low_columns((8, width), 0)
    me = me_ref[0]
    upper = jnp.bitwise_and(me, 2) > 0
    odd = jnp.bitwise_and(me, 1) > 0
    same = upper == odd
    for r in range(rows):
        f = row(0, r).astype(jnp.float32) + added[length * r : length * r + length]
        tiles = [f[8 * w : 8 * w + 8] for w in range(16)]
        own, own_second, second = tiles[:7], tiles[7], tiles[8:11]
        third = (jnp.where(odd, tiles[13], tiles[11]), tiles[14], jnp.where(odd, tiles[11], tiles[13]))
        middle, third_own = jnp.where(same, tiles[12], tiles[15]), jnp.where(same, tiles[15], tiles[12])
        after_own = jnp.where(upper, third_own, own_second)
        before_own = jnp.where(upper, own_second, third_own)
        whole = [before_own, *own, after_own]
        whole += [jnp.where(upper, middle, after_own), *second, jnp.where(upper, before_own, middle)]
        whole += [jnp.where(upper, after_own, middle), *third, jnp.where(upper, middle, before_own)]
        for l in range(8):
            at = 2 * l if l < 4 else (9, 11, 14, 16)[l - 4]
            before, a, after = whole[at : at + 3]
            piece = jnp.concatenate([jnp.where(mask, before, a), jnp.where(mask, a, after)], 0)
            placed[l, r] = piece.astype(jnp.bfloat16)
    for i, d in enumerate(ORDER):
        if d < 4:
            if start:
                outs[i][:start] = earlier[i - 4][...]
            outs[i][start:] = placed[jnp.bitwise_xor(jnp.bitwise_and(me, 3), d)]
        else:
            outs[i][...] = placed[d // 2 * 2 + jnp.bitwise_xor(jnp.bitwise_and(me, 1), d % 2)]


def row_layer(start, rows, me, parts, w_out, earlier):
    width = w_out.shape[0]
    length = 128
    far = jax.ShapeDtypeStruct((rows, 16, width), jnp.bfloat16)
    near = jax.ShapeDtypeStruct((start + rows, 16, width), jnp.bfloat16)
    vmem = pl.BlockSpec(memory_space=pltpu.VMEM)
    inputs = [*parts, w_out, *earlier]
    rest = parts[15].shape[1]
    work = pltpu.VMEM((rows, rest, width), jnp.bfloat16)
    return pl.pallas_call(
        functools.partial(row_kernel, start, rows),
        out_shape=(far,) * 4 + (near,) * 4,
        in_specs=[pl.BlockSpec(memory_space=pltpu.SMEM)] + [vmem] * len(inputs),
        out_specs=(vmem,) * 8,
        scratch_shapes=[
            pltpu.VMEM((rows * length, width), jnp.bfloat16),
            pltpu.VMEM((8, rows, 16, width), jnp.bfloat16),
        ]
        + [work] * (3 if start else 0),
        compiler_params=pltpu.CompilerParams(vmem_limit_bytes=36 * 1024 * 1024),
        cost_estimate=pl.CostEstimate(
            flops=0, bytes_accessed=1 << 16, transcendentals=0
        ),
        name="row_layer",
    )(me, *inputs)


def place_kernel(spots, me_ref, *refs):
    pieces, out_ref, sems = refs[: len(spots)], refs[-2], refs[-1]
    copies = []
    for i, (d, start) in enumerate(spots):
        at = jnp.bitwise_xor(me_ref[0], d) * 8 + start
        copies.append(pltpu.make_async_copy(pieces[i], out_ref.at[pl.ds(at, pieces[i].shape[0])], sems.at[i]))
        copies[-1].start()
    for copy in copies:
        copy.wait()


def place(spots, me, pieces, so_far, shape):
    vmem = pl.BlockSpec(memory_space=pltpu.VMEM)
    hbm = pl.BlockSpec(memory_space=pltpu.HBM)
    n = len(pieces)
    more = () if so_far is None else (so_far,)
    return pl.pallas_call(
        functools.partial(place_kernel, spots),
        out_shape=jax.ShapeDtypeStruct(shape, jnp.bfloat16),
        in_specs=[pl.BlockSpec(memory_space=pltpu.SMEM)] + [vmem] * n + [hbm] * len(more),
        out_specs=hbm,
        scratch_shapes=[pltpu.SemaphoreType.DMA((n,))],
        input_output_aliases={n + 1: 0} if more else {},
        compiler_params=pltpu.CompilerParams(vmem_limit_bytes=8 * 1024 * 1024),
        cost_estimate=pl.CostEstimate(flops=0, bytes_accessed=4 << 20, transcendentals=0),
        name="place",
    )(me, *pieces, *more)


def exchanged(piece, distance):
    count = lax.axis_size("lon")
    return lax.ppermute(piece, "lon", [(s, s ^ distance) for s in range(count)])


def gathered_bands(
    fields, ocean, w_query1, w_key1, w_value1, w_out1, w_query2, w_key2, w_value2, w_out2
):
    me = lax.axis_index("lon").astype(jnp.int32).reshape(1)
    weights = (w_query1, w_key1, w_value1, w_out1, w_query2, w_key2, w_value2)
    weights = (ready(weights), *weights)

    packed = dict(zip(ORDER, pack(ORDER, me, ocean.T, fields)))
    got = {d: exchanged(packed[d], d) if d else packed[d] for d in ORDER}
    got[4], *near = lax.optimization_barrier((got[4], got[2], got[3], got[1]))
    got[2], got[3], got[1] = near
    own = window_layer(0, me, [got[d] for d in range(4)], (), weights)
    second = window_layer(1, me, [got[4], got[5]], own[5:], weights)
    edges = (*own[5:7], *second[5:7])
    third = window_layer(2, me, [got[6]], (*edges, second[7]), weights)
    fourth = window_layer(3, me, [got[7]], (*edges, *third[5:]), weights)
    parts = (*own[:5], *second[:5], *third[:5], *fourth)
    first = row_layer(0, ROWS_FIRST, me, parts, w_out2, ())
    last = row_layer(ROWS_FIRST, 8 - ROWS_FIRST, me, parts, w_out2, (*first[4:], w_query2, w_key2, w_value2))
    far = [exchanged(piece, d) for d, piece in zip(ORDER[:4], first)]
    last = list(last)
    for i in range(4):
        last[i], last[4 + i], far[i] = lax.optimization_barrier((last[i], last[4 + i], far[i]))
    far_last = [exchanged(piece, d) for d, piece in zip(ORDER[:4], last)]
    near = [exchanged(piece, d) if d else piece for d, piece in zip(ORDER[4:], last[4:])]
    out = place([(d, 0) for d in ORDER], me, far + near, None, fields.shape)
    return place([(d, ROWS_FIRST) for d in ORDER[:4]], me, far_last, out, fields.shape)


def on_device(fields, *rest):
    rows, cols, width = fields.shape
    if lax.axis_size("lon") == 8 and rows == 64 and cols == 16 and width == 64 * HEADS:
        return gathered_bands(fields, *rest)
    return spread_rows(fields, *rest)


def solution(mesh):
    in_specs = (
        P(("grp", "lat"), "lon", None),
        P(("grp", "lat"), "lon"),
        P(),
        P(),
        P(),
        P(),
        P(),
        P(),
        P(),
        P(),
    )
    out_specs = P(("grp", "lat"), "lon", None)
    return jax.shard_map(
        on_device, mesh=mesh, in_specs=in_specs, out_specs=out_specs, check_vma=False
    )
```

```python
import functools

import jax
import jax.numpy as jnp
from jax import lax
from jax.experimental import pallas as pl
from jax.experimental.pallas import tpu as pltpu
from jax.sharding import PartitionSpec as P

HEADS = 12


EPS = 1e-05
NEG = -1e30

PACK_VMEM = 52 * 1024 * 1024

PAIRS = [slice(128 * p, 128 * p + 128) for p in range(HEADS // 2)]


def passed_along(value, axis, steps):
    count = lax.axis_size(axis)
    pairs = [(source, (source + steps) % count) for source in range(count)]
    return lax.ppermute(value, axis, pairs)


def norm_rows(a):
    af = a.astype(jnp.float32)
    mean = jnp.mean(af, -1, keepdims=True)
    var = jnp.mean((af - mean) * (af - mean), -1, keepdims=True)
    return ((af - mean) * lax.rsqrt(var + EPS)).astype(jnp.bfloat16)


def project(h, weight):
    return jnp.dot(h, weight, preferred_element_type=jnp.float32).astype(jnp.bfloat16)


def masked_softmax(scores, key_ok, land_query):
    top = jnp.max(jnp.where(key_ok, scores, NEG), -1, keepdims=True)
    expo = jnp.where(key_ok, jnp.exp(scores - top), 0.0)
    total = jnp.sum(expo, -1, keepdims=True) + land_query[..., None]
    return (expo / total).astype(jnp.bfloat16)


def window_attend(query, keys, values, flags):
    rows, cols, width = query.shape
    nh = HEADS
    hd = width // nh
    scale = hd ** (-0.5)

    def tiles(a):
        a = a.reshape(rows // 8, 8, cols // 8, 8, nh, hd).transpose(0, 2, 4, 1, 3, 5)
        return a.reshape(rows // 8, cols // 8, nh, 64, hd)

    marks = (
        flags.reshape(rows // 8, 8, cols // 8, 8)
        .transpose(0, 2, 1, 3)
        .reshape(rows // 8, cols // 8, 64)
    )
    key_ok = (marks > 0)[:, :, None, None, :]
    land_query = (marks <= 0).astype(jnp.float32)[:, :, None, :]
    scores = (
        jnp.einsum(
            "abhqd,abhkd->abhqk", tiles(query), tiles(keys), preferred_element_type=jnp.float32
        )
        * scale
    )
    probs = masked_softmax(scores, key_ok, land_query)
    outs = jnp.einsum(
        "abhqk,abhkd->abhqd", probs, tiles(values), preferred_element_type=jnp.float32
    )
    outs = outs * (1.0 - land_query)[..., None]
    outs = outs.astype(jnp.bfloat16).reshape(rows // 8, cols // 8, nh, 8, 8, hd)
    return outs.transpose(0, 3, 1, 4, 2, 5).reshape(rows, cols, width)


def row_attend(query, keys, values, flags):
    rows, length, width = query.shape
    nh = HEADS
    hd = width // nh
    scale = hd ** (-0.5)
    key_ok = (flags > 0)[:, None, :]
    land_query = (flags <= 0).astype(jnp.float32)

    def head(index):
        qh = lax.dynamic_slice_in_dim(query, index * hd, hd, 2)
        kh = lax.dynamic_slice_in_dim(keys, index * hd, hd, 2)
        vh = lax.dynamic_slice_in_dim(values, index * hd, hd, 2)
        scores = jnp.einsum("rqd,rkd->rqk", qh, kh, preferred_element_type=jnp.float32) * scale
        probs = masked_softmax(scores, key_ok, land_query)
        return jnp.einsum("rqk,rkd->rqd", probs, vh, preferred_element_type=jnp.float32)

    outs = lax.map(head, jnp.arange(nh, dtype=jnp.int32))
    outs = outs.transpose(1, 2, 0, 3).reshape(rows, length, width)
    return (outs * (1.0 - land_query)[..., None]).astype(jnp.bfloat16)


def attend_columns(columns, marks, w_query1, w_key1, w_value1):
    return window_attend(
        project(columns, w_query1), project(columns, w_key1), project(columns, w_value1), marks
    )


def spread_rows(
    fields, ocean, w_query1, w_key1, w_value1, w_out1, w_query2, w_key2, w_value2, w_out2
):
    rows, cols, width = fields.shape
    normed = norm_rows(fields)
    marks = ocean.astype(jnp.bfloat16)
    edge_feats, edge_marks = passed_along((normed[:, cols - 4 :], marks[:, cols - 4 :]), "lon", 1)
    columns = jnp.concatenate([edge_feats, normed[:, : cols - 4]], 1)
    column_marks = jnp.concatenate([edge_marks, marks[:, : cols - 4]], 1)
    extended = attend_columns(columns, column_marks, w_query1, w_key1, w_value1)
    returned = passed_along(extended[:, :4], "lon", -1)
    o1 = jnp.concatenate([extended[:, 4:], returned], 1)
    y1 = (
        fields.astype(jnp.float32) + jnp.dot(o1, w_out1, preferred_element_type=jnp.float32)
    ).astype(jnp.bfloat16)
    h2 = norm_rows(y1)
    q2 = project(h2, w_query2)
    k2 = project(h2, w_key2)
    v2 = project(h2, w_value2)
    row_q, row_k, row_v, row_marks = (
        lax.all_to_all(q2, "lon", split_axis=0, concat_axis=1, tiled=True),
        lax.all_to_all(k2, "lon", split_axis=0, concat_axis=1, tiled=True),
        lax.all_to_all(v2, "lon", split_axis=0, concat_axis=1, tiled=True),
        lax.all_to_all(marks, "lon", split_axis=0, concat_axis=1, tiled=True),
    )
    row_out = row_attend(row_q, row_k, row_v, row_marks)
    o2 = lax.all_to_all(row_out, "lon", split_axis=1, concat_axis=0, tiled=True)
    return (
        y1.astype(jnp.float32) + jnp.dot(o2, w_out2, preferred_element_type=jnp.float32)
    ).astype(jnp.bfloat16)


def normed_f32(a):
    mean = jnp.mean(a, -1, keepdims=True)
    centred = a - mean
    var = jnp.mean(centred * centred, -1, keepdims=True)
    return (centred * lax.rsqrt(var + EPS)).astype(jnp.bfloat16)


def dot_f32(a, b):
    return jnp.dot(a, b, preferred_element_type=jnp.float32)


def low_columns(shape, axis):
    return lax.broadcasted_iota(jnp.int32, shape, axis) % 8 < 4


def attend(queries, keys, values, marks):
    n = marks.shape[0]
    low = lax.broadcasted_iota(jnp.int32, (n, 128), 1) < 64
    land = 1.0 - marks
    bias = jnp.concatenate([land * NEG] * (2 * n // 128), 1)
    scores = []
    for q, k in zip(queries, keys):
        zero = jnp.zeros_like(q)
        both = jnp.concatenate([jnp.where(low, q, zero), jnp.where(low, zero, q)], 0)
        scores.append(lax.dot_general(k, both, (((1,), (1,)), ((), ())), preferred_element_type=jnp.float32) + bias)
    expos = [jnp.exp(s - jnp.max(s, 0, keepdims=True)).astype(jnp.bfloat16) for s in scores]
    outs = []
    for expo, v in zip(expos, values):
        wide = jnp.concatenate([v, jnp.ones_like(v)], 1)
        sums = lax.dot_general(expo, wide, (((0,), (0,)), ((), ())), preferred_element_type=jnp.float32)
        upper = jnp.where(low, sums[:n, :128], sums[n:, :128])
        total = jnp.where(low, sums[:n, 128:], sums[n:, 128:]) + land
        outs.append((upper / total * marks).astype(jnp.bfloat16))
    return outs


ORDER = (4, 5, 6, 7, 1, 2, 3, 0)


def pack_kernel(distances, me_ref, marks_ref, fields_ref, *refs):
    outs, (held, held_marks, sems) = refs[: len(distances)], refs[len(distances) :]
    me = me_ref[0]
    tiles = fields_ref.shape[-1] // 128
    copies = [pltpu.make_async_copy(marks_ref, held_marks, sems.at[len(distances)])]
    for i, d in enumerate(distances):
        there = jnp.bitwise_xor(me, d)
        copies.append(pltpu.make_async_copy(fields_ref.at[pl.ds(there * 8, 8)], held.at[i], sems.at[i]))
    for copy in copies:
        copy.start()
    copies[0].wait()
    marks = held_marks[...].astype(jnp.float32)
    marks = jnp.concatenate([marks, jnp.zeros((16, 128 - marks.shape[1]), jnp.float32)], 1).astype(jnp.bfloat16)
    for i in range(len(distances)):
        copies[i + 1].wait()
        piece = held[i].reshape(128, 128 * tiles)
        for t in range(tiles):
            outs[i][128 * t : 128 * t + 128, :] = piece[:, 128 * t : 128 * t + 128]
        outs[i][128 * tiles :, :] = marks


def pack(distances, me, marks, fields):
    cols, width = fields.shape[1:]
    vmem = pl.BlockSpec(memory_space=pltpu.VMEM)
    anywhere = pl.BlockSpec(memory_space=pl.ANY)
    piece = jax.ShapeDtypeStruct((width + 16, 128), jnp.bfloat16)
    n = len(distances)
    return pl.pallas_call(
        functools.partial(pack_kernel, distances),
        out_shape=(piece,) * n,
        in_specs=[pl.BlockSpec(memory_space=pltpu.SMEM), anywhere, anywhere],
        out_specs=(vmem,) * n,
        scratch_shapes=[
            pltpu.VMEM((n, 8, cols, width), jnp.bfloat16),
            pltpu.VMEM(marks.shape, marks.dtype),
            pltpu.SemaphoreType.DMA((n + 1,)),
        ],
        compiler_params=pltpu.CompilerParams(vmem_limit_bytes=PACK_VMEM),
        cost_estimate=pl.CostEstimate(flops=n * 200000, bytes_accessed=n * 400000, transcendentals=0),
        name="pack",
    )(me, marks, fields)


def ready_kernel(*refs):
    refs[-1][...] = jnp.zeros_like(refs[-1])


def ready(weights):
    vmem = pl.BlockSpec(memory_space=pltpu.VMEM)
    return pl.pallas_call(
        ready_kernel,
        out_shape=jax.ShapeDtypeStruct((8, 128), jnp.float32),
        in_specs=[vmem] * len(weights),
        out_specs=vmem,
        compiler_params=pltpu.CompilerParams(vmem_limit_bytes=16 * 1024 * 1024),
        cost_estimate=pl.CostEstimate(flops=0, bytes_accessed=32 << 20, transcendentals=0),
        name="ready",
    )(*weights)


def unpacked(me, piece):
    tiles = (piece.shape[0] - 16) // 128
    lanes = [piece[128 * t : 128 * t + 128] for t in range(tiles)]
    marks = pltpu.roll(piece[128 * tiles :].astype(jnp.float32), jnp.bitwise_and(128 - 8 * me, 127), 1)
    marks = jnp.concatenate([jnp.broadcast_to(marks[:, r : r + 1], (16, 128)) for r in range(8)], 0)
    whole = jnp.concatenate(lanes + [marks.astype(jnp.bfloat16)], 1).astype(jnp.float32)
    whole = whole.reshape(8, 2, 8, 128 * tiles + 128)
    return whole[:, 0], whole[:, 1]


STAGES = ((7, 6), (4, 4), (2, 2), (3, 4))

ROWS_FIRST = 4


def window_kernel(stage, me_ref, *refs):
    pieces = refs[: (4, 2, 1, 1)[stage]]
    refs = refs[len(pieces) :]
    carried = refs[: (0, 3, 5, 7)[stage]]
    refs = refs[len(carried) :]
    _, wq, wk, wv, wo, wq2, wk2, wv2, y_ref, q2_ref, k2_ref, v2_ref, m_ref = refs[:13]
    refs = refs[13:]
    passed = refs[: 3 if stage < 3 else 0]
    placed, q_s, k_s, v_s, o_s, rows_s = refs[len(passed) :]
    width = wq.shape[0]
    scale = (width // HEADS) ** (-0.5)
    me = me_ref[0]
    upper = jnp.bitwise_and(me, 2) > 0
    odd = jnp.bitwise_and(me, 1) > 0
    low = jnp.bitwise_and(me, len(pieces) - 1)
    for d, piece in enumerate(pieces):
        placed[jnp.bitwise_xor(low, d)] = piece[...]
    columns = [unpacked(me, placed[l]) for l in range(len(pieces))]
    mask = low_columns((8, 8, width + 128), 1)
    full = (64, width + 128)

    def whole_window(l):
        return jnp.where(mask, columns[l][1], columns[l][0]).reshape(full)

    def straddling_window(left, right):
        return jnp.where(mask, right, left).reshape(full)

    def either(if_upper, if_lower):
        return jnp.where(upper, if_upper, if_lower)

    windows = [whole_window(0)]
    for l in range(1, len(pieces)):
        windows += [straddling_window(columns[l - 1][1], columns[l][0]), whole_window(l)]
    first, last = columns[0][0], columns[-1][1]
    if stage < 3:
        passed[0][...] = first.reshape(full)
        passed[1][...] = last.reshape(full)
    edges = [a[...].reshape(8, 8, width + 128) for a in carried[:-1]]
    if stage == 1:
        own_first, own_last = edges
        windows = [straddling_window(either(last, own_last), either(own_first, first))] + windows
    if stage >= 2:
        own_first, own_last, second_first, second_last = edges[:4]
        before, after = either(own_last, second_last), either(second_first, own_first)
    if stage == 2:
        windows.append(straddling_window(jnp.where(odd, last, before), jnp.where(odd, after, first)))
    if stage == 3:
        one_first, one_last = edges[4:]
        windows.append(straddling_window(jnp.where(odd, last, one_last), jnp.where(odd, one_first, first)))
        windows.append(straddling_window(jnp.where(odd, before, last), jnp.where(odd, first, after)))
    count = len(windows)
    x = jnp.concatenate([w[:, :width] for w in windows], 0)
    marks = [w[:, width:] for w in windows]
    h = normed_f32(x)
    q_s[...] = (dot_f32(h, wq[...]) * scale).astype(jnp.bfloat16)
    k_s[...] = dot_f32(h, wk[...]).astype(jnp.bfloat16)
    v_s[...] = dot_f32(h, wv[...]).astype(jnp.bfloat16)
    for w in range(count):
        here = slice(64 * w, 64 * w + 64)
        outs = attend(*([a[here, lanes] for lanes in PAIRS] for a in (q_s, k_s, v_s)), marks[w])
        for lanes, out in zip(PAIRS, outs):
            o_s[here, lanes] = out
    y = (x + dot_f32(o_s[...], wo[...])).astype(jnp.bfloat16).astype(jnp.float32)
    skip = 0
    if stage > 0:
        skip = 1
        rows_s[:, :8, :] = carried[-1][...]
    for w in range(count):
        for r in range(8):
            at = 64 * w + 8 * r
            to = 8 * (w + skip)
            if stage < 3 and w == count - 1:
                passed[2][r, :, :width] = y[at : at + 8]
                passed[2][r, :, width:] = marks[w][8 * r : 8 * r + 8]
            else:
                rows_s[r, to : to + 8, :width] = y[at : at + 8]
                rows_s[r, to : to + 8, width:] = marks[w][8 * r : 8 * r + 8]
    m_ref[...] = rows_s[:, :, width:].astype(jnp.bfloat16)
    y_ref[...] = rows_s[:, :, :width].astype(jnp.bfloat16)
    rows = q2_ref.shape[0]
    h = normed_f32(rows_s[:rows, :, :width].reshape(rows * rows_s.shape[1], width))
    q2_ref[...] = (dot_f32(h, wq2[...]) * scale).astype(jnp.bfloat16).reshape(q2_ref.shape)
    k2_ref[...] = dot_f32(h, wk2[...]).astype(jnp.bfloat16).reshape(k2_ref.shape)
    v2_ref[...] = dot_f32(h, wv2[...]).astype(jnp.bfloat16).reshape(v2_ref.shape)


def window_layer(stage, me, pieces, carried, weights):
    width = weights[1].shape[0]
    tokens = 64 * STAGES[stage][0]
    columns = 8 * STAGES[stage][1]
    part = jax.ShapeDtypeStruct((8, columns, width), jnp.bfloat16)
    marks = jax.ShapeDtypeStruct((8, columns, 128), jnp.bfloat16)
    edge = jax.ShapeDtypeStruct((64, width + 128), jnp.float32)
    tail = jax.ShapeDtypeStruct((8, 8, width + 128), jnp.float32)
    projected = part if stage < 3 else jax.ShapeDtypeStruct((ROWS_FIRST, columns, width), jnp.bfloat16)
    outs = (part, projected, projected, projected, marks) + ((edge, edge, tail) if stage < 3 else ())
    vmem = pl.BlockSpec(memory_space=pltpu.VMEM)
    work = pltpu.VMEM((tokens, width), jnp.bfloat16)
    inputs = [*pieces, *carried, *weights]
    return pl.pallas_call(
        functools.partial(window_kernel, stage),
        out_shape=outs,
        in_specs=[pl.BlockSpec(memory_space=pltpu.SMEM)] + [vmem] * len(inputs),
        out_specs=(vmem,) * len(outs),
        scratch_shapes=[
            pltpu.VMEM((len(pieces), width + 16, 128), jnp.bfloat16),
            work, work, work, work,
            pltpu.VMEM((8, columns, width + 128), jnp.float32),
        ],
        compiler_params=pltpu.CompilerParams(vmem_limit_bytes=36 * 1024 * 1024),
        cost_estimate=pl.CostEstimate(
            flops=2 * tokens * width * (7 * width + 512), bytes_accessed=16 << 20, transcendentals=tokens * 64 * HEADS
        ),
        name="window_layer",
    )(me, *inputs)


def row_kernel(start, rows, me_ref, *refs):
    parts, wo, refs = [refs[at : at + 5] for at in range(0, 20, 5)], refs[20], refs[21:]
    width = wo.shape[0]
    length = 128
    earlier = ()
    if start:
        earlier, weights, refs = refs[:4], refs[4:7], refs[7:]
        *refs, q_s, k_s, v_s = refs
        y = parts[3][0][start:].astype(jnp.float32)
        h = normed_f32(y.reshape(rows * y.shape[1], width))
        for to, weight, factor in zip((q_s, k_s, v_s), weights, ((width // HEADS) ** (-0.5), 1.0, 1.0)):
            to[...] = (dot_f32(h, weight[...]) * factor).astype(jnp.bfloat16).reshape(to.shape)
    outs, (o_s, placed) = refs[:8], refs[8:]

    def row(i, r, lanes=slice(None)):
        pieces = [part[i][start + r, :, lanes] for part in parts[:3]]
        if 1 <= i <= 3:
            pieces.append((q_s, k_s, v_s)[i - 1][r, :, lanes] if start else parts[3][i][r, :, lanes])
        else:
            pieces.append(parts[3][i][start + r, :, lanes])
        return jnp.concatenate(pieces, 0)

    for r in range(rows):
        here = slice(length * r, length * r + length)
        heads = attend(*([row(i, r, lanes) for lanes in PAIRS] for i in (1, 2, 3)), row(4, r).astype(jnp.float32))
        for lanes, out in zip(PAIRS, heads):
            o_s[here, lanes] = out
    added = dot_f32(o_s[...], wo[...])
    mask = low_columns((8, width), 0)
    me = me_ref[0]
    upper = jnp.bitwise_and(me, 2) > 0
    odd = jnp.bitwise_and(me, 1) > 0
    same = upper == odd
    for r in range(rows):
        f = row(0, r).astype(jnp.float32) + added[length * r : length * r + length]
        tiles = [f[8 * w : 8 * w + 8] for w in range(16)]
        own, own_second, second = tiles[:7], tiles[7], tiles[8:11]
        third = (jnp.where(odd, tiles[13], tiles[11]), tiles[14], jnp.where(odd, tiles[11], tiles[13]))
        middle, third_own = jnp.where(same, tiles[12], tiles[15]), jnp.where(same, tiles[15], tiles[12])
        after_own = jnp.where(upper, third_own, own_second)
        before_own = jnp.where(upper, own_second, third_own)
        whole = [before_own, *own, after_own]
        whole += [jnp.where(upper, middle, after_own), *second, jnp.where(upper, before_own, middle)]
        whole += [jnp.where(upper, after_own, middle), *third, jnp.where(upper, middle, before_own)]
        for l in range(8):
            at = 2 * l if l < 4 else (9, 11, 14, 16)[l - 4]
            before, a, after = whole[at : at + 3]
            piece = jnp.concatenate([jnp.where(mask, before, a), jnp.where(mask, a, after)], 0)
            placed[l, r] = piece.astype(jnp.bfloat16)
    for i, d in enumerate(ORDER):
        if d < 4:
            if start:
                outs[i][:start] = earlier[i - 4][...]
            outs[i][start:] = placed[jnp.bitwise_xor(jnp.bitwise_and(me, 3), d)]
        else:
            outs[i][...] = placed[d // 2 * 2 + jnp.bitwise_xor(jnp.bitwise_and(me, 1), d % 2)]


def row_layer(start, rows, me, parts, w_out, earlier):
    width = w_out.shape[0]
    length = 128
    far = jax.ShapeDtypeStruct((rows, 16, width), jnp.bfloat16)
    near = jax.ShapeDtypeStruct((start + rows, 16, width), jnp.bfloat16)
    vmem = pl.BlockSpec(memory_space=pltpu.VMEM)
    inputs = [*parts, w_out, *earlier]
    rest = parts[15].shape[1]
    work = pltpu.VMEM((rows, rest, width), jnp.bfloat16)
    return pl.pallas_call(
        functools.partial(row_kernel, start, rows),
        out_shape=(far,) * 4 + (near,) * 4,
        in_specs=[pl.BlockSpec(memory_space=pltpu.SMEM)] + [vmem] * len(inputs),
        out_specs=(vmem,) * 8,
        scratch_shapes=[
            pltpu.VMEM((rows * length, width), jnp.bfloat16),
            pltpu.VMEM((8, rows, 16, width), jnp.bfloat16),
        ]
        + [work] * (3 if start else 0),
        compiler_params=pltpu.CompilerParams(vmem_limit_bytes=36 * 1024 * 1024),
        cost_estimate=pl.CostEstimate(
            flops=0, bytes_accessed=1 << 16, transcendentals=0
        ),
        name="row_layer",
    )(me, *inputs)


def place_kernel(spots, me_ref, *refs):
    pieces, out_ref, sems = refs[: len(spots)], refs[-2], refs[-1]
    copies = []
    for i, (d, start) in enumerate(spots):
        at = jnp.bitwise_xor(me_ref[0], d) * 8 + start
        copies.append(pltpu.make_async_copy(pieces[i], out_ref.at[pl.ds(at, pieces[i].shape[0])], sems.at[i]))
        copies[-1].start()
    for copy in copies:
        copy.wait()


def place(spots, me, pieces, so_far, shape):
    vmem = pl.BlockSpec(memory_space=pltpu.VMEM)
    hbm = pl.BlockSpec(memory_space=pltpu.HBM)
    n = len(pieces)
    more = () if so_far is None else (so_far,)
    return pl.pallas_call(
        functools.partial(place_kernel, spots),
        out_shape=jax.ShapeDtypeStruct(shape, jnp.bfloat16),
        in_specs=[pl.BlockSpec(memory_space=pltpu.SMEM)] + [vmem] * n + [hbm] * len(more),
        out_specs=hbm,
        scratch_shapes=[pltpu.SemaphoreType.DMA((n,))],
        input_output_aliases={n + 1: 0} if more else {},
        compiler_params=pltpu.CompilerParams(vmem_limit_bytes=8 * 1024 * 1024),
        cost_estimate=pl.CostEstimate(flops=0, bytes_accessed=4 << 20, transcendentals=0),
        name="place",
    )(me, *pieces, *more)


def exchanged(piece, distance):
    count = lax.axis_size("lon")
    return lax.ppermute(piece, "lon", [(s, s ^ distance) for s in range(count)])


def gathered_bands(
    fields, ocean, w_query1, w_key1, w_value1, w_out1, w_query2, w_key2, w_value2, w_out2
):
    me = lax.axis_index("lon").astype(jnp.int32).reshape(1)
    weights = (w_query1, w_key1, w_value1, w_out1, w_query2, w_key2, w_value2)
    weights = (ready(weights), *weights)

    packed = dict(zip(ORDER, pack(ORDER, me, ocean.T, fields)))
    got = {d: exchanged(packed[d], d) if d else packed[d] for d in ORDER}
    got[4], *near = lax.optimization_barrier((got[4], got[2], got[3], got[1]))
    got[2], got[3], got[1] = near
    own = window_layer(0, me, [got[d] for d in range(4)], (), weights)
    second = window_layer(1, me, [got[4], got[5]], own[5:], weights)
    edges = (*own[5:7], *second[5:7])
    third = window_layer(2, me, [got[6]], (*edges, second[7]), weights)
    fourth = window_layer(3, me, [got[7]], (*edges, *third[5:]), weights)
    parts = (*own[:5], *second[:5], *third[:5], *fourth)
    first = row_layer(0, ROWS_FIRST, me, parts, w_out2, ())
    last = row_layer(ROWS_FIRST, 8 - ROWS_FIRST, me, parts, w_out2, (*first[4:], w_query2, w_key2, w_value2))
    far = [exchanged(piece, d) for d, piece in zip(ORDER[:4], first)]
    last = list(last)
    for i in range(4):
        last[i], far[i] = lax.optimization_barrier((last[i], far[i]))
    far_last = [exchanged(piece, d) for d, piece in zip(ORDER[:4], last)]
    near = {d: exchanged(piece, d) if d else piece for d, piece in zip(ORDER[4:], last[4:])}
    near = [near[d] for d in ORDER[4:]]
    out = place([(d, 0) for d in ORDER], me, far + near, None, fields.shape)
    return place([(d, ROWS_FIRST) for d in ORDER[:4]], me, far_last, out, fields.shape)


def on_device(fields, *rest):
    rows, cols, width = fields.shape
    if lax.axis_size("lon") == 8 and rows == 64 and cols == 16 and width == 64 * HEADS:
        return gathered_bands(fields, *rest)
    return spread_rows(fields, *rest)


def solution(mesh):
    in_specs = (
        P(("grp", "lat"), "lon", None),
        P(("grp", "lat"), "lon"),
        P(),
        P(),
        P(),
        P(),
        P(),
        P(),
        P(),
        P(),
    )
    out_specs = P(("grp", "lat"), "lon", None)
    return jax.shard_map(
        on_device, mesh=mesh, in_specs=in_specs, out_specs=out_specs, check_vma=False
    )
```

```python
import functools

import jax
import jax.numpy as jnp
from jax import lax
from jax.experimental import pallas as pl
from jax.experimental.pallas import tpu as pltpu
from jax.sharding import PartitionSpec as P

HEADS = 12


EPS = 1e-05
NEG = -1e30

PACK_VMEM = 52 * 1024 * 1024

PAIRS = [slice(128 * p, 128 * p + 128) for p in range(HEADS // 2)]


def passed_along(value, axis, steps):
    count = lax.axis_size(axis)
    pairs = [(source, (source + steps) % count) for source in range(count)]
    return lax.ppermute(value, axis, pairs)


def norm_rows(a):
    af = a.astype(jnp.float32)
    mean = jnp.mean(af, -1, keepdims=True)
    var = jnp.mean((af - mean) * (af - mean), -1, keepdims=True)
    return ((af - mean) * lax.rsqrt(var + EPS)).astype(jnp.bfloat16)


def project(h, weight):
    return jnp.dot(h, weight, preferred_element_type=jnp.float32).astype(jnp.bfloat16)


def masked_softmax(scores, key_ok, land_query):
    top = jnp.max(jnp.where(key_ok, scores, NEG), -1, keepdims=True)
    expo = jnp.where(key_ok, jnp.exp(scores - top), 0.0)
    total = jnp.sum(expo, -1, keepdims=True) + land_query[..., None]
    return (expo / total).astype(jnp.bfloat16)


def window_attend(query, keys, values, flags):
    rows, cols, width = query.shape
    nh = HEADS
    hd = width // nh
    scale = hd ** (-0.5)

    def tiles(a):
        a = a.reshape(rows // 8, 8, cols // 8, 8, nh, hd).transpose(0, 2, 4, 1, 3, 5)
        return a.reshape(rows // 8, cols // 8, nh, 64, hd)

    marks = (
        flags.reshape(rows // 8, 8, cols // 8, 8)
        .transpose(0, 2, 1, 3)
        .reshape(rows // 8, cols // 8, 64)
    )
    key_ok = (marks > 0)[:, :, None, None, :]
    land_query = (marks <= 0).astype(jnp.float32)[:, :, None, :]
    scores = (
        jnp.einsum(
            "abhqd,abhkd->abhqk", tiles(query), tiles(keys), preferred_element_type=jnp.float32
        )
        * scale
    )
    probs = masked_softmax(scores, key_ok, land_query)
    outs = jnp.einsum(
        "abhqk,abhkd->abhqd", probs, tiles(values), preferred_element_type=jnp.float32
    )
    outs = outs * (1.0 - land_query)[..., None]
    outs = outs.astype(jnp.bfloat16).reshape(rows // 8, cols // 8, nh, 8, 8, hd)
    return outs.transpose(0, 3, 1, 4, 2, 5).reshape(rows, cols, width)


def row_attend(query, keys, values, flags):
    rows, length, width = query.shape
    nh = HEADS
    hd = width // nh
    scale = hd ** (-0.5)
    key_ok = (flags > 0)[:, None, :]
    land_query = (flags <= 0).astype(jnp.float32)

    def head(index):
        qh = lax.dynamic_slice_in_dim(query, index * hd, hd, 2)
        kh = lax.dynamic_slice_in_dim(keys, index * hd, hd, 2)
        vh = lax.dynamic_slice_in_dim(values, index * hd, hd, 2)
        scores = jnp.einsum("rqd,rkd->rqk", qh, kh, preferred_element_type=jnp.float32) * scale
        probs = masked_softmax(scores, key_ok, land_query)
        return jnp.einsum("rqk,rkd->rqd", probs, vh, preferred_element_type=jnp.float32)

    outs = lax.map(head, jnp.arange(nh, dtype=jnp.int32))
    outs = outs.transpose(1, 2, 0, 3).reshape(rows, length, width)
    return (outs * (1.0 - land_query)[..., None]).astype(jnp.bfloat16)


def attend_columns(columns, marks, w_query1, w_key1, w_value1):
    return window_attend(
        project(columns, w_query1), project(columns, w_key1), project(columns, w_value1), marks
    )


def spread_rows(
    fields, ocean, w_query1, w_key1, w_value1, w_out1, w_query2, w_key2, w_value2, w_out2
):
    rows, cols, width = fields.shape
    normed = norm_rows(fields)
    marks = ocean.astype(jnp.bfloat16)
    edge_feats, edge_marks = passed_along((normed[:, cols - 4 :], marks[:, cols - 4 :]), "lon", 1)
    columns = jnp.concatenate([edge_feats, normed[:, : cols - 4]], 1)
    column_marks = jnp.concatenate([edge_marks, marks[:, : cols - 4]], 1)
    extended = attend_columns(columns, column_marks, w_query1, w_key1, w_value1)
    returned = passed_along(extended[:, :4], "lon", -1)
    o1 = jnp.concatenate([extended[:, 4:], returned], 1)
    y1 = (
        fields.astype(jnp.float32) + jnp.dot(o1, w_out1, preferred_element_type=jnp.float32)
    ).astype(jnp.bfloat16)
    h2 = norm_rows(y1)
    q2 = project(h2, w_query2)
    k2 = project(h2, w_key2)
    v2 = project(h2, w_value2)
    row_q, row_k, row_v, row_marks = (
        lax.all_to_all(q2, "lon", split_axis=0, concat_axis=1, tiled=True),
        lax.all_to_all(k2, "lon", split_axis=0, concat_axis=1, tiled=True),
        lax.all_to_all(v2, "lon", split_axis=0, concat_axis=1, tiled=True),
        lax.all_to_all(marks, "lon", split_axis=0, concat_axis=1, tiled=True),
    )
    row_out = row_attend(row_q, row_k, row_v, row_marks)
    o2 = lax.all_to_all(row_out, "lon", split_axis=1, concat_axis=0, tiled=True)
    return (
        y1.astype(jnp.float32) + jnp.dot(o2, w_out2, preferred_element_type=jnp.float32)
    ).astype(jnp.bfloat16)


def normed_f32(a):
    mean = jnp.mean(a, -1, keepdims=True)
    centred = a - mean
    var = jnp.mean(centred * centred, -1, keepdims=True)
    return (centred * lax.rsqrt(var + EPS)).astype(jnp.bfloat16)


def dot_f32(a, b):
    return jnp.dot(a, b, preferred_element_type=jnp.float32)


def low_columns(shape, axis):
    return lax.broadcasted_iota(jnp.int32, shape, axis) % 8 < 4


def attend(queries, keys, values, marks):
    n = marks.shape[0]
    low = lax.broadcasted_iota(jnp.int32, (n, 128), 1) < 64
    land = 1.0 - marks
    bias = jnp.concatenate([land * NEG] * (2 * n // 128), 1)
    scores = []
    for q, k in zip(queries, keys):
        zero = jnp.zeros_like(q)
        both = jnp.concatenate([jnp.where(low, q, zero), jnp.where(low, zero, q)], 0)
        scores.append(lax.dot_general(k, both, (((1,), (1,)), ((), ())), preferred_element_type=jnp.float32) + bias)
    expos = [jnp.exp(s - jnp.max(s, 0, keepdims=True)).astype(jnp.bfloat16) for s in scores]
    outs = []
    for expo, v in zip(expos, values):
        wide = jnp.concatenate([v, jnp.ones_like(v)], 1)
        sums = lax.dot_general(expo, wide, (((0,), (0,)), ((), ())), preferred_element_type=jnp.float32)
        upper = jnp.where(low, sums[:n, :128], sums[n:, :128])
        total = jnp.where(low, sums[:n, 128:], sums[n:, 128:]) + land
        outs.append((upper / total * marks).astype(jnp.bfloat16))
    return outs


ORDER = (4, 5, 6, 7, 1, 2, 3, 0)


def pack_kernel(distances, me_ref, marks_ref, fields_ref, *refs):
    outs, (held, held_marks, sems) = refs[: len(distances)], refs[len(distances) :]
    me = me_ref[0]
    tiles = fields_ref.shape[-1] // 128
    copies = [pltpu.make_async_copy(marks_ref, held_marks, sems.at[len(distances)])]
    for i, d in enumerate(distances):
        there = jnp.bitwise_xor(me, d)
        copies.append(pltpu.make_async_copy(fields_ref.at[pl.ds(there * 8, 8)], held.at[i], sems.at[i]))
    for copy in copies:
        copy.start()
    copies[0].wait()
    marks = held_marks[...].astype(jnp.float32)
    marks = jnp.concatenate([marks, jnp.zeros((16, 128 - marks.shape[1]), jnp.float32)], 1).astype(jnp.bfloat16)
    for i in range(len(distances)):
        copies[i + 1].wait()
        piece = held[i].reshape(128, 128 * tiles)
        for t in range(tiles):
            outs[i][128 * t : 128 * t + 128, :] = piece[:, 128 * t : 128 * t + 128]
        outs[i][128 * tiles :, :] = marks


def pack(distances, me, marks, fields):
    cols, width = fields.shape[1:]
    vmem = pl.BlockSpec(memory_space=pltpu.VMEM)
    anywhere = pl.BlockSpec(memory_space=pl.ANY)
    piece = jax.ShapeDtypeStruct((width + 16, 128), jnp.bfloat16)
    n = len(distances)
    return pl.pallas_call(
        functools.partial(pack_kernel, distances),
        out_shape=(piece,) * n,
        in_specs=[pl.BlockSpec(memory_space=pltpu.SMEM), anywhere, anywhere],
        out_specs=(vmem,) * n,
        scratch_shapes=[
            pltpu.VMEM((n, 8, cols, width), jnp.bfloat16),
            pltpu.VMEM(marks.shape, marks.dtype),
            pltpu.SemaphoreType.DMA((n + 1,)),
        ],
        compiler_params=pltpu.CompilerParams(vmem_limit_bytes=PACK_VMEM),
        cost_estimate=pl.CostEstimate(flops=n * 200000, bytes_accessed=n * 400000, transcendentals=0),
        name="pack",
    )(me, marks, fields)


def ready_kernel(*refs):
    refs[-1][...] = jnp.zeros_like(refs[-1])


def ready(weights):
    vmem = pl.BlockSpec(memory_space=pltpu.VMEM)
    return pl.pallas_call(
        ready_kernel,
        out_shape=jax.ShapeDtypeStruct((8, 128), jnp.float32),
        in_specs=[vmem] * len(weights),
        out_specs=vmem,
        compiler_params=pltpu.CompilerParams(vmem_limit_bytes=16 * 1024 * 1024),
        cost_estimate=pl.CostEstimate(flops=0, bytes_accessed=32 << 20, transcendentals=0),
        name="ready",
    )(*weights)


def unpacked(me, piece):
    tiles = (piece.shape[0] - 16) // 128
    lanes = [piece[128 * t : 128 * t + 128] for t in range(tiles)]
    marks = pltpu.roll(piece[128 * tiles :].astype(jnp.float32), jnp.bitwise_and(128 - 8 * me, 127), 1)
    marks = jnp.concatenate([jnp.broadcast_to(marks[:, r : r + 1], (16, 128)) for r in range(8)], 0)
    whole = jnp.concatenate(lanes + [marks.astype(jnp.bfloat16)], 1).astype(jnp.float32)
    whole = whole.reshape(8, 2, 8, 128 * tiles + 128)
    return whole[:, 0], whole[:, 1]


STAGES = ((7, 6), (4, 4), (2, 2), (3, 4))

ROWS_FIRST = 4


def window_kernel(stage, me_ref, *refs):
    pieces = refs[: (4, 2, 1, 1)[stage]]
    refs = refs[len(pieces) :]
    carried = refs[: (0, 3, 5, 7)[stage]]
    refs = refs[len(carried) :]
    _, wq, wk, wv, wo, wq2, wk2, wv2, y_ref, q2_ref, k2_ref, v2_ref, m_ref = refs[:13]
    refs = refs[13:]
    passed = refs[: 3 if stage < 3 else 0]
    placed, q_s, k_s, v_s, o_s, rows_s = refs[len(passed) :]
    width = wq.shape[0]
    scale = (width // HEADS) ** (-0.5)
    me = me_ref[0]
    upper = jnp.bitwise_and(me, 2) > 0
    odd = jnp.bitwise_and(me, 1) > 0
    low = jnp.bitwise_and(me, len(pieces) - 1)
    for d, piece in enumerate(pieces):
        placed[jnp.bitwise_xor(low, d)] = piece[...]
    columns = [unpacked(me, placed[l]) for l in range(len(pieces))]
    mask = low_columns((8, 8, width + 128), 1)
    full = (64, width + 128)

    def whole_window(l):
        return jnp.where(mask, columns[l][1], columns[l][0]).reshape(full)

    def straddling_window(left, right):
        return jnp.where(mask, right, left).reshape(full)

    def either(if_upper, if_lower):
        return jnp.where(upper, if_upper, if_lower)

    windows = [whole_window(0)]
    for l in range(1, len(pieces)):
        windows += [straddling_window(columns[l - 1][1], columns[l][0]), whole_window(l)]
    first, last = columns[0][0], columns[-1][1]
    if stage < 3:
        passed[0][...] = first.reshape(full)
        passed[1][...] = last.reshape(full)
    edges = [a[...].reshape(8, 8, width + 128) for a in carried[:-1]]
    if stage == 1:
        own_first, own_last = edges
        windows = [straddling_window(either(last, own_last), either(own_first, first))] + windows
    if stage >= 2:
        own_first, own_last, second_first, second_last = edges[:4]
        before, after = either(own_last, second_last), either(second_first, own_first)
    if stage == 2:
        windows.append(straddling_window(jnp.where(odd, last, before), jnp.where(odd, after, first)))
    if stage == 3:
        one_first, one_last = edges[4:]
        windows.append(straddling_window(jnp.where(odd, last, one_last), jnp.where(odd, one_first, first)))
        windows.append(straddling_window(jnp.where(odd, before, last), jnp.where(odd, first, after)))
    count = len(windows)
    x = jnp.concatenate([w[:, :width] for w in windows], 0)
    marks = [w[:, width:] for w in windows]
    h = normed_f32(x)
    q_s[...] = (dot_f32(h, wq[...]) * scale).astype(jnp.bfloat16)
    k_s[...] = dot_f32(h, wk[...]).astype(jnp.bfloat16)
    v_s[...] = dot_f32(h, wv[...]).astype(jnp.bfloat16)
    for w in range(count):
        here = slice(64 * w, 64 * w + 64)
        outs = attend(*([a[here, lanes] for lanes in PAIRS] for a in (q_s, k_s, v_s)), marks[w])
        for lanes, out in zip(PAIRS, outs):
            o_s[here, lanes] = out
    y = (x + dot_f32(o_s[...], wo[...])).astype(jnp.bfloat16).astype(jnp.float32)
    skip = 0
    if stage > 0:
        skip = 1
        rows_s[:, :8, :] = carried[-1][...]
    for w in range(count):
        for r in range(8):
            at = 64 * w + 8 * r
            to = 8 * (w + skip)
            if stage < 3 and w == count - 1:
                passed[2][r, :, :width] = y[at : at + 8]
                passed[2][r, :, width:] = marks[w][8 * r : 8 * r + 8]
            else:
                rows_s[r, to : to + 8, :width] = y[at : at + 8]
                rows_s[r, to : to + 8, width:] = marks[w][8 * r : 8 * r + 8]
    m_ref[...] = rows_s[:, :, width:].astype(jnp.bfloat16)
    y_ref[...] = rows_s[:, :, :width].astype(jnp.bfloat16)
    rows = q2_ref.shape[0]
    h = normed_f32(rows_s[:rows, :, :width].reshape(rows * rows_s.shape[1], width))
    q2_ref[...] = (dot_f32(h, wq2[...]) * scale).astype(jnp.bfloat16).reshape(q2_ref.shape)
    k2_ref[...] = dot_f32(h, wk2[...]).astype(jnp.bfloat16).reshape(k2_ref.shape)
    v2_ref[...] = dot_f32(h, wv2[...]).astype(jnp.bfloat16).reshape(v2_ref.shape)


def window_layer(stage, me, pieces, carried, weights):
    width = weights[1].shape[0]
    tokens = 64 * STAGES[stage][0]
    columns = 8 * STAGES[stage][1]
    part = jax.ShapeDtypeStruct((8, columns, width), jnp.bfloat16)
    marks = jax.ShapeDtypeStruct((8, columns, 128), jnp.bfloat16)
    edge = jax.ShapeDtypeStruct((64, width + 128), jnp.float32)
    tail = jax.ShapeDtypeStruct((8, 8, width + 128), jnp.float32)
    projected = part if stage < 3 else jax.ShapeDtypeStruct((ROWS_FIRST, columns, width), jnp.bfloat16)
    outs = (part, projected, projected, projected, marks) + ((edge, edge, tail) if stage < 3 else ())
    vmem = pl.BlockSpec(memory_space=pltpu.VMEM)
    work = pltpu.VMEM((tokens, width), jnp.bfloat16)
    inputs = [*pieces, *carried, *weights]
    return pl.pallas_call(
        functools.partial(window_kernel, stage),
        out_shape=outs,
        in_specs=[pl.BlockSpec(memory_space=pltpu.SMEM)] + [vmem] * len(inputs),
        out_specs=(vmem,) * len(outs),
        scratch_shapes=[
            pltpu.VMEM((len(pieces), width + 16, 128), jnp.bfloat16),
            work, work, work, work,
            pltpu.VMEM((8, columns, width + 128), jnp.float32),
        ],
        compiler_params=pltpu.CompilerParams(vmem_limit_bytes=36 * 1024 * 1024),
        cost_estimate=pl.CostEstimate(
            flops=2 * tokens * width * (7 * width + 512), bytes_accessed=16 << 20, transcendentals=tokens * 64 * HEADS
        ),
        name="window_layer",
    )(me, *inputs)


def row_kernel(start, rows, me_ref, *refs):
    parts, wo, refs = [refs[at : at + 5] for at in range(0, 20, 5)], refs[20], refs[21:]
    width = wo.shape[0]
    length = 128
    earlier = ()
    if start:
        earlier, weights, refs = refs[:4], refs[4:7], refs[7:]
        *refs, q_s, k_s, v_s = refs
        y = parts[3][0][start:].astype(jnp.float32)
        h = normed_f32(y.reshape(rows * y.shape[1], width))
        for to, weight, factor in zip((q_s, k_s, v_s), weights, ((width // HEADS) ** (-0.5), 1.0, 1.0)):
            to[...] = (dot_f32(h, weight[...]) * factor).astype(jnp.bfloat16).reshape(to.shape)
    outs, (o_s, placed) = refs[:8], refs[8:]

    def row(i, r, lanes=slice(None)):
        pieces = [part[i][start + r, :, lanes] for part in parts[:3]]
        if 1 <= i <= 3:
            pieces.append((q_s, k_s, v_s)[i - 1][r, :, lanes] if start else parts[3][i][r, :, lanes])
        else:
            pieces.append(parts[3][i][start + r, :, lanes])
        return jnp.concatenate(pieces, 0)

    for r in range(rows):
        here = slice(length * r, length * r + length)
        heads = attend(*([row(i, r, lanes) for lanes in PAIRS] for i in (1, 2, 3)), row(4, r).astype(jnp.float32))
        for lanes, out in zip(PAIRS, heads):
            o_s[here, lanes] = out
    added = dot_f32(o_s[...], wo[...])
    mask = low_columns((8, width), 0)
    me = me_ref[0]
    upper = jnp.bitwise_and(me, 2) > 0
    odd = jnp.bitwise_and(me, 1) > 0
    same = upper == odd
    for r in range(rows):
        f = row(0, r).astype(jnp.float32) + added[length * r : length * r + length]
        tiles = [f[8 * w : 8 * w + 8] for w in range(16)]
        own, own_second, second = tiles[:7], tiles[7], tiles[8:11]
        third = (jnp.where(odd, tiles[13], tiles[11]), tiles[14], jnp.where(odd, tiles[11], tiles[13]))
        middle, third_own = jnp.where(same, tiles[12], tiles[15]), jnp.where(same, tiles[15], tiles[12])
        after_own = jnp.where(upper, third_own, own_second)
        before_own = jnp.where(upper, own_second, third_own)
        whole = [before_own, *own, after_own]
        whole += [jnp.where(upper, middle, after_own), *second, jnp.where(upper, before_own, middle)]
        whole += [jnp.where(upper, after_own, middle), *third, jnp.where(upper, middle, before_own)]
        for l in range(8):
            at = 2 * l if l < 4 else (9, 11, 14, 16)[l - 4]
            before, a, after = whole[at : at + 3]
            piece = jnp.concatenate([jnp.where(mask, before, a), jnp.where(mask, a, after)], 0)
            placed[l, r] = piece.astype(jnp.bfloat16)
    for i, d in enumerate(ORDER):
        if d < 4:
            if start:
                outs[i][:start] = earlier[i - 4][...]
            outs[i][start:] = placed[jnp.bitwise_xor(jnp.bitwise_and(me, 3), d)]
        else:
            outs[i][...] = placed[d // 2 * 2 + jnp.bitwise_xor(jnp.bitwise_and(me, 1), d % 2)]


def row_layer(start, rows, me, parts, w_out, earlier):
    width = w_out.shape[0]
    length = 128
    far = jax.ShapeDtypeStruct((rows, 16, width), jnp.bfloat16)
    near = jax.ShapeDtypeStruct((start + rows, 16, width), jnp.bfloat16)
    vmem = pl.BlockSpec(memory_space=pltpu.VMEM)
    inputs = [*parts, w_out, *earlier]
    rest = parts[15].shape[1]
    work = pltpu.VMEM((rows, rest, width), jnp.bfloat16)
    return pl.pallas_call(
        functools.partial(row_kernel, start, rows),
        out_shape=(far,) * 4 + (near,) * 4,
        in_specs=[pl.BlockSpec(memory_space=pltpu.SMEM)] + [vmem] * len(inputs),
        out_specs=(vmem,) * 8,
        scratch_shapes=[
            pltpu.VMEM((rows * length, width), jnp.bfloat16),
            pltpu.VMEM((8, rows, 16, width), jnp.bfloat16),
        ]
        + [work] * (3 if start else 0),
        compiler_params=pltpu.CompilerParams(vmem_limit_bytes=36 * 1024 * 1024),
        cost_estimate=pl.CostEstimate(
            flops=0, bytes_accessed=1 << 16, transcendentals=0
        ),
        name="row_layer",
    )(me, *inputs)


def place_kernel(spots, me_ref, *refs):
    pieces, out_ref, sems = refs[: len(spots)], refs[-2], refs[-1]
    copies = []
    for i, (d, start) in enumerate(spots):
        at = jnp.bitwise_xor(me_ref[0], d) * 8 + start
        copies.append(pltpu.make_async_copy(pieces[i], out_ref.at[pl.ds(at, pieces[i].shape[0])], sems.at[i]))
        copies[-1].start()
    for copy in copies:
        copy.wait()


def place(spots, me, pieces, so_far, shape):
    vmem = pl.BlockSpec(memory_space=pltpu.VMEM)
    hbm = pl.BlockSpec(memory_space=pltpu.HBM)
    n = len(pieces)
    more = () if so_far is None else (so_far,)
    return pl.pallas_call(
        functools.partial(place_kernel, spots),
        out_shape=jax.ShapeDtypeStruct(shape, jnp.bfloat16),
        in_specs=[pl.BlockSpec(memory_space=pltpu.SMEM)] + [vmem] * n + [hbm] * len(more),
        out_specs=hbm,
        scratch_shapes=[pltpu.SemaphoreType.DMA((n,))],
        input_output_aliases={n + 1: 0} if more else {},
        compiler_params=pltpu.CompilerParams(vmem_limit_bytes=8 * 1024 * 1024),
        cost_estimate=pl.CostEstimate(flops=0, bytes_accessed=4 << 20, transcendentals=0),
        name="place",
    )(me, *pieces, *more)


def exchanged(piece, distance):
    count = lax.axis_size("lon")
    return lax.ppermute(piece, "lon", [(s, s ^ distance) for s in range(count)])


def gathered_bands(
    fields, ocean, w_query1, w_key1, w_value1, w_out1, w_query2, w_key2, w_value2, w_out2
):
    me = lax.axis_index("lon").astype(jnp.int32).reshape(1)
    weights = (w_query1, w_key1, w_value1, w_out1, w_query2, w_key2, w_value2)
    weights = (ready(weights[:3]), *weights)

    packed = dict(zip(ORDER, pack(ORDER, me, ocean.T, fields)))
    got = {d: exchanged(packed[d], d) if d else packed[d] for d in ORDER}
    got[4], *near = lax.optimization_barrier((got[4], got[2], got[3], got[1]))
    got[2], got[3], got[1] = near
    own = window_layer(0, me, [got[d] for d in range(4)], (), weights)
    second = window_layer(1, me, [got[4], got[5]], own[5:], weights)
    edges = (*own[5:7], *second[5:7])
    third = window_layer(2, me, [got[6]], (*edges, second[7]), weights)
    fourth = window_layer(3, me, [got[7]], (*edges, *third[5:]), weights)
    parts = (*own[:5], *second[:5], *third[:5], *fourth)
    first = row_layer(0, ROWS_FIRST, me, parts, w_out2, ())
    last = row_layer(ROWS_FIRST, 8 - ROWS_FIRST, me, parts, w_out2, (*first[4:], w_query2, w_key2, w_value2))
    far = [exchanged(piece, d) for d, piece in zip(ORDER[:4], first)]
    last = list(last)
    for i in range(4):
        last[i], far[i] = lax.optimization_barrier((last[i], far[i]))
    far_last = [exchanged(piece, d) for d, piece in zip(ORDER[:4], last)]
    near = {d: exchanged(piece, d) if d else piece for d, piece in zip(ORDER[4:], last[4:])}
    near = [near[d] for d in ORDER[4:]]
    out = place([(d, 0) for d in ORDER], me, far + near, None, fields.shape)
    return place([(d, ROWS_FIRST) for d in ORDER[:4]], me, far_last, out, fields.shape)


def on_device(fields, *rest):
    rows, cols, width = fields.shape
    if lax.axis_size("lon") == 8 and rows == 64 and cols == 16 and width == 64 * HEADS:
        return gathered_bands(fields, *rest)
    return spread_rows(fields, *rest)


def solution(mesh):
    in_specs = (
        P(("grp", "lat"), "lon", None),
        P(("grp", "lat"), "lon"),
        P(),
        P(),
        P(),
        P(),
        P(),
        P(),
        P(),
        P(),
    )
    out_specs = P(("grp", "lat"), "lon", None)
    return jax.shard_map(
        on_device, mesh=mesh, in_specs=in_specs, out_specs=out_specs, check_vma=False
    )
```

```python
import functools

import jax
import jax.numpy as jnp
from jax import lax
from jax.experimental import pallas as pl
from jax.experimental.pallas import tpu as pltpu
from jax.sharding import PartitionSpec as P

HEADS = 12


EPS = 1e-05
NEG = -1e30

PACK_VMEM = (54 * 1024 * 1024, 52 * 1024 * 1024)

PAIRS = [slice(128 * p, 128 * p + 128) for p in range(HEADS // 2)]


def passed_along(value, axis, steps):
    count = lax.axis_size(axis)
    pairs = [(source, (source + steps) % count) for source in range(count)]
    return lax.ppermute(value, axis, pairs)


def norm_rows(a):
    af = a.astype(jnp.float32)
    mean = jnp.mean(af, -1, keepdims=True)
    var = jnp.mean((af - mean) * (af - mean), -1, keepdims=True)
    return ((af - mean) * lax.rsqrt(var + EPS)).astype(jnp.bfloat16)


def project(h, weight):
    return jnp.dot(h, weight, preferred_element_type=jnp.float32).astype(jnp.bfloat16)


def masked_softmax(scores, key_ok, land_query):
    top = jnp.max(jnp.where(key_ok, scores, NEG), -1, keepdims=True)
    expo = jnp.where(key_ok, jnp.exp(scores - top), 0.0)
    total = jnp.sum(expo, -1, keepdims=True) + land_query[..., None]
    return (expo / total).astype(jnp.bfloat16)


def window_attend(query, keys, values, flags):
    rows, cols, width = query.shape
    nh = HEADS
    hd = width // nh
    scale = hd ** (-0.5)

    def tiles(a):
        a = a.reshape(rows // 8, 8, cols // 8, 8, nh, hd).transpose(0, 2, 4, 1, 3, 5)
        return a.reshape(rows // 8, cols // 8, nh, 64, hd)

    marks = (
        flags.reshape(rows // 8, 8, cols // 8, 8)
        .transpose(0, 2, 1, 3)
        .reshape(rows // 8, cols // 8, 64)
    )
    key_ok = (marks > 0)[:, :, None, None, :]
    land_query = (marks <= 0).astype(jnp.float32)[:, :, None, :]
    scores = (
        jnp.einsum(
            "abhqd,abhkd->abhqk", tiles(query), tiles(keys), preferred_element_type=jnp.float32
        )
        * scale
    )
    probs = masked_softmax(scores, key_ok, land_query)
    outs = jnp.einsum(
        "abhqk,abhkd->abhqd", probs, tiles(values), preferred_element_type=jnp.float32
    )
    outs = outs * (1.0 - land_query)[..., None]
    outs = outs.astype(jnp.bfloat16).reshape(rows // 8, cols // 8, nh, 8, 8, hd)
    return outs.transpose(0, 3, 1, 4, 2, 5).reshape(rows, cols, width)


def row_attend(query, keys, values, flags):
    rows, length, width = query.shape
    nh = HEADS
    hd = width // nh
    scale = hd ** (-0.5)
    key_ok = (flags > 0)[:, None, :]
    land_query = (flags <= 0).astype(jnp.float32)

    def head(index):
        qh = lax.dynamic_slice_in_dim(query, index * hd, hd, 2)
        kh = lax.dynamic_slice_in_dim(keys, index * hd, hd, 2)
        vh = lax.dynamic_slice_in_dim(values, index * hd, hd, 2)
        scores = jnp.einsum("rqd,rkd->rqk", qh, kh, preferred_element_type=jnp.float32) * scale
        probs = masked_softmax(scores, key_ok, land_query)
        return jnp.einsum("rqk,rkd->rqd", probs, vh, preferred_element_type=jnp.float32)

    outs = lax.map(head, jnp.arange(nh, dtype=jnp.int32))
    outs = outs.transpose(1, 2, 0, 3).reshape(rows, length, width)
    return (outs * (1.0 - land_query)[..., None]).astype(jnp.bfloat16)


def attend_columns(columns, marks, w_query1, w_key1, w_value1):
    return window_attend(
        project(columns, w_query1), project(columns, w_key1), project(columns, w_value1), marks
    )


def spread_rows(
    fields, ocean, w_query1, w_key1, w_value1, w_out1, w_query2, w_key2, w_value2, w_out2
):
    rows, cols, width = fields.shape
    normed = norm_rows(fields)
    marks = ocean.astype(jnp.bfloat16)
    edge_feats, edge_marks = passed_along((normed[:, cols - 4 :], marks[:, cols - 4 :]), "lon", 1)
    columns = jnp.concatenate([edge_feats, normed[:, : cols - 4]], 1)
    column_marks = jnp.concatenate([edge_marks, marks[:, : cols - 4]], 1)
    extended = attend_columns(columns, column_marks, w_query1, w_key1, w_value1)
    returned = passed_along(extended[:, :4], "lon", -1)
    o1 = jnp.concatenate([extended[:, 4:], returned], 1)
    y1 = (
        fields.astype(jnp.float32) + jnp.dot(o1, w_out1, preferred_element_type=jnp.float32)
    ).astype(jnp.bfloat16)
    h2 = norm_rows(y1)
    q2 = project(h2, w_query2)
    k2 = project(h2, w_key2)
    v2 = project(h2, w_value2)
    row_q, row_k, row_v, row_marks = (
        lax.all_to_all(q2, "lon", split_axis=0, concat_axis=1, tiled=True),
        lax.all_to_all(k2, "lon", split_axis=0, concat_axis=1, tiled=True),
        lax.all_to_all(v2, "lon", split_axis=0, concat_axis=1, tiled=True),
        lax.all_to_all(marks, "lon", split_axis=0, concat_axis=1, tiled=True),
    )
    row_out = row_attend(row_q, row_k, row_v, row_marks)
    o2 = lax.all_to_all(row_out, "lon", split_axis=1, concat_axis=0, tiled=True)
    return (
        y1.astype(jnp.float32) + jnp.dot(o2, w_out2, preferred_element_type=jnp.float32)
    ).astype(jnp.bfloat16)


def normed_f32(a):
    mean = jnp.mean(a, -1, keepdims=True)
    centred = a - mean
    var = jnp.mean(centred * centred, -1, keepdims=True)
    return (centred * lax.rsqrt(var + EPS)).astype(jnp.bfloat16)


def dot_f32(a, b):
    return jnp.dot(a, b, preferred_element_type=jnp.float32)


def low_columns(shape, axis):
    return lax.broadcasted_iota(jnp.int32, shape, axis) % 8 < 4


def attend(queries, keys, values, marks):
    n = marks.shape[0]
    low = lax.broadcasted_iota(jnp.int32, (n, 128), 1) < 64
    land = 1.0 - marks
    bias = jnp.concatenate([land * NEG] * (2 * n // 128), 1)
    scores = []
    for q, k in zip(queries, keys):
        zero = jnp.zeros_like(q)
        both = jnp.concatenate([jnp.where(low, q, zero), jnp.where(low, zero, q)], 0)
        scores.append(lax.dot_general(k, both, (((1,), (1,)), ((), ())), preferred_element_type=jnp.float32) + bias)
    expos = [jnp.exp(s - jnp.max(s, 0, keepdims=True)).astype(jnp.bfloat16) for s in scores]
    outs = []
    for expo, v in zip(expos, values):
        wide = jnp.concatenate([v, jnp.ones_like(v)], 1)
        sums = lax.dot_general(expo, wide, (((0,), (0,)), ((), ())), preferred_element_type=jnp.float32)
        upper = jnp.where(low, sums[:n, :128], sums[n:, :128])
        total = jnp.where(low, sums[:n, 128:], sums[n:, 128:]) + land
        outs.append((upper / total * marks).astype(jnp.bfloat16))
    return outs


ORDER = (4, 5, 6, 7, 1, 2, 3, 0)


def pack_kernel(distances, me_ref, marks_ref, fields_ref, *refs):
    outs, (held, held_marks, sems) = refs[: len(distances)], refs[len(distances) :]
    me = me_ref[0]
    tiles = fields_ref.shape[-1] // 128
    copies = [pltpu.make_async_copy(marks_ref, held_marks, sems.at[len(distances)])]
    for i, d in enumerate(distances):
        there = jnp.bitwise_xor(me, d)
        copies.append(pltpu.make_async_copy(fields_ref.at[pl.ds(there * 8, 8)], held.at[i], sems.at[i]))
    for copy in copies:
        copy.start()
    copies[0].wait()
    marks = held_marks[...].astype(jnp.float32)
    marks = jnp.concatenate([marks, jnp.zeros((16, 128 - marks.shape[1]), jnp.float32)], 1).astype(jnp.bfloat16)
    for i in range(len(distances)):
        copies[i + 1].wait()
        piece = held[i].reshape(128, 128 * tiles)
        for t in range(tiles):
            outs[i][128 * t : 128 * t + 128, :] = piece[:, 128 * t : 128 * t + 128]
        outs[i][128 * tiles :, :] = marks


def pack(distances, me, marks, fields):
    cols, width = fields.shape[1:]
    vmem = pl.BlockSpec(memory_space=pltpu.VMEM)
    anywhere = pl.BlockSpec(memory_space=pl.ANY)
    piece = jax.ShapeDtypeStruct((width + 16, 128), jnp.bfloat16)
    n = len(distances)
    return pl.pallas_call(
        functools.partial(pack_kernel, distances),
        out_shape=(piece,) * n,
        in_specs=[pl.BlockSpec(memory_space=pltpu.SMEM), anywhere, anywhere],
        out_specs=(vmem,) * n,
        scratch_shapes=[
            pltpu.VMEM((n, 8, cols, width), jnp.bfloat16),
            pltpu.VMEM(marks.shape, marks.dtype),
            pltpu.SemaphoreType.DMA((n + 1,)),
        ],
        compiler_params=pltpu.CompilerParams(vmem_limit_bytes=PACK_VMEM[n > 1]),
        cost_estimate=pl.CostEstimate(flops=n * 200000, bytes_accessed=n * 400000, transcendentals=0),
        name="pack",
    )(me, marks, fields)


def ready_kernel(*refs):
    refs[-1][...] = jnp.zeros_like(refs[-1])


def ready(weights):
    vmem = pl.BlockSpec(memory_space=pltpu.VMEM)
    return pl.pallas_call(
        ready_kernel,
        out_shape=jax.ShapeDtypeStruct((8, 128), jnp.float32),
        in_specs=[vmem] * len(weights),
        out_specs=vmem,
        compiler_params=pltpu.CompilerParams(vmem_limit_bytes=16 * 1024 * 1024),
        cost_estimate=pl.CostEstimate(flops=0, bytes_accessed=32 << 20, transcendentals=0),
        name="ready",
    )(*weights)


def unpacked(me, piece):
    tiles = (piece.shape[0] - 16) // 128
    lanes = [piece[128 * t : 128 * t + 128] for t in range(tiles)]
    marks = pltpu.roll(piece[128 * tiles :].astype(jnp.float32), jnp.bitwise_and(128 - 8 * me, 127), 1)
    marks = jnp.concatenate([jnp.broadcast_to(marks[:, r : r + 1], (16, 128)) for r in range(8)], 0)
    whole = jnp.concatenate(lanes + [marks.astype(jnp.bfloat16)], 1).astype(jnp.float32)
    whole = whole.reshape(8, 2, 8, 128 * tiles + 128)
    return whole[:, 0], whole[:, 1]


STAGES = ((7, 6), (4, 4), (2, 2), (3, 4))

ROWS_FIRST = 4


def window_kernel(stage, me_ref, *refs):
    pieces = refs[: (4, 2, 1, 1)[stage]]
    refs = refs[len(pieces) :]
    carried = refs[: (0, 3, 5, 7)[stage]]
    refs = refs[len(carried) :]
    _, wq, wk, wv, wo, wq2, wk2, wv2, y_ref, q2_ref, k2_ref, v2_ref, m_ref = refs[:13]
    refs = refs[13:]
    passed = refs[: 3 if stage < 3 else 0]
    placed, q_s, k_s, v_s, o_s, rows_s = refs[len(passed) :]
    width = wq.shape[0]
    scale = (width // HEADS) ** (-0.5)
    me = me_ref[0]
    upper = jnp.bitwise_and(me, 2) > 0
    odd = jnp.bitwise_and(me, 1) > 0
    low = jnp.bitwise_and(me, len(pieces) - 1)
    for d, piece in enumerate(pieces):
        placed[jnp.bitwise_xor(low, d)] = piece[...]
    columns = [unpacked(me, placed[l]) for l in range(len(pieces))]
    mask = low_columns((8, 8, width + 128), 1)
    full = (64, width + 128)

    def whole_window(l):
        return jnp.where(mask, columns[l][1], columns[l][0]).reshape(full)

    def straddling_window(left, right):
        return jnp.where(mask, right, left).reshape(full)

    def either(if_upper, if_lower):
        return jnp.where(upper, if_upper, if_lower)

    windows = [whole_window(0)]
    for l in range(1, len(pieces)):
        windows += [straddling_window(columns[l - 1][1], columns[l][0]), whole_window(l)]
    first, last = columns[0][0], columns[-1][1]
    if stage < 3:
        passed[0][...] = first.reshape(full)
        passed[1][...] = last.reshape(full)
    edges = [a[...].reshape(8, 8, width + 128) for a in carried[:-1]]
    if stage == 1:
        own_first, own_last = edges
        windows = [straddling_window(either(last, own_last), either(own_first, first))] + windows
    if stage >= 2:
        own_first, own_last, second_first, second_last = edges[:4]
        before, after = either(own_last, second_last), either(second_first, own_first)
    if stage == 2:
        windows.append(straddling_window(jnp.where(odd, last, before), jnp.where(odd, after, first)))
    if stage == 3:
        one_first, one_last = edges[4:]
        windows.append(straddling_window(jnp.where(odd, last, one_last), jnp.where(odd, one_first, first)))
        windows.append(straddling_window(jnp.where(odd, before, last), jnp.where(odd, first, after)))
    count = len(windows)
    x = jnp.concatenate([w[:, :width] for w in windows], 0)
    marks = [w[:, width:] for w in windows]
    h = normed_f32(x)
    q_s[...] = (dot_f32(h, wq[...]) * scale).astype(jnp.bfloat16)
    k_s[...] = dot_f32(h, wk[...]).astype(jnp.bfloat16)
    v_s[...] = dot_f32(h, wv[...]).astype(jnp.bfloat16)
    for w in range(count):
        here = slice(64 * w, 64 * w + 64)
        outs = attend(*([a[here, lanes] for lanes in PAIRS] for a in (q_s, k_s, v_s)), marks[w])
        for lanes, out in zip(PAIRS, outs):
            o_s[here, lanes] = out
    y = (x + dot_f32(o_s[...], wo[...])).astype(jnp.bfloat16).astype(jnp.float32)
    skip = 0
    if stage > 0:
        skip = 1
        rows_s[:, :8, :] = carried[-1][...]
    for w in range(count):
        for r in range(8):
            at = 64 * w + 8 * r
            to = 8 * (w + skip)
            if stage < 3 and w == count - 1:
                passed[2][r, :, :width] = y[at : at + 8]
                passed[2][r, :, width:] = marks[w][8 * r : 8 * r + 8]
            else:
                rows_s[r, to : to + 8, :width] = y[at : at + 8]
                rows_s[r, to : to + 8, width:] = marks[w][8 * r : 8 * r + 8]
    m_ref[...] = rows_s[:, :, width:].astype(jnp.bfloat16)
    y_ref[...] = rows_s[:, :, :width].astype(jnp.bfloat16)
    rows = q2_ref.shape[0]
    h = normed_f32(rows_s[:rows, :, :width].reshape(rows * rows_s.shape[1], width))
    q2_ref[...] = (dot_f32(h, wq2[...]) * scale).astype(jnp.bfloat16).reshape(q2_ref.shape)
    k2_ref[...] = dot_f32(h, wk2[...]).astype(jnp.bfloat16).reshape(k2_ref.shape)
    v2_ref[...] = dot_f32(h, wv2[...]).astype(jnp.bfloat16).reshape(v2_ref.shape)


def window_layer(stage, me, pieces, carried, weights):
    width = weights[1].shape[0]
    tokens = 64 * STAGES[stage][0]
    columns = 8 * STAGES[stage][1]
    part = jax.ShapeDtypeStruct((8, columns, width), jnp.bfloat16)
    marks = jax.ShapeDtypeStruct((8, columns, 128), jnp.bfloat16)
    edge = jax.ShapeDtypeStruct((64, width + 128), jnp.float32)
    tail = jax.ShapeDtypeStruct((8, 8, width + 128), jnp.float32)
    projected = part if stage < 3 else jax.ShapeDtypeStruct((ROWS_FIRST, columns, width), jnp.bfloat16)
    outs = (part, projected, projected, projected, marks) + ((edge, edge, tail) if stage < 3 else ())
    vmem = pl.BlockSpec(memory_space=pltpu.VMEM)
    work = pltpu.VMEM((tokens, width), jnp.bfloat16)
    inputs = [*pieces, *carried, *weights]
    return pl.pallas_call(
        functools.partial(window_kernel, stage),
        out_shape=outs,
        in_specs=[pl.BlockSpec(memory_space=pltpu.SMEM)] + [vmem] * len(inputs),
        out_specs=(vmem,) * len(outs),
        scratch_shapes=[
            pltpu.VMEM((len(pieces), width + 16, 128), jnp.bfloat16),
            work, work, work, work,
            pltpu.VMEM((8, columns, width + 128), jnp.float32),
        ],
        compiler_params=pltpu.CompilerParams(vmem_limit_bytes=36 * 1024 * 1024),
        cost_estimate=pl.CostEstimate(
            flops=2 * tokens * width * (7 * width + 512), bytes_accessed=16 << 20, transcendentals=tokens * 64 * HEADS
        ),
        name="window_layer",
    )(me, *inputs)


def row_kernel(start, rows, me_ref, *refs):
    parts, wo, refs = [refs[at : at + 5] for at in range(0, 20, 5)], refs[20], refs[21:]
    width = wo.shape[0]
    length = 128
    earlier = ()
    if start:
        earlier, weights, refs = refs[:4], refs[4:7], refs[7:]
        *refs, q_s, k_s, v_s = refs
        y = parts[3][0][start:].astype(jnp.float32)
        h = normed_f32(y.reshape(rows * y.shape[1], width))
        for to, weight, factor in zip((q_s, k_s, v_s), weights, ((width // HEADS) ** (-0.5), 1.0, 1.0)):
            to[...] = (dot_f32(h, weight[...]) * factor).astype(jnp.bfloat16).reshape(to.shape)
    outs, (o_s, placed) = refs[:8], refs[8:]

    def row(i, r, lanes=slice(None)):
        pieces = [part[i][start + r, :, lanes] for part in parts[:3]]
        if 1 <= i <= 3:
            pieces.append((q_s, k_s, v_s)[i - 1][r, :, lanes] if start else parts[3][i][r, :, lanes])
        else:
            pieces.append(parts[3][i][start + r, :, lanes])
        return jnp.concatenate(pieces, 0)

    for r in range(rows):
        here = slice(length * r, length * r + length)
        heads = attend(*([row(i, r, lanes) for lanes in PAIRS] for i in (1, 2, 3)), row(4, r).astype(jnp.float32))
        for lanes, out in zip(PAIRS, heads):
            o_s[here, lanes] = out
    added = dot_f32(o_s[...], wo[...])
    mask = low_columns((8, width), 0)
    me = me_ref[0]
    upper = jnp.bitwise_and(me, 2) > 0
    odd = jnp.bitwise_and(me, 1) > 0
    same = upper == odd
    for r in range(rows):
        f = row(0, r).astype(jnp.float32) + added[length * r : length * r + length]
        tiles = [f[8 * w : 8 * w + 8] for w in range(16)]
        own, own_second, second = tiles[:7], tiles[7], tiles[8:11]
        third = (jnp.where(odd, tiles[13], tiles[11]), tiles[14], jnp.where(odd, tiles[11], tiles[13]))
        middle, third_own = jnp.where(same, tiles[12], tiles[15]), jnp.where(same, tiles[15], tiles[12])
        after_own = jnp.where(upper, third_own, own_second)
        before_own = jnp.where(upper, own_second, third_own)
        whole = [before_own, *own, after_own]
        whole += [jnp.where(upper, middle, after_own), *second, jnp.where(upper, before_own, middle)]
        whole += [jnp.where(upper, after_own, middle), *third, jnp.where(upper, middle, before_own)]
        for l in range(8):
            at = 2 * l if l < 4 else (9, 11, 14, 16)[l - 4]
            before, a, after = whole[at : at + 3]
            piece = jnp.concatenate([jnp.where(mask, before, a), jnp.where(mask, a, after)], 0)
            placed[l, r] = piece.astype(jnp.bfloat16)
    for i, d in enumerate(ORDER):
        if d < 4:
            if start:
                outs[i][:start] = earlier[i - 4][...]
            outs[i][start:] = placed[jnp.bitwise_xor(jnp.bitwise_and(me, 3), d)]
        else:
            outs[i][...] = placed[d // 2 * 2 + jnp.bitwise_xor(jnp.bitwise_and(me, 1), d % 2)]


def row_layer(start, rows, me, parts, w_out, earlier):
    width = w_out.shape[0]
    length = 128
    far = jax.ShapeDtypeStruct((rows, 16, width), jnp.bfloat16)
    near = jax.ShapeDtypeStruct((start + rows, 16, width), jnp.bfloat16)
    vmem = pl.BlockSpec(memory_space=pltpu.VMEM)
    inputs = [*parts, w_out, *earlier]
    rest = parts[15].shape[1]
    work = pltpu.VMEM((rows, rest, width), jnp.bfloat16)
    return pl.pallas_call(
        functools.partial(row_kernel, start, rows),
        out_shape=(far,) * 4 + (near,) * 4,
        in_specs=[pl.BlockSpec(memory_space=pltpu.SMEM)] + [vmem] * len(inputs),
        out_specs=(vmem,) * 8,
        scratch_shapes=[
            pltpu.VMEM((rows * length, width), jnp.bfloat16),
            pltpu.VMEM((8, rows, 16, width), jnp.bfloat16),
        ]
        + [work] * (3 if start else 0),
        compiler_params=pltpu.CompilerParams(vmem_limit_bytes=36 * 1024 * 1024),
        cost_estimate=pl.CostEstimate(
            flops=0, bytes_accessed=1 << 16, transcendentals=0
        ),
        name="row_layer",
    )(me, *inputs)


def place_kernel(spots, me_ref, *refs):
    pieces, out_ref, sems = refs[: len(spots)], refs[-2], refs[-1]
    copies = []
    for i, (d, start) in enumerate(spots):
        at = jnp.bitwise_xor(me_ref[0], d) * 8 + start
        copies.append(pltpu.make_async_copy(pieces[i], out_ref.at[pl.ds(at, pieces[i].shape[0])], sems.at[i]))
        copies[-1].start()
    for copy in copies:
        copy.wait()


def place(spots, me, pieces, so_far, shape):
    vmem = pl.BlockSpec(memory_space=pltpu.VMEM)
    hbm = pl.BlockSpec(memory_space=pltpu.HBM)
    n = len(pieces)
    more = () if so_far is None else (so_far,)
    return pl.pallas_call(
        functools.partial(place_kernel, spots),
        out_shape=jax.ShapeDtypeStruct(shape, jnp.bfloat16),
        in_specs=[pl.BlockSpec(memory_space=pltpu.SMEM)] + [vmem] * n + [hbm] * len(more),
        out_specs=hbm,
        scratch_shapes=[pltpu.SemaphoreType.DMA((n,))],
        input_output_aliases={n + 1: 0} if more else {},
        compiler_params=pltpu.CompilerParams(vmem_limit_bytes=8 * 1024 * 1024),
        cost_estimate=pl.CostEstimate(flops=0, bytes_accessed=4 << 20, transcendentals=0),
        name="place",
    )(me, *pieces, *more)


def exchanged(piece, distance):
    count = lax.axis_size("lon")
    return lax.ppermute(piece, "lon", [(s, s ^ distance) for s in range(count)])


def gathered_bands(
    fields, ocean, w_query1, w_key1, w_value1, w_out1, w_query2, w_key2, w_value2, w_out2
):
    me = lax.axis_index("lon").astype(jnp.int32).reshape(1)
    weights = (w_query1, w_key1, w_value1, w_out1, w_query2, w_key2, w_value2)
    weights = (ready(weights[:3]), *weights)

    packed = {ORDER[0]: pack(ORDER[:1], me, ocean.T, fields)[0]}
    packed.update(zip(ORDER[1:], pack(ORDER[1:], me, ocean.T, fields)))
    got = {d: exchanged(packed[d], d) if d else packed[d] for d in ORDER}
    got[4], *near = lax.optimization_barrier((got[4], got[2], got[3], got[1]))
    got[2], got[3], got[1] = near
    own = window_layer(0, me, [got[d] for d in range(4)], (), weights)
    second = window_layer(1, me, [got[4], got[5]], own[5:], weights)
    edges = (*own[5:7], *second[5:7])
    third = window_layer(2, me, [got[6]], (*edges, second[7]), weights)
    fourth = window_layer(3, me, [got[7]], (*edges, *third[5:]), weights)
    parts = (*own[:5], *second[:5], *third[:5], *fourth)
    first = row_layer(0, ROWS_FIRST, me, parts, w_out2, ())
    last = row_layer(ROWS_FIRST, 8 - ROWS_FIRST, me, parts, w_out2, (*first[4:], w_query2, w_key2, w_value2))
    far = [exchanged(piece, d) for d, piece in zip(ORDER[:4], first)]
    last = list(last)
    for i in range(4):
        last[i], far[i] = lax.optimization_barrier((last[i], far[i]))
    far_last = [exchanged(piece, d) for d, piece in zip(ORDER[:4], last)]
    near = {d: exchanged(piece, d) if d else piece for d, piece in zip(ORDER[4:], last[4:])}
    near = [near[d] for d in ORDER[4:]]
    out = place([(d, 0) for d in ORDER], me, far + near, None, fields.shape)
    return place([(d, ROWS_FIRST) for d in ORDER[:4]], me, far_last, out, fields.shape)


def on_device(fields, *rest):
    rows, cols, width = fields.shape
    if lax.axis_size("lon") == 8 and rows == 64 and cols == 16 and width == 64 * HEADS:
        return gathered_bands(fields, *rest)
    return spread_rows(fields, *rest)


def solution(mesh):
    in_specs = (
        P(("grp", "lat"), "lon", None),
        P(("grp", "lat"), "lon"),
        P(),
        P(),
        P(),
        P(),
        P(),
        P(),
        P(),
        P(),
    )
    out_specs = P(("grp", "lat"), "lon", None)
    return jax.shard_map(
        on_device, mesh=mesh, in_specs=in_specs, out_specs=out_specs, check_vma=False
    )
```

```python
import functools

import jax
import jax.numpy as jnp
from jax import lax
from jax.experimental import pallas as pl
from jax.experimental.pallas import tpu as pltpu
from jax.sharding import PartitionSpec as P

HEADS = 12


EPS = 1e-05
NEG = -1e30

PACK_VMEM = 52 * 1024 * 1024

PAIRS = [slice(128 * p, 128 * p + 128) for p in range(HEADS // 2)]


def passed_along(value, axis, steps):
    count = lax.axis_size(axis)
    pairs = [(source, (source + steps) % count) for source in range(count)]
    return lax.ppermute(value, axis, pairs)


def norm_rows(a):
    af = a.astype(jnp.float32)
    mean = jnp.mean(af, -1, keepdims=True)
    var = jnp.mean((af - mean) * (af - mean), -1, keepdims=True)
    return ((af - mean) * lax.rsqrt(var + EPS)).astype(jnp.bfloat16)


def project(h, weight):
    return jnp.dot(h, weight, preferred_element_type=jnp.float32).astype(jnp.bfloat16)


def masked_softmax(scores, key_ok, land_query):
    top = jnp.max(jnp.where(key_ok, scores, NEG), -1, keepdims=True)
    expo = jnp.where(key_ok, jnp.exp(scores - top), 0.0)
    total = jnp.sum(expo, -1, keepdims=True) + land_query[..., None]
    return (expo / total).astype(jnp.bfloat16)


def window_attend(query, keys, values, flags):
    rows, cols, width = query.shape
    nh = HEADS
    hd = width // nh
    scale = hd ** (-0.5)

    def tiles(a):
        a = a.reshape(rows // 8, 8, cols // 8, 8, nh, hd).transpose(0, 2, 4, 1, 3, 5)
        return a.reshape(rows // 8, cols // 8, nh, 64, hd)

    marks = (
        flags.reshape(rows // 8, 8, cols // 8, 8)
        .transpose(0, 2, 1, 3)
        .reshape(rows // 8, cols // 8, 64)
    )
    key_ok = (marks > 0)[:, :, None, None, :]
    land_query = (marks <= 0).astype(jnp.float32)[:, :, None, :]
    scores = (
        jnp.einsum(
            "abhqd,abhkd->abhqk", tiles(query), tiles(keys), preferred_element_type=jnp.float32
        )
        * scale
    )
    probs = masked_softmax(scores, key_ok, land_query)
    outs = jnp.einsum(
        "abhqk,abhkd->abhqd", probs, tiles(values), preferred_element_type=jnp.float32
    )
    outs = outs * (1.0 - land_query)[..., None]
    outs = outs.astype(jnp.bfloat16).reshape(rows // 8, cols // 8, nh, 8, 8, hd)
    return outs.transpose(0, 3, 1, 4, 2, 5).reshape(rows, cols, width)


def row_attend(query, keys, values, flags):
    rows, length, width = query.shape
    nh = HEADS
    hd = width // nh
    scale = hd ** (-0.5)
    key_ok = (flags > 0)[:, None, :]
    land_query = (flags <= 0).astype(jnp.float32)

    def head(index):
        qh = lax.dynamic_slice_in_dim(query, index * hd, hd, 2)
        kh = lax.dynamic_slice_in_dim(keys, index * hd, hd, 2)
        vh = lax.dynamic_slice_in_dim(values, index * hd, hd, 2)
        scores = jnp.einsum("rqd,rkd->rqk", qh, kh, preferred_element_type=jnp.float32) * scale
        probs = masked_softmax(scores, key_ok, land_query)
        return jnp.einsum("rqk,rkd->rqd", probs, vh, preferred_element_type=jnp.float32)

    outs = lax.map(head, jnp.arange(nh, dtype=jnp.int32))
    outs = outs.transpose(1, 2, 0, 3).reshape(rows, length, width)
    return (outs * (1.0 - land_query)[..., None]).astype(jnp.bfloat16)


def attend_columns(columns, marks, w_query1, w_key1, w_value1):
    return window_attend(
        project(columns, w_query1), project(columns, w_key1), project(columns, w_value1), marks
    )


def spread_rows(
    fields, ocean, w_query1, w_key1, w_value1, w_out1, w_query2, w_key2, w_value2, w_out2
):
    rows, cols, width = fields.shape
    normed = norm_rows(fields)
    marks = ocean.astype(jnp.bfloat16)
    edge_feats, edge_marks = passed_along((normed[:, cols - 4 :], marks[:, cols - 4 :]), "lon", 1)
    columns = jnp.concatenate([edge_feats, normed[:, : cols - 4]], 1)
    column_marks = jnp.concatenate([edge_marks, marks[:, : cols - 4]], 1)
    extended = attend_columns(columns, column_marks, w_query1, w_key1, w_value1)
    returned = passed_along(extended[:, :4], "lon", -1)
    o1 = jnp.concatenate([extended[:, 4:], returned], 1)
    y1 = (
        fields.astype(jnp.float32) + jnp.dot(o1, w_out1, preferred_element_type=jnp.float32)
    ).astype(jnp.bfloat16)
    h2 = norm_rows(y1)
    q2 = project(h2, w_query2)
    k2 = project(h2, w_key2)
    v2 = project(h2, w_value2)
    row_q, row_k, row_v, row_marks = (
        lax.all_to_all(q2, "lon", split_axis=0, concat_axis=1, tiled=True),
        lax.all_to_all(k2, "lon", split_axis=0, concat_axis=1, tiled=True),
        lax.all_to_all(v2, "lon", split_axis=0, concat_axis=1, tiled=True),
        lax.all_to_all(marks, "lon", split_axis=0, concat_axis=1, tiled=True),
    )
    row_out = row_attend(row_q, row_k, row_v, row_marks)
    o2 = lax.all_to_all(row_out, "lon", split_axis=1, concat_axis=0, tiled=True)
    return (
        y1.astype(jnp.float32) + jnp.dot(o2, w_out2, preferred_element_type=jnp.float32)
    ).astype(jnp.bfloat16)


def normed_f32(a):
    mean = jnp.mean(a, -1, keepdims=True)
    centred = a - mean
    var = jnp.mean(centred * centred, -1, keepdims=True)
    return (centred * lax.rsqrt(var + EPS)).astype(jnp.bfloat16)


def dot_f32(a, b):
    return jnp.dot(a, b, preferred_element_type=jnp.float32)


def low_columns(shape, axis):
    return lax.broadcasted_iota(jnp.int32, shape, axis) % 8 < 4


def attend(queries, keys, values, marks):
    n = marks.shape[0]
    low = lax.broadcasted_iota(jnp.int32, (n, 128), 1) < 64
    land = 1.0 - marks
    bias = jnp.concatenate([land * NEG] * (2 * n // 128), 1)
    scores = []
    for q, k in zip(queries, keys):
        zero = jnp.zeros_like(q)
        both = jnp.concatenate([jnp.where(low, q, zero), jnp.where(low, zero, q)], 0)
        scores.append(lax.dot_general(k, both, (((1,), (1,)), ((), ())), preferred_element_type=jnp.float32) + bias)
    expos = [jnp.exp(s - jnp.max(s, 0, keepdims=True)).astype(jnp.bfloat16) for s in scores]
    outs = []
    for expo, v in zip(expos, values):
        wide = jnp.concatenate([v, jnp.ones_like(v)], 1)
        sums = lax.dot_general(expo, wide, (((0,), (0,)), ((), ())), preferred_element_type=jnp.float32)
        upper = jnp.where(low, sums[:n, :128], sums[n:, :128])
        total = jnp.where(low, sums[:n, 128:], sums[n:, 128:]) + land
        outs.append((upper / total * marks).astype(jnp.bfloat16))
    return outs


ORDER = (4, 5, 6, 7, 1, 2, 3, 0)


def pack_kernel(distances, me_ref, marks_ref, fields_ref, *refs):
    outs, (held, held_marks, sems) = refs[: len(distances)], refs[len(distances) :]
    me = me_ref[0]
    tiles = fields_ref.shape[-1] // 128
    copies = [pltpu.make_async_copy(marks_ref, held_marks, sems.at[len(distances)])]
    for i, d in enumerate(distances):
        there = jnp.bitwise_xor(me, d)
        copies.append(pltpu.make_async_copy(fields_ref.at[pl.ds(there * 8, 8)], held.at[i], sems.at[i]))
    for copy in copies:
        copy.start()
    copies[0].wait()
    marks = held_marks[...].astype(jnp.float32)
    marks = jnp.concatenate([marks, jnp.zeros((16, 128 - marks.shape[1]), jnp.float32)], 1).astype(jnp.bfloat16)
    for i in range(len(distances)):
        copies[i + 1].wait()
        piece = held[i].reshape(128, 128 * tiles)
        for t in range(tiles):
            outs[i][128 * t : 128 * t + 128, :] = piece[:, 128 * t : 128 * t + 128]
        outs[i][128 * tiles :, :] = marks


def pack(distances, me, marks, fields):
    cols, width = fields.shape[1:]
    vmem = pl.BlockSpec(memory_space=pltpu.VMEM)
    anywhere = pl.BlockSpec(memory_space=pl.ANY)
    piece = jax.ShapeDtypeStruct((width + 16, 128), jnp.bfloat16)
    n = len(distances)
    return pl.pallas_call(
        functools.partial(pack_kernel, distances),
        out_shape=(piece,) * n,
        in_specs=[pl.BlockSpec(memory_space=pltpu.SMEM), anywhere, anywhere],
        out_specs=(vmem,) * n,
        scratch_shapes=[
            pltpu.VMEM((n, 8, cols, width), jnp.bfloat16),
            pltpu.VMEM(marks.shape, marks.dtype),
            pltpu.SemaphoreType.DMA((n + 1,)),
        ],
        compiler_params=pltpu.CompilerParams(vmem_limit_bytes=PACK_VMEM),
        cost_estimate=pl.CostEstimate(flops=n * 200000, bytes_accessed=n * 400000, transcendentals=0),
        name="pack",
    )(me, marks, fields)


def ready_kernel(*refs):
    refs[-1][...] = jnp.zeros_like(refs[-1])


def ready(weights):
    vmem = pl.BlockSpec(memory_space=pltpu.VMEM)
    return pl.pallas_call(
        ready_kernel,
        out_shape=jax.ShapeDtypeStruct((8, 128), jnp.float32),
        in_specs=[vmem] * len(weights),
        out_specs=vmem,
        compiler_params=pltpu.CompilerParams(vmem_limit_bytes=16 * 1024 * 1024),
        cost_estimate=pl.CostEstimate(flops=0, bytes_accessed=32 << 20, transcendentals=0),
        name="ready",
    )(*weights)


def unpacked(me, piece):
    tiles = (piece.shape[0] - 16) // 128
    lanes = [piece[128 * t : 128 * t + 128] for t in range(tiles)]
    marks = pltpu.roll(piece[128 * tiles :].astype(jnp.float32), jnp.bitwise_and(128 - 8 * me, 127), 1)
    marks = jnp.concatenate([jnp.broadcast_to(marks[:, r : r + 1], (16, 128)) for r in range(8)], 0)
    whole = jnp.concatenate(lanes + [marks.astype(jnp.bfloat16)], 1).astype(jnp.float32)
    whole = whole.reshape(8, 2, 8, 128 * tiles + 128)
    return whole[:, 0], whole[:, 1]


STAGES = ((7, 6), (4, 4), (2, 2), (3, 4))

ROWS_FIRST = 4


def window_kernel(stage, me_ref, *refs):
    pieces = refs[: (4, 2, 1, 1)[stage]]
    refs = refs[len(pieces) :]
    carried = refs[: (0, 3, 5, 7)[stage]]
    refs = refs[len(carried) :]
    _, wq, wk, wv, wo, wq2, wk2, wv2, y_ref, q2_ref, k2_ref, v2_ref, m_ref = refs[:13]
    refs = refs[13:]
    passed = refs[: 3 if stage < 3 else 0]
    placed, q_s, k_s, v_s, o_s, rows_s = refs[len(passed) :]
    width = wq.shape[0]
    scale = (width // HEADS) ** (-0.5)
    me = me_ref[0]
    upper = jnp.bitwise_and(me, 2) > 0
    odd = jnp.bitwise_and(me, 1) > 0
    low = jnp.bitwise_and(me, len(pieces) - 1)
    for d, piece in enumerate(pieces):
        placed[jnp.bitwise_xor(low, d)] = piece[...]
    columns = [unpacked(me, placed[l]) for l in range(len(pieces))]
    mask = low_columns((8, 8, width + 128), 1)
    full = (64, width + 128)

    def whole_window(l):
        return jnp.where(mask, columns[l][1], columns[l][0]).reshape(full)

    def straddling_window(left, right):
        return jnp.where(mask, right, left).reshape(full)

    def either(if_upper, if_lower):
        return jnp.where(upper, if_upper, if_lower)

    windows = [whole_window(0)]
    for l in range(1, len(pieces)):
        windows += [straddling_window(columns[l - 1][1], columns[l][0]), whole_window(l)]
    first, last = columns[0][0], columns[-1][1]
    if stage < 3:
        passed[0][...] = first.reshape(full)
        passed[1][...] = last.reshape(full)
    edges = [a[...].reshape(8, 8, width + 128) for a in carried[:-1]]
    if stage == 1:
        own_first, own_last = edges
        windows = [straddling_window(either(last, own_last), either(own_first, first))] + windows
    if stage >= 2:
        own_first, own_last, second_first, second_last = edges[:4]
        before, after = either(own_last, second_last), either(second_first, own_first)
    if stage == 2:
        windows.append(straddling_window(jnp.where(odd, last, before), jnp.where(odd, after, first)))
    if stage == 3:
        one_first, one_last = edges[4:]
        windows.append(straddling_window(jnp.where(odd, last, one_last), jnp.where(odd, one_first, first)))
        windows.append(straddling_window(jnp.where(odd, before, last), jnp.where(odd, first, after)))
    count = len(windows)
    x = jnp.concatenate([w[:, :width] for w in windows], 0)
    marks = [w[:, width:] for w in windows]
    h = normed_f32(x)
    q_s[...] = (dot_f32(h, wq[...]) * scale).astype(jnp.bfloat16)
    k_s[...] = dot_f32(h, wk[...]).astype(jnp.bfloat16)
    v_s[...] = dot_f32(h, wv[...]).astype(jnp.bfloat16)
    for w in range(count):
        here = slice(64 * w, 64 * w + 64)
        outs = attend(*([a[here, lanes] for lanes in PAIRS] for a in (q_s, k_s, v_s)), marks[w])
        for lanes, out in zip(PAIRS, outs):
            o_s[here, lanes] = out
    y = (x + dot_f32(o_s[...], wo[...])).astype(jnp.bfloat16).astype(jnp.float32)
    skip = 0
    if stage > 0:
        skip = 1
        rows_s[:, :8, :] = carried[-1][...]
    for w in range(count):
        for r in range(8):
            at = 64 * w + 8 * r
            to = 8 * (w + skip)
            if stage < 3 and w == count - 1:
                passed[2][r, :, :width] = y[at : at + 8]
                passed[2][r, :, width:] = marks[w][8 * r : 8 * r + 8]
            else:
                rows_s[r, to : to + 8, :width] = y[at : at + 8]
                rows_s[r, to : to + 8, width:] = marks[w][8 * r : 8 * r + 8]
    m_ref[...] = rows_s[:, :, width:].astype(jnp.bfloat16)
    y_ref[...] = rows_s[:, :, :width].astype(jnp.bfloat16)
    rows = q2_ref.shape[0]
    h = normed_f32(rows_s[:rows, :, :width].reshape(rows * rows_s.shape[1], width))
    q2_ref[...] = (dot_f32(h, wq2[...]) * scale).astype(jnp.bfloat16).reshape(q2_ref.shape)
    k2_ref[...] = dot_f32(h, wk2[...]).astype(jnp.bfloat16).reshape(k2_ref.shape)
    v2_ref[...] = dot_f32(h, wv2[...]).astype(jnp.bfloat16).reshape(v2_ref.shape)


def window_layer(stage, me, pieces, carried, weights):
    width = weights[1].shape[0]
    tokens = 64 * STAGES[stage][0]
    columns = 8 * STAGES[stage][1]
    part = jax.ShapeDtypeStruct((8, columns, width), jnp.bfloat16)
    marks = jax.ShapeDtypeStruct((8, columns, 128), jnp.bfloat16)
    edge = jax.ShapeDtypeStruct((64, width + 128), jnp.float32)
    tail = jax.ShapeDtypeStruct((8, 8, width + 128), jnp.float32)
    projected = part if stage < 3 else jax.ShapeDtypeStruct((ROWS_FIRST, columns, width), jnp.bfloat16)
    outs = (part, projected, projected, projected, marks) + ((edge, edge, tail) if stage < 3 else ())
    vmem = pl.BlockSpec(memory_space=pltpu.VMEM)
    work = pltpu.VMEM((tokens, width), jnp.bfloat16)
    inputs = [*pieces, *carried, *weights]
    return pl.pallas_call(
        functools.partial(window_kernel, stage),
        out_shape=outs,
        in_specs=[pl.BlockSpec(memory_space=pltpu.SMEM)] + [vmem] * len(inputs),
        out_specs=(vmem,) * len(outs),
        scratch_shapes=[
            pltpu.VMEM((len(pieces), width + 16, 128), jnp.bfloat16),
            work, work, work, work,
            pltpu.VMEM((8, columns, width + 128), jnp.float32),
        ],
        compiler_params=pltpu.CompilerParams(vmem_limit_bytes=36 * 1024 * 1024),
        cost_estimate=pl.CostEstimate(
            flops=2 * tokens * width * (7 * width + 512), bytes_accessed=16 << 20, transcendentals=tokens * 64 * HEADS
        ),
        name="window_layer",
    )(me, *inputs)


def row_kernel(start, rows, me_ref, *refs):
    parts, wo, refs = [refs[at : at + 5] for at in range(0, 20, 5)], refs[20], refs[21:]
    width = wo.shape[0]
    length = 128
    earlier = ()
    if start:
        earlier, weights, refs = refs[:4], refs[4:7], refs[7:]
        *refs, q_s, k_s, v_s = refs
        y = parts[3][0][start:].astype(jnp.float32)
        h = normed_f32(y.reshape(rows * y.shape[1], width))
        for to, weight, factor in zip((q_s, k_s, v_s), weights, ((width // HEADS) ** (-0.5), 1.0, 1.0)):
            to[...] = (dot_f32(h, weight[...]) * factor).astype(jnp.bfloat16).reshape(to.shape)
    outs, (o_s, placed) = refs[:8], refs[8:]

    def row(i, r, lanes=slice(None)):
        pieces = [part[i][start + r, :, lanes] for part in parts[:3]]
        if 1 <= i <= 3:
            pieces.append((q_s, k_s, v_s)[i - 1][r, :, lanes] if start else parts[3][i][r, :, lanes])
        else:
            pieces.append(parts[3][i][start + r, :, lanes])
        return jnp.concatenate(pieces, 0)

    for r in range(rows):
        here = slice(length * r, length * r + length)
        heads = attend(*([row(i, r, lanes) for lanes in PAIRS] for i in (1, 2, 3)), row(4, r).astype(jnp.float32))
        for lanes, out in zip(PAIRS, heads):
            o_s[here, lanes] = out
    added = dot_f32(o_s[...], wo[...])
    mask = low_columns((8, width), 0)
    me = me_ref[0]
    upper = jnp.bitwise_and(me, 2) > 0
    odd = jnp.bitwise_and(me, 1) > 0
    same = upper == odd
    for r in range(rows):
        f = row(0, r).astype(jnp.float32) + added[length * r : length * r + length]
        tiles = [f[8 * w : 8 * w + 8] for w in range(16)]
        own, own_second, second = tiles[:7], tiles[7], tiles[8:11]
        third = (jnp.where(odd, tiles[13], tiles[11]), tiles[14], jnp.where(odd, tiles[11], tiles[13]))
        middle, third_own = jnp.where(same, tiles[12], tiles[15]), jnp.where(same, tiles[15], tiles[12])
        after_own = jnp.where(upper, third_own, own_second)
        before_own = jnp.where(upper, own_second, third_own)
        whole = [before_own, *own, after_own]
        whole += [jnp.where(upper, middle, after_own), *second, jnp.where(upper, before_own, middle)]
        whole += [jnp.where(upper, after_own, middle), *third, jnp.where(upper, middle, before_own)]
        for l in range(8):
            at = 2 * l if l < 4 else (9, 11, 14, 16)[l - 4]
            before, a, after = whole[at : at + 3]
            piece = jnp.concatenate([jnp.where(mask, before, a), jnp.where(mask, a, after)], 0)
            placed[l, r] = piece.astype(jnp.bfloat16)
    for i, d in enumerate(ORDER):
        if d < 4:
            if start:
                outs[i][:start] = earlier[i - 4][...]
            outs[i][start:] = placed[jnp.bitwise_xor(jnp.bitwise_and(me, 3), d)]
        else:
            outs[i][...] = placed[d // 2 * 2 + jnp.bitwise_xor(jnp.bitwise_and(me, 1), d % 2)]


def row_layer(start, rows, me, parts, w_out, earlier):
    width = w_out.shape[0]
    length = 128
    far = jax.ShapeDtypeStruct((rows, 16, width), jnp.bfloat16)
    near = jax.ShapeDtypeStruct((start + rows, 16, width), jnp.bfloat16)
    vmem = pl.BlockSpec(memory_space=pltpu.VMEM)
    inputs = [*parts, w_out, *earlier]
    rest = parts[15].shape[1]
    work = pltpu.VMEM((rows, rest, width), jnp.bfloat16)
    return pl.pallas_call(
        functools.partial(row_kernel, start, rows),
        out_shape=(far,) * 4 + (near,) * 4,
        in_specs=[pl.BlockSpec(memory_space=pltpu.SMEM)] + [vmem] * len(inputs),
        out_specs=(vmem,) * 8,
        scratch_shapes=[
            pltpu.VMEM((rows * length, width), jnp.bfloat16),
            pltpu.VMEM((8, rows, 16, width), jnp.bfloat16),
        ]
        + [work] * (3 if start else 0),
        compiler_params=pltpu.CompilerParams(vmem_limit_bytes=36 * 1024 * 1024),
        cost_estimate=pl.CostEstimate(
            flops=0, bytes_accessed=1 << 16, transcendentals=0
        ),
        name="row_layer",
    )(me, *inputs)


def place_kernel(spots, me_ref, *refs):
    pieces, out_ref, sems = refs[: len(spots)], refs[-2], refs[-1]
    copies = []
    for i, (d, start) in enumerate(spots):
        at = jnp.bitwise_xor(me_ref[0], d) * 8 + start
        copies.append(pltpu.make_async_copy(pieces[i], out_ref.at[pl.ds(at, pieces[i].shape[0])], sems.at[i]))
        copies[-1].start()
    for copy in copies:
        copy.wait()


def place(spots, me, pieces, so_far, shape):
    vmem = pl.BlockSpec(memory_space=pltpu.VMEM)
    hbm = pl.BlockSpec(memory_space=pltpu.HBM)
    n = len(pieces)
    more = () if so_far is None else (so_far,)
    return pl.pallas_call(
        functools.partial(place_kernel, spots),
        out_shape=jax.ShapeDtypeStruct(shape, jnp.bfloat16),
        in_specs=[pl.BlockSpec(memory_space=pltpu.SMEM)] + [vmem] * n + [hbm] * len(more),
        out_specs=hbm,
        scratch_shapes=[pltpu.SemaphoreType.DMA((n,))],
        input_output_aliases={n + 1: 0} if more else {},
        compiler_params=pltpu.CompilerParams(vmem_limit_bytes=8 * 1024 * 1024),
        cost_estimate=pl.CostEstimate(flops=0, bytes_accessed=4 << 20, transcendentals=0),
        name="place",
    )(me, *pieces, *more)


def exchanged(piece, distance):
    count = lax.axis_size("lon")
    return lax.ppermute(piece, "lon", [(s, s ^ distance) for s in range(count)])


def gathered_bands(
    fields, ocean, w_query1, w_key1, w_value1, w_out1, w_query2, w_key2, w_value2, w_out2
):
    me = lax.axis_index("lon").astype(jnp.int32).reshape(1)
    weights = (w_query1, w_key1, w_value1, w_out1, w_query2, w_key2, w_value2)
    weights = (ready(weights[:5]), *weights)

    packed = dict(zip(ORDER, pack(ORDER, me, ocean.T, fields)))
    got = {d: exchanged(packed[d], d) if d else packed[d] for d in ORDER}
    got[4], *near = lax.optimization_barrier((got[4], got[2], got[3], got[1]))
    got[2], got[3], got[1] = near
    own = window_layer(0, me, [got[d] for d in range(4)], (), weights)
    second = window_layer(1, me, [got[4], got[5]], own[5:], weights)
    edges = (*own[5:7], *second[5:7])
    third = window_layer(2, me, [got[6]], (*edges, second[7]), weights)
    fourth = window_layer(3, me, [got[7]], (*edges, *third[5:]), weights)
    parts = (*own[:5], *second[:5], *third[:5], *fourth)
    first = row_layer(0, ROWS_FIRST, me, parts, w_out2, ())
    last = row_layer(ROWS_FIRST, 8 - ROWS_FIRST, me, parts, w_out2, (*first[4:], w_query2, w_key2, w_value2))
    far = [exchanged(piece, d) for d, piece in zip(ORDER[:4], first)]
    last = list(last)
    for i in range(4):
        last[i], far[i] = lax.optimization_barrier((last[i], far[i]))
    far_last = [exchanged(piece, d) for d, piece in zip(ORDER[:4], last)]
    near = {d: exchanged(piece, d) if d else piece for d, piece in zip(ORDER[4:], last[4:])}
    near = [near[d] for d in ORDER[4:]]
    out = place([(d, 0) for d in ORDER], me, far + near, None, fields.shape)
    return place([(d, ROWS_FIRST) for d in ORDER[:4]], me, far_last, out, fields.shape)


def on_device(fields, *rest):
    rows, cols, width = fields.shape
    if lax.axis_size("lon") == 8 and rows == 64 and cols == 16 and width == 64 * HEADS:
        return gathered_bands(fields, *rest)
    return spread_rows(fields, *rest)


def solution(mesh):
    in_specs = (
        P(("grp", "lat"), "lon", None),
        P(("grp", "lat"), "lon"),
        P(),
        P(),
        P(),
        P(),
        P(),
        P(),
        P(),
        P(),
    )
    out_specs = P(("grp", "lat"), "lon", None)
    return jax.shard_map(
        on_device, mesh=mesh, in_specs=in_specs, out_specs=out_specs, check_vma=False
    )
```
